256 devices in a mesh: ctx: 32 (over x, z), head: 8 (over y, core).
Axes of the slice: x: 4, y: 4, z: 8, core: 2. Of those that a mesh axis runs over, the one named last changes fastest.
Arguments:
- query: bfloat16 [16384, 32, 128], P('ctx', 'head'), may hold values from -24 to 24
- key: bfloat16 [16384, 32, 128], P('ctx', 'head'), may hold values from -6 to 6
- value: bfloat16 [16384, 32, 128], P('ctx', 'head'), may hold values from -6 to 6
- out_grad: bfloat16 [16384, 32, 128], P('ctx', 'head'), may hold values from -6 to 6
- random_links: int32 [256, 32, 3], P(None, 'head'), may hold values from 0 to 255, as said below
Outputs:
- attended: bfloat16 [16384, 32, 128], P('ctx', 'head')
- query_grad: bfloat16 [16384, 32, 128], P('ctx', 'head')
- key_grad: bfloat16 [16384, 32, 128], P('ctx', 'head')
- value_grad: bfloat16 [16384, 32, 128], P('ctx', 'head')
The draws below stay inside these ranges and needn't reach their ends.
Inputs may be any that keep to these rules, and one draw needn't show every extreme that they name: `random_links`: within one head, the 24 random entries of the query blocks o * 8 to o * 8 + 7 name blocks of any one run p * 8 to p * 8 + 7 at most 2 times, and for each such run of query blocks and head some run p is named exactly 2 times.
All inputs are finite; a program needn't handle non-finite values.
Results may differ from the reference program's by a relative error of at most 0.012.
Values may be sent and summed in bfloat16 or wider, within the bound.
A program may use at most 128 MiB of HBM per device.

```python
import math
import jax
import jax.numpy as jnp
from jax import lax

BLOCK = 64
HD = 128
R = 3
HEADS = 32
BPD = 8
NB = 256
SEQ = 16384
CAP = 2
N_CTX = 32


def draw_query(key, part):
    base_key = jax.random.fold_in(key, 21)
    drawn = jnp.clip(jax.random.normal(base_key, (SEQ, HEADS, HD), jnp.float32), -6.0, 6.0)
    return drawn.astype(jnp.bfloat16)


def draw_key(key, part):
    base_key = jax.random.fold_in(key, 22)
    drawn = jnp.clip(jax.random.normal(base_key, (SEQ, HEADS, HD), jnp.float32), -6.0, 6.0)
    return drawn.astype(jnp.bfloat16)


def one_table(table_key):
    slot_count = N_CTX * CAP
    ref_count = BPD * R
    first_key, second_key, third_key, fourth_key = jax.random.split(table_key, 4)
    shuffled = jax.random.permutation(first_key, slot_count)
    priority = jnp.zeros((slot_count,), jnp.int32).at[shuffled].set(jnp.arange(slot_count, dtype=jnp.int32))
    favored = jax.random.randint(second_key, (), 0, N_CTX)
    priority = jnp.where(jnp.arange(slot_count, dtype=jnp.int32) // CAP == favored, -1, priority)
    picked = jnp.argsort(priority, stable=True)[:ref_count]
    holders = (picked // CAP)[jax.random.permutation(third_key, ref_count)]
    within = jax.random.randint(fourth_key, (ref_count,), 0, BPD)
    return (holders * BPD + within).astype(jnp.int32)


def draw_random_links(key, part):
    table_keys = jax.random.split(jax.random.fold_in(key, 31), N_CTX * HEADS)
    tables = jax.vmap(one_table)(table_keys)
    return tables.reshape(N_CTX, HEADS, BPD, R).transpose(0, 2, 1, 3).reshape(NB, HEADS, R)


def steps_of(own_key, shape, pieces, least, top_value):
    gain, own = 1.0, jax.random.fold_in(own_key, 6)
    for position, shards_of in pieces:
        heights = jnp.exp(jax.random.uniform(jax.random.fold_in(own, position), (shards_of,), jnp.float32, least / len(pieces), top_value / len(pieces)))
        gain = gain * jnp.repeat(heights, shape[position] // shards_of).reshape([-1 if axis == position else 1 for axis in range(len(shape))])
    return gain


def scatter_about(stream_key, dims, spread, reach, cuts=(), kind=jnp.bfloat16):
    values = jax.random.normal(stream_key, dims, jnp.float32) * spread
    if len(cuts) > 0:
        values = steps_of(stream_key, dims, cuts, -0.22, 0.18) * values
    return jnp.clip(values, min=-reach, max=reach).astype(kind)


def setup_inputs(seed: int = 0) -> dict:
    key_list = jax.random.split(jax.random.key(seed), 6)
    return {
        "query": draw_query(jax.random.fold_in(key_list[5], 71), 0),
        "key": draw_key(jax.random.fold_in(key_list[5], 71), 0),
        "value": scatter_about(key_list[2], (SEQ, HEADS, HD), 1.0, 6.0, ((0, 32), (1, 8))),
        "out_grad": scatter_about(key_list[3], (SEQ, HEADS, HD), 1.0, 6.0, ((0, 32), (1, 8))),
        "random_links": draw_random_links(jax.random.fold_in(key_list[5], 71), 0),
    }


def to_low(array):
    return lax.optimization_barrier(array.astype(jnp.bfloat16)).astype(jnp.float32)

def take_blocks(table_one, index_one):
    return table_one[index_one]

def add_blocks(total_one, index_one, terms_one):
    return total_one.at[index_one].add(terms_one)

def reference(query, key, value, out_grad, random_links):
    scaling = 1.0 / math.sqrt(HD)
    kind_count = 5 + R

    def head_major(array):
        return array.reshape(NB, BLOCK, HEADS, HD).transpose(2, 0, 1, 3)
    query_all = head_major(query)
    key_all = head_major(key)
    value_all = head_major(value)
    grad_all = head_major(out_grad)
    block_ids = jnp.arange(NB, dtype=jnp.int32)
    previous = jnp.maximum(block_ids - 1, 0)
    following = jnp.minimum(block_ids + 1, NB - 1)
    fixed_ids = jnp.stack((previous, block_ids, following, jnp.zeros_like(block_ids), jnp.full_like(block_ids, NB - 1)), axis=1)
    key_lists = jnp.concatenate((jnp.broadcast_to(fixed_ids[:, None, :], (NB, HEADS, 5)), random_links.astype(jnp.int32)), axis=2)
    usable = jnp.concatenate(((block_ids > 0)[:, None], jnp.ones((NB, 1), bool), (block_ids < NB - 1)[:, None], jnp.ones((NB, kind_count - 3), bool)), axis=1)
    col_valid = jnp.repeat(usable, BLOCK, axis=1)
    far_entry = (jnp.arange(kind_count) >= 5)[None, None, :, None, None]

    def advance(carried, group):
        key_total, value_total = carried
        start = (group * BPD).astype(jnp.int32)
        query_group = lax.dynamic_slice_in_dim(query_all, start, BPD, 1).astype(jnp.float32)
        grad_group = lax.dynamic_slice_in_dim(grad_all, start, BPD, 1).astype(jnp.float32)
        list_group = lax.dynamic_slice_in_dim(key_lists, start, BPD, 0).transpose(1, 0, 2)
        valid_group = lax.dynamic_slice_in_dim(col_valid, start, BPD, 0)
        key_group = jax.vmap(take_blocks)(key_all, list_group).reshape(HEADS, BPD, kind_count * BLOCK, HD).astype(jnp.float32)
        value_group = jax.vmap(take_blocks)(value_all, list_group).reshape(HEADS, BPD, kind_count * BLOCK, HD).astype(jnp.float32)
        scores = jnp.einsum('hgbd,hgkd->hgbk', query_group, key_group) * scaling
        valid_mask = valid_group[None, :, None, :]
        scores = jnp.where(valid_mask, scores, -1e+30)
        row_max = lax.optimization_barrier(jnp.max(scores, axis=-1, keepdims=True))
        powers = jnp.where(valid_mask, jnp.exp(scores - row_max), 0.0)
        probs = powers / lax.optimization_barrier(jnp.sum(powers, axis=-1, keepdims=True))
        probs_low = to_low(probs)
        attended = jnp.einsum('hgbk,hgkd->hgbd', probs_low, value_group).astype(jnp.bfloat16)
        row_delta = lax.optimization_barrier(jnp.sum(grad_group * attended.astype(jnp.float32), axis=-1))
        grad_probs = jnp.einsum('hgbd,hgkd->hgbk', grad_group, value_group)
        grad_scores = to_low(probs * (grad_probs - row_delta[..., None]))
        query_part = (scaling * jnp.einsum('hgbk,hgkd->hgbd', grad_scores, key_group)).astype(jnp.bfloat16)
        key_terms = scaling * jnp.einsum('hgbk,hgbd->hgkd', grad_scores, query_group)
        value_terms = jnp.einsum('hgbk,hgbd->hgkd', probs_low, grad_group)
        key_terms = key_terms.reshape(HEADS, BPD, kind_count, BLOCK, HD)
        value_terms = value_terms.reshape(HEADS, BPD, kind_count, BLOCK, HD)
        key_terms = jnp.where(far_entry, to_low(key_terms), key_terms)
        value_terms = jnp.where(far_entry, to_low(value_terms), value_terms)
        flat_ids = list_group.reshape(HEADS, BPD * kind_count)
        key_total = jax.vmap(add_blocks)(key_total, flat_ids, key_terms.reshape(HEADS, BPD * kind_count, BLOCK, HD))
        value_total = jax.vmap(add_blocks)(value_total, flat_ids, value_terms.reshape(HEADS, BPD * kind_count, BLOCK, HD))
        return ((key_total, value_total), (attended, query_part))
    zeros_start = jnp.zeros((HEADS, NB, BLOCK, HD), jnp.float32)
    (key_total, value_total), (attended, query_part) = lax.scan(advance, (zeros_start, zeros_start), jnp.arange(NB // BPD, dtype=jnp.int32))

    def seq_from_groups(array):
        return array.transpose(0, 2, 3, 1, 4).reshape(SEQ, HEADS, HD)

    def seq_from_heads(array):
        return array.transpose(1, 2, 0, 3).reshape(SEQ, HEADS, HD)
    return (seq_from_groups(attended), seq_from_groups(query_part), seq_from_heads(key_total).astype(jnp.bfloat16), seq_from_heads(value_total).astype(jnp.bfloat16))
```

```python
import math

import jax
import jax.numpy as jnp
from jax import lax
from jax.experimental import pallas as pl
from jax.experimental.pallas import tpu as pltpu
from jax.sharding import PartitionSpec as P

BLOCK = 64
HD = 128
NX = 4
NZ = 8
BPD = 8
HALF = BPD // 2
H = 4
R = 3
REFS = BPD * R
TARGETS = NZ * BPD
MAIN = 16
RELAY = 8
MERGED = MAIN + 2
RELAYED = RELAY + 1
FROM_R, FROM_L, OWN = 0, MERGED, 2 * MERGED
RECEIVED = OWN + MAIN
B_RR = 2 * MERGED
B_RL = B_RR + RELAY
B_OWN = B_RL + RELAY
B_ZERO = B_OWN + MAIN
B_SIZE = B_ZERO + 1
DEEP = 8
F32 = jnp.float32
BF16 = jnp.bfloat16
MESH = pl.DeviceIdType.MESH
SCALE = 1.0 / math.sqrt(HD)


def slot_tables(links):
    ctx = lax.axis_index("ctx")
    x, z = ctx // NZ, ctx % NZ
    row = lax.dynamic_slice_in_dim(links.reshape(NX, NZ, BPD, H, R), z, 1, 1)[:, 0]
    named = row.transpose(2, 0, 1, 3).reshape(H, NX, REFS)
    planes = jnp.arange(NX, dtype=jnp.int32)
    away = (named // TARGETS - planes[None, :, None]) % NX
    target = named % TARGETS
    entry = jnp.arange(REFS, dtype=jnp.int32)
    before = entry[None, :] < entry[:, None]
    rank = jnp.sum(
        ((away[..., None, :] == away[..., :, None]) & before).astype(jnp.int32), axis=-1
    )
    n_r = jnp.sum((away == 1).astype(jnp.int32), axis=-1)
    n_o = jnp.sum((away == 2).astype(jnp.int32), axis=-1)
    n_l = jnp.sum((away == 3).astype(jnp.int32), axis=-1)
    by_right = jnp.minimum(n_o, jnp.minimum(RELAY, MAIN - n_r))[..., None]
    right_way = rank < by_right
    place = jnp.where(
        away == 0,
        OWN + rank,
        jnp.where(
            away == 1,
            FROM_R + rank,
            jnp.where(
                away == 3,
                FROM_L + rank,
                jnp.where(
                    right_way,
                    FROM_R + n_r[..., None] + rank,
                    FROM_L + n_l[..., None] + rank - by_right,
                ),
            ),
        ),
    )
    relay_rank = jnp.where(right_way, rank, rank - by_right)
    code = jnp.where(away == 2, TARGETS + relay_rank, target)
    spots = jnp.arange(RECEIVED, dtype=jnp.int32)
    hit = place[..., None] == spots
    merged = jnp.sum(jnp.where(hit, code[..., None], 0), axis=2)
    relay_place = jnp.where(away == 2, jnp.where(right_way, 0, RELAY) + relay_rank, -1)
    relays = jnp.sum(
        jnp.where(
            relay_place[..., None] == jnp.arange(2 * RELAY, dtype=jnp.int32), target[..., None], 0
        ),
        axis=2,
    )
    own_place = lax.dynamic_slice_in_dim(place, x, 1, 1)[:, 0]
    giver = jnp.sum(
        jnp.where(own_place[..., None] == spots, entry[None, :, None], 0), axis=1
    )
    landing = jnp.where(
        away == 0,
        B_OWN + rank,
        jnp.where(
            away == 1,
            FROM_L + rank,
            jnp.where(
                away == 3, FROM_R + rank, jnp.where(right_way, B_RL, B_RR) + relay_rank
            ),
        ),
    ).reshape(H, NX * REFS)
    here = jnp.where(named // TARGETS == x, target, -1).reshape(H, NX * REFS)
    every = jnp.arange(NX * REFS, dtype=jnp.int32)
    same = (here[:, None, :] == here[:, :, None]) & (every[None, :] < every[:, None])
    depth = jnp.sum(same.astype(jnp.int32), axis=-1)
    cell = jnp.where(here >= 0, here * DEEP + depth, -1)
    cells = jnp.arange(TARGETS * DEEP, dtype=jnp.int32)
    sources = B_ZERO + jnp.sum(
        jnp.where(cell[:, :, None] == cells, landing[:, :, None] - B_ZERO, 0), axis=1
    )
    counts = jnp.stack((n_r, n_l), axis=-1).reshape(H, 2 * NX)
    return (
        merged.reshape(H, NX * RECEIVED),
        relays.reshape(H, NX * 2 * RELAY),
        own_place,
        giver,
        counts,
        sources,
    )


def kernel(
    kv,
    query,
    grad,
    merged_t,
    relay_t,
    place_t,
    giver_t,
    count_t,
    source_t,
    out_o,
    out_q,
    out_k,
    out_v,
    table,
    relay_out,
    relay_in,
    merged_out,
    received,
    terms_in,
    terms_relay,
    sums_r,
    sums_l,
    near,
    anchor_acc,
    anchor_kv,
    wide,
    terms,
    ag_send,
    ag_recv,
    f1_send,
    f1_recv,
    f2_send,
    f2_recv,
    b1_send,
    b1_recv,
    b2_send,
    b2_recv,
    rs_send,
    rs_recv,
):
    ctx = lax.axis_index("ctx")
    x, z = ctx // NZ, ctx % NZ
    z_r = x * NZ + lax.rem(z + 1, NZ)
    z_l = x * NZ + lax.rem(z + NZ - 1, NZ)
    p_r = lax.rem(x + 1, NX)
    p_l = lax.rem(x + NX - 1, NX)
    p_o = lax.rem(x + 2, NX)
    x_r = p_r * NZ + z
    x_l = p_l * NZ + z

    def to(device, src, dst, send, recv):
        return pltpu.make_async_remote_copy(
            src_ref=src,
            dst_ref=dst,
            send_sem=send,
            recv_sem=recv,
            device_id={"ctx": device},
            device_id_type=MESH,
        )

    barrier = pltpu.get_barrier_semaphore()
    for device in (z_r, z_l, x_r, x_l):
        pl.semaphore_signal(barrier, inc=1, device_id={"ctx": device}, device_id_type=MESH)
    pl.semaphore_wait(barrier, 4)

    def gather_copy(h, s, half, right):
        row = lax.rem(z + NZ - (s - 1), NZ) if right else lax.rem(z + s - 1, NZ)
        src = (
            kv.at[h, pl.ds(half * HALF, HALF)]
            if s == 1
            else table[h].at[pl.ds(row * BPD + half * HALF, HALF)]
        )
        dst = table[h].at[pl.ds(row * BPD + half * HALF, HALF)]
        way = 0 if right else 1
        return to(
            z_r if right else z_l, src, dst, ag_send.at[h, s - 1, half, way],
            ag_recv.at[h, s - 1, half, way],
        )

    def gather_moves(s):
        return [
            (half, right)
            for half in (0, 1)
            for right in (True, False)
            if s < 4 or right == (half == 0)
        ]

    def gather_start(h):
        for half, right in gather_moves(1):
            gather_copy(h, 1, half, right).start()

    def gather_step(h, s):
        for half, right in gather_moves(s - 1):
            gather_copy(h, s - 1, half, right).wait_recv()
            if (half, right) in gather_moves(s):
                gather_copy(h, s, half, right).start()

    def gather_end(h):
        for half, right in gather_moves(4):
            gather_copy(h, 4, half, right).wait_recv()

    def gather_sent(h):
        for s in (1, 2, 3, 4):
            for half, right in gather_moves(s):
                gather_copy(h, s, half, right).wait_send()

    def place_own(h):
        @pl.loop(0, BPD)
        def _(b):
            table[h][z * BPD + b] = kv[h, b]

    def relay_copy(h, side):
        return to(
            (x_r, x_l)[side], relay_out[h].at[side], relay_in[h].at[1 - side],
            f1_send.at[h, side], f1_recv.at[h, side],
        )

    def merged_copy(h, side):
        return to(
            (x_r, x_l)[side],
            merged_out[h].at[side],
            received[h].at[pl.ds((FROM_L, FROM_R)[side], MERGED)],
            f2_send.at[h, side],
            f2_recv.at[h, side],
        )

    def send_relays(h):
        @pl.loop(0, RELAY)
        def _(k):
            relay_out[h][0, k] = table[h][relay_t[h, p_o * 2 * RELAY + RELAY + k]]
            relay_out[h][1, k] = table[h][relay_t[h, p_o * 2 * RELAY + k]]

        corner = jnp.where(x == 0, table[h][0], table[h][TARGETS - 1])
        relay_out[h][0, RELAY] = corner
        relay_out[h][1, RELAY] = corner
        for side in (0, 1):
            relay_copy(h, side).start()

        @pl.loop(0, MAIN)
        def _(k):
            received[h][OWN + k] = table[h][merged_t[h, x * RECEIVED + OWN + k]]

    def send_merged(h):
        for side in (0, 1):
            relay_copy(h, side).wait_recv()

        @pl.loop(0, MAIN)
        def _(k):
            for side, plane, first, back in ((0, p_r, FROM_L, 1), (1, p_l, FROM_R, 0)):
                code = merged_t[h, plane * RECEIVED + first + k]
                direct = table[h][jnp.minimum(code, TARGETS - 1)]
                passed = relay_in[h][back, jnp.maximum(code - TARGETS, 0)]
                merged_out[h][side, k] = jnp.where(code < TARGETS, direct, passed)

        merged_out[h][0, MAIN] = relay_in[h][1, RELAY]
        merged_out[h][1, MAIN] = relay_in[h][0, RELAY]
        merged_out[h][0, MAIN + 1] = table[h][TARGETS - 1]
        merged_out[h][1, MAIN + 1] = table[h][0]
        for side in (0, 1):
            merged_copy(h, side).start()

    def compute(h):
        for side in (0, 1):
            merged_copy(h, side).wait_recv()
        above = jnp.where(
            z > 0,
            table[h][lax.rem(z + NZ - 1, NZ) * BPD + BPD - 1],
            received[h][FROM_L + MAIN + 1],
        )
        below = jnp.where(z < NZ - 1, table[h][lax.rem(z + 1, NZ) * BPD], received[h][FROM_R + MAIN + 1])
        relay_r, relay_l = relay_in[h][0, RELAY], relay_in[h][1, RELAY]
        first = jnp.where(
            x == 0,
            table[h][0],
            jnp.where(x == 1, relay_l, jnp.where(x == 3, relay_r, received[h][FROM_L + MAIN])),
        )
        last = jnp.where(
            x == 3,
            table[h][TARGETS - 1],
            jnp.where(x == 2, relay_r, jnp.where(x == 0, relay_l, received[h][FROM_R + MAIN])),
        )
        for p in (0, 1):
            wide[p, 0:BLOCK] = above[p]
            wide[p, BLOCK * (BPD + 1) : BLOCK * (BPD + 2)] = below[p]
            anchor_kv[p, 0:BLOCK] = first[p]
            anchor_kv[p, BLOCK : 2 * BLOCK] = last[p]
            for b in range(BPD):
                wide[p, BLOCK * (b + 1) : BLOCK * (b + 2)] = kv[h, b, p]
        near[h][...] = jnp.zeros_like(near[h])
        anchor_acc[h][...] = jnp.zeros_like(anchor_acc[h])
        column = lax.broadcasted_iota(jnp.int32, (1, 8 * BLOCK), 1)

        @pl.loop(0, BPD)
        def _(i):
            rows = pl.ds(pl.multiple_of(i * BLOCK, BLOCK), 3 * BLOCK)
            spots = [place_t[h, i * R + r] for r in range(R)]
            keys, values = (
                jnp.concatenate(
                    [wide[p, rows], anchor_kv[p]] + [received[h][s, p] for s in spots], axis=0
                )
                for p in (0, 1)
            )
            q, g = query[h, i], grad[h, i]
            block = ctx * BPD + i
            low = jnp.where(block == 0, BLOCK, 0)
            cut = jnp.where(block == NX * NZ * BPD - 1, 2 * BLOCK, 3 * BLOCK)
            masked = (column < low) | ((column >= cut) & (column < 3 * BLOCK))
            contract_last = (((1,), (1,)), ((), ()))
            contract_first = (((0,), (0,)), ((), ()))
            scores = lax.dot_general(q, keys, contract_last, preferred_element_type=F32) * SCALE
            scores = jnp.where(masked, -1e30, scores)
            powers = jnp.exp(scores - jnp.max(scores, axis=-1, keepdims=True))
            probs = powers * (1.0 / jnp.sum(powers, axis=-1, keepdims=True))
            low_probs = probs.astype(BF16)
            attended = jnp.dot(low_probs, values, preferred_element_type=F32).astype(BF16)
            out_o[h, i] = attended
            delta = jnp.sum(g.astype(F32) * attended.astype(F32), axis=-1, keepdims=True)
            grad_probs = lax.dot_general(g, values, contract_last, preferred_element_type=F32)
            grad_scores = (probs * (grad_probs - delta)).astype(BF16)
            out_q[h, i] = (
                jnp.dot(grad_scores, keys, preferred_element_type=F32) * SCALE
            ).astype(BF16)
            key_part = (
                lax.dot_general(grad_scores, q, contract_first, preferred_element_type=F32) * SCALE
            )
            value_part = lax.dot_general(
                low_probs, g, contract_first, preferred_element_type=F32
            )
            for p, part in ((0, key_part), (1, value_part)):
                near[h][p, rows] += part[: 3 * BLOCK]
                anchor_acc[h][p] += part[3 * BLOCK : 5 * BLOCK]
                for r in range(R):
                    terms[i * R + r, p] = part[(5 + r) * BLOCK : (6 + r) * BLOCK].astype(BF16)

    def terms_copy(h, side):
        return to(
            (x_r, x_l)[side],
            merged_out[h].at[side],
            terms_in[h].at[pl.ds((FROM_L, FROM_R)[side], MERGED)],
            b1_send.at[h, side],
            b1_recv.at[h, side],
        )

    def terms_relay_copy(h, side):
        return to(
            (x_r, x_l)[side], relay_out[h].at[side], terms_relay[h].at[1 - side],
            b2_send.at[h, side], b2_recv.at[h, side],
        )

    def anchor(h, which):
        return anchor_acc[h][:, which * BLOCK : (which + 1) * BLOCK]

    def send_terms(h):
        for side in (0, 1):
            merged_copy(h, side).wait_send()

        @pl.loop(0, MAIN)
        def _(k):
            merged_out[h][0, k] = terms[giver_t[h, FROM_R + k]]
            merged_out[h][1, k] = terms[giver_t[h, FROM_L + k]]
            terms_in[h][B_OWN + k] = terms[giver_t[h, OWN + k]]

        terms_in[h][B_ZERO] = jnp.zeros((2, BLOCK, HD), BF16)
        merged_out[h][0, MAIN] = anchor(h, 1).astype(BF16)
        merged_out[h][1, MAIN] = anchor(h, 0).astype(BF16)
        merged_out[h][0, MAIN + 1] = near[h][:, (BPD + 1) * BLOCK :].astype(BF16)
        merged_out[h][1, MAIN + 1] = near[h][:, :BLOCK].astype(BF16)
        for side in (0, 1):
            terms_copy(h, side).start()

    def relay_terms(h):
        for side in (0, 1):
            relay_copy(h, side).wait_send()
            terms_copy(h, side).wait_recv()

        @pl.loop(0, RELAY)
        def _(k):
            from_left = count_t[h, p_l * 2] + k
            from_right = count_t[h, p_r * 2 + 1] + k
            relay_out[h][0, k] = terms_in[h][FROM_L + jnp.minimum(from_left, MAIN - 1)]
            relay_out[h][1, k] = terms_in[h][FROM_R + jnp.minimum(from_right, MAIN - 1)]

        first, last = anchor(h, 0), anchor(h, 1)
        relay_out[h][0, RELAY] = jnp.where(
            x == 3, first, last + terms_in[h][FROM_L + MAIN].astype(F32)
        ).astype(BF16)
        relay_out[h][1, RELAY] = jnp.where(
            x == 0, last, first + terms_in[h][FROM_R + MAIN].astype(F32)
        ).astype(BF16)
        for side in (0, 1):
            terms_relay_copy(h, side).start()

    def gather_terms(h):
        gather_sent(h)
        for side in (0, 1):
            terms_relay_copy(h, side).wait_recv()

        @pl.loop(0, RELAY)
        def _(k):
            terms_in[h][B_RR + k] = terms_relay[h][0, k]
            terms_in[h][B_RL + k] = terms_relay[h][1, k]

        @pl.loop(0, TARGETS)
        def _(t):
            total = terms_in[h][source_t[h, t * DEEP]].astype(F32)
            for k in range(1, DEEP):
                total += terms_in[h][source_t[h, t * DEEP + k]].astype(F32)
            table[h][t] = total.astype(BF16)

        def add(t, part):
            table[h][t] = (table[h][t].astype(F32) + part).astype(BF16)

        relayed = terms_relay[h][0, RELAY].astype(F32) + terms_relay[h][1, RELAY].astype(F32)

        @pl.when(x == 0)
        def _():
            add(0, anchor(h, 0) + relayed)

        @pl.when(x == NX - 1)
        def _():
            add(TARGETS - 1, anchor(h, 1) + relayed)

        @pl.when(z == NZ - 1)
        def _():
            add(0, terms_in[h][FROM_L + MAIN + 1].astype(F32))

        @pl.when(z == 0)
        def _():
            add(TARGETS - 1, terms_in[h][FROM_R + MAIN + 1].astype(F32))

        @pl.when(z > 0)
        def _():
            add((z - 1) * BPD + BPD - 1, near[h][:, :BLOCK])

        @pl.when(z < NZ - 1)
        def _():
            add((z + 1) * BPD, near[h][:, (BPD + 1) * BLOCK :])

    def sum_copy(h, s, half, right):
        row = lax.rem(z + 5 - s, NZ) if right else lax.rem(z + NZ - 5 + s, NZ)
        way = 0 if right else 1
        return to(
            z_r if right else z_l,
            table[h].at[pl.ds(row * BPD + half * HALF, HALF)],
            (sums_r if right else sums_l)[h].at[s - 1, pl.ds(half * HALF, HALF)],
            rs_send.at[h, s - 1, half, way],
            rs_recv.at[h, s - 1, half, way],
        )

    def sum_moves(s):
        return gather_moves(4 if s == 1 else 1)

    def sum_step(h, s):
        for half, right in sum_moves(s):
            if s > 1 and (half, right) in sum_moves(s - 1):
                sum_copy(h, s - 1, half, right).wait_recv()
                row = lax.rem(z + 5 - s, NZ) if right else lax.rem(z + NZ - 5 + s, NZ)
                came = (sums_r if right else sums_l)[h]

                @pl.loop(0, HALF)
                def _(b):
                    here = row * BPD + half * HALF + b
                    table[h][here] = (
                        table[h][here].astype(F32) + came[s - 2, half * HALF + b].astype(F32)
                    ).astype(BF16)

            sum_copy(h, s, half, right).start()

    def finish(h):
        for half, right in sum_moves(4):
            sum_copy(h, 4, half, right).wait_recv()

        @pl.loop(0, BPD)
        def _(b):
            total = (
                table[h][z * BPD + b].astype(F32)
                + sums_r[h][3, b].astype(F32)
                + sums_l[h][3, b].astype(F32)
                + near[h][:, pl.ds(pl.multiple_of((b + 1) * BLOCK, BLOCK), BLOCK)]
            ).astype(BF16)
            out_k[h, b] = total[0]
            out_v[h, b] = total[1]

    def drain(h):
        for s in (1, 2, 3, 4):
            for half, right in sum_moves(s):
                sum_copy(h, s, half, right).wait_send()
        for side in (0, 1):
            terms_copy(h, side).wait_send()
            terms_relay_copy(h, side).wait_send()

    gather_start(0)
    for h in range(H):
        place_own(h)
    for h in range(H):
        gather_step(h, 2)
        if h > 0:
            send_merged(h - 1)
        gather_step(h, 3)
        gather_step(h, 4)
        if h + 1 < H:
            gather_start(h + 1)
        gather_end(h)
        send_relays(h)
        if h > 1:
            compute(h - 2)
            send_terms(h - 2)
        if h > 2:
            relay_terms(h - 3)
    send_merged(H - 1)
    compute(H - 2)
    send_terms(H - 2)
    gather_terms(0)
    for s in (1, 2):
        sum_step(0, s)
    relay_terms(1)
    for s in (3, 4):
        sum_step(0, s)
    compute(H - 1)
    send_terms(H - 1)
    gather_terms(1)
    for s in (1, 2):
        sum_step(1, s)
    relay_terms(2)
    for s in (3, 4):
        sum_step(1, s)
    finish(0)
    relay_terms(3)
    gather_terms(2)
    for s in (1, 2, 3, 4):
        sum_step(2, s)
    finish(1)
    gather_terms(3)
    for s in (1, 2, 3, 4):
        sum_step(3, s)
    finish(2)
    finish(3)
    for h in range(H):
        drain(h)


def local(query, key, value, out_grad, random_links):
    def head_major(array):
        return array.reshape(BPD, BLOCK, H, HD).transpose(2, 0, 1, 3)

    def seq_major(array):
        return array.transpose(1, 2, 0, 3).reshape(BPD * BLOCK, H, HD)

    tables = slot_tables(random_links)
    kv = jnp.stack((head_major(key), head_major(value)), axis=2)
    slots = (2, BLOCK, HD)

    def per_head(*shape, dtype=BF16):
        return [pltpu.VMEM(shape, dtype) for _ in range(H)]

    dma = pltpu.SemaphoreType.DMA
    vmem = pl.BlockSpec(memory_space=pltpu.VMEM)
    smem = pl.BlockSpec(memory_space=pltpu.SMEM)
    outs = pl.pallas_call(
        kernel,
        out_shape=[jax.ShapeDtypeStruct((H, BPD, BLOCK, HD), BF16)] * 4,
        in_specs=[vmem] * 3 + [smem] * len(tables),
        out_specs=[vmem] * 4,
        scratch_shapes=[
            per_head(TARGETS, *slots),
            per_head(2, RELAYED, *slots),
            per_head(2, RELAYED, *slots),
            per_head(2, MERGED, *slots),
            per_head(RECEIVED, *slots),
            per_head(B_SIZE, *slots),
            per_head(2, RELAYED, *slots),
            per_head(4, BPD, *slots),
            per_head(4, BPD, *slots),
            per_head(2, (BPD + 2) * BLOCK, HD, dtype=F32),
            per_head(2, 2 * BLOCK, HD, dtype=F32),
            pltpu.VMEM((2, 2 * BLOCK, HD), BF16),
            pltpu.VMEM((2, (BPD + 2) * BLOCK, HD), BF16),
            pltpu.VMEM((REFS, *slots), BF16),
            dma((H, 4, 2, 2)),
            dma((H, 4, 2, 2)),
            dma((H, 2)),
            dma((H, 2)),
            dma((H, 2)),
            dma((H, 2)),
            dma((H, 2)),
            dma((H, 2)),
            dma((H, 2)),
            dma((H, 2)),
            dma((H, 4, 2, 2)),
            dma((H, 4, 2, 2)),
        ],
        compiler_params=pltpu.CompilerParams(
            collective_id=0, has_side_effects=True, vmem_limit_bytes=60 * 2**20
        ),
        cost_estimate=pl.CostEstimate(
            flops=2 * 6 * BLOCK * 8 * BLOCK * HD * H * BPD,
            bytes_accessed=4 * 2**20,
            transcendentals=H * BPD * BLOCK * 8 * BLOCK,
        ),
    )(kv, head_major(query), head_major(out_grad), *tables)
    return tuple(seq_major(array) for array in outs)


def solution(mesh):
    split = P("ctx", "head", None)
    return jax.shard_map(
        local,
        mesh=mesh,
        in_specs=(split, split, split, split, P(None, "head", None)),
        out_specs=(split, split, split, split),
        check_vma=False,
    )
```

```python
import math

import jax
import jax.numpy as jnp
from jax import lax
from jax.experimental import pallas as pl
from jax.experimental.pallas import tpu as pltpu
from jax.sharding import PartitionSpec as P

BLOCK = 64
HD = 128
NX = 4
NZ = 8
BPD = 8
HALF = BPD // 2
H = 4
R = 3
REFS = BPD * R
TARGETS = NZ * BPD
MAIN = 16
RELAY = 8
UNITS = 2 * H
FROM_R, FROM_L, OWN = 0, MAIN, 2 * MAIN
RECEIVED = OWN + MAIN
B_RR = 2 * MAIN
B_RL = B_RR + RELAY
B_OWN = B_RL + RELAY
B_ZERO = B_OWN + MAIN
B_SIZE = B_ZERO + 1
PIECES = 2
DEEP = 8
F32 = jnp.float32
BF16 = jnp.bfloat16
MESH = pl.DeviceIdType.MESH
SCALE = 1.0 / math.sqrt(HD)


def slot_tables(links):
    ctx = lax.axis_index("ctx")
    x, z = ctx // NZ, ctx % NZ
    row = lax.dynamic_slice_in_dim(links.reshape(NX, NZ, BPD, H, R), z, 1, 1)[:, 0]
    named = row.transpose(2, 0, 1, 3).reshape(H, NX, REFS)
    planes = jnp.arange(NX, dtype=jnp.int32)
    away = (named // TARGETS - planes[None, :, None]) % NX
    target = named % TARGETS
    entry = jnp.arange(REFS, dtype=jnp.int32)
    before = entry[None, :] < entry[:, None]
    rank = jnp.sum(
        ((away[..., None, :] == away[..., :, None]) & before).astype(jnp.int32), axis=-1
    )
    n_r = jnp.sum((away == 1).astype(jnp.int32), axis=-1)
    n_o = jnp.sum((away == 2).astype(jnp.int32), axis=-1)
    n_l = jnp.sum((away == 3).astype(jnp.int32), axis=-1)
    by_right = jnp.minimum(n_o, jnp.minimum(RELAY, MAIN - n_r))[..., None]
    right_way = rank < by_right
    place = jnp.where(
        away == 0,
        OWN + rank,
        jnp.where(
            away == 1,
            FROM_R + rank,
            jnp.where(
                away == 3,
                FROM_L + rank,
                jnp.where(
                    right_way,
                    FROM_R + n_r[..., None] + rank,
                    FROM_L + n_l[..., None] + rank - by_right,
                ),
            ),
        ),
    )
    relay_rank = jnp.where(right_way, rank, rank - by_right)
    code = jnp.where(away == 2, TARGETS + relay_rank, target)
    spots = jnp.arange(RECEIVED, dtype=jnp.int32)
    hit = place[..., None] == spots
    merged = jnp.sum(jnp.where(hit, code[..., None], 0), axis=2)
    relay_place = jnp.where(away == 2, jnp.where(right_way, 0, RELAY) + relay_rank, -1)
    relays = jnp.sum(
        jnp.where(
            relay_place[..., None] == jnp.arange(2 * RELAY, dtype=jnp.int32), target[..., None], 0
        ),
        axis=2,
    )
    own_place = lax.dynamic_slice_in_dim(place, x, 1, 1)[:, 0]
    giver = jnp.sum(
        jnp.where(own_place[..., None] == spots, entry[None, :, None], 0), axis=1
    )
    landing = jnp.where(
        away == 0,
        B_OWN + rank,
        jnp.where(
            away == 1,
            FROM_L + rank,
            jnp.where(
                away == 3, FROM_R + rank, jnp.where(right_way, B_RL, B_RR) + relay_rank
            ),
        ),
    ).reshape(H, NX * REFS)
    here = jnp.where(named // TARGETS == x, target, -1).reshape(H, NX * REFS)
    every = jnp.arange(NX * REFS, dtype=jnp.int32)
    same = (here[:, None, :] == here[:, :, None]) & (every[None, :] < every[:, None])
    depth = jnp.sum(same.astype(jnp.int32), axis=-1)
    cell = jnp.where(here >= 0, here * DEEP + depth, -1)
    cells = jnp.arange(TARGETS * DEEP, dtype=jnp.int32)
    sources = B_ZERO + jnp.sum(
        jnp.where(cell[:, :, None] == cells, landing[:, :, None] - B_ZERO, 0), axis=1
    )
    counts = jnp.stack((n_r, n_l), axis=-1).reshape(H, 2 * NX)
    return (
        merged.reshape(H, NX * RECEIVED),
        relays.reshape(H, NX * 2 * RELAY),
        own_place,
        giver,
        counts,
        sources,
    )


ORDER = (
    ("GS", 0), ("PO", 0), ("PO", 1), ("PO", 2), ("PO", 3), ("G", 0, 2, 0), ("G", 0, 2, 1),
    ("G", 0, 3, 0), ("G", 0, 3, 1), ("GS", 1), ("G", 0, 4, 0), ("G", 0, 4, 1), ("G", 1, 2, 0),
    ("G", 1, 2, 1), ("GE", 0), ("SR", 0), ("G", 1, 3, 0), ("G", 1, 3, 1), ("GS", 2),
    ("G", 1, 4, 0), ("SM", 0), ("G", 1, 4, 1), ("G", 2, 2, 0), ("G", 2, 2, 1), ("GE", 1),
    ("SR", 1), ("G", 2, 3, 0), ("G", 2, 3, 1), ("GS", 3), ("G", 2, 4, 0), ("SM", 1),
    ("G", 2, 4, 1), ("G", 3, 2, 0), ("G", 3, 2, 1), ("GE", 2), ("SR", 2), ("G", 3, 3, 0),
    ("G", 3, 3, 1), ("C", 0, 0), ("SM", 2), ("G", 3, 4, 0), ("G", 3, 4, 1), ("C", 0, 1), ("ST", 0),
    ("GE", 3), ("SR", 3), ("ST", 1), ("GS", 4), ("G", 4, 2, 0), ("G", 4, 2, 1), ("G", 4, 3, 0),
    ("G", 4, 3, 1), ("GS", 5), ("RT", 0), ("G", 4, 4, 0), ("G", 4, 4, 1), ("SM", 3),
    ("G", 5, 2, 0), ("G", 5, 2, 1), ("GE", 4), ("SR", 4), ("G", 5, 3, 0), ("RT", 1),
    ("G", 5, 3, 1), ("GS", 6), ("G", 5, 4, 0), ("L", 0), ("R", 0, 1), ("SS", 0), ("R", 0, 2),
    ("G", 5, 4, 1), ("R", 0, 3), ("R", 0, 4), ("R", 0, 5), ("G", 6, 2, 0), ("G", 6, 2, 1),
    ("S", 0, 2, 0), ("S", 0, 2, 1), ("C", 1, 0), ("SM", 4), ("G", 6, 3, 0), ("G", 6, 3, 1),
    ("GE", 5), ("SR", 5), ("S", 0, 3, 0), ("C", 1, 1), ("S", 0, 3, 1), ("L", 1), ("ST", 2),
    ("G", 6, 4, 0), ("G", 6, 4, 1), ("R", 1, 1), ("SS", 1), ("R", 1, 2), ("R", 1, 3),
    ("S", 0, 4, 0), ("R", 1, 4), ("R", 1, 5), ("ST", 3), ("S", 0, 4, 1), ("GS", 7), ("GE", 6),
    ("SR", 6), ("SM", 5), ("S", 1, 2, 0), ("S", 1, 2, 1), ("F", 0), ("G", 7, 2, 0), ("RT", 2),
    ("G", 7, 2, 1), ("S", 1, 3, 0), ("S", 1, 3, 1), ("G", 7, 3, 0), ("RT", 3), ("G", 7, 3, 1),
    ("S", 1, 4, 0), ("SM", 6), ("S", 1, 4, 1), ("G", 7, 4, 0), ("G", 7, 4, 1), ("C", 2, 0),
    ("L", 2), ("F", 1), ("R", 2, 1), ("SS", 2), ("R", 2, 2), ("R", 2, 3), ("R", 2, 4), ("R", 2, 5),
    ("GE", 7), ("SR", 7), ("L", 3), ("R", 3, 1), ("SS", 3), ("R", 3, 2), ("R", 3, 3),
    ("S", 2, 2, 0), ("S", 2, 2, 1), ("R", 3, 4), ("R", 3, 5), ("C", 2, 1), ("S", 2, 3, 0),
    ("S", 3, 2, 0), ("S", 2, 3, 1), ("S", 3, 2, 1), ("ST", 4), ("ST", 5), ("SM", 7),
    ("S", 2, 4, 0), ("S", 3, 3, 0), ("S", 2, 4, 1), ("S", 3, 3, 1), ("RT", 4), ("S", 3, 4, 0),
    ("F", 2), ("S", 3, 4, 1), ("RT", 5), ("F", 3), ("C", 3, 0), ("L", 4), ("R", 4, 1), ("SS", 4),
    ("R", 4, 2), ("R", 4, 3), ("R", 4, 4), ("R", 4, 5), ("C", 3, 1), ("S", 4, 2, 0),
    ("S", 4, 2, 1), ("L", 5), ("ST", 6), ("R", 5, 1), ("SS", 5), ("R", 5, 2), ("R", 5, 3),
    ("R", 5, 4), ("R", 5, 5), ("ST", 7), ("S", 4, 3, 0), ("S", 4, 3, 1), ("S", 5, 2, 0),
    ("S", 5, 2, 1), ("S", 4, 4, 0), ("RT", 6), ("S", 4, 4, 1), ("S", 5, 3, 0), ("S", 5, 3, 1),
    ("RT", 7), ("F", 4), ("S", 5, 4, 0), ("L", 6), ("R", 6, 1), ("SS", 6), ("S", 5, 4, 1),
    ("R", 6, 2), ("R", 6, 3), ("R", 6, 4), ("R", 6, 5), ("L", 7), ("R", 7, 1), ("SS", 7),
    ("R", 7, 2), ("S", 6, 2, 0), ("S", 6, 2, 1), ("R", 7, 3), ("R", 7, 4), ("F", 5), ("R", 7, 5),
    ("S", 7, 2, 0), ("S", 7, 2, 1), ("S", 6, 3, 0), ("S", 6, 3, 1), ("S", 7, 3, 0), ("S", 7, 3, 1),
    ("S", 6, 4, 0), ("S", 6, 4, 1), ("S", 7, 4, 0), ("S", 7, 4, 1), ("F", 6), ("F", 7),
)


def kernel(
    kv,
    query,
    grad,
    merged_t,
    relay_t,
    place_t,
    giver_t,
    count_t,
    source_t,
    out_o,
    out_q,
    out_k,
    out_v,
    table,
    relay_out,
    relay_in,
    merged_out,
    received,
    terms_in,
    terms_relay,
    sums_r,
    sums_l,
    near,
    anchor_acc,
    anchor_in,
    part_out,
    part_in,
    edge_out,
    edge_in,
    edge_part_out,
    edge_part_in,
    anchor_kv,
    wide,
    terms,
    ag_sem,
    rs_sem,
    x_sem,
    anchor_sem,
    part_sem,
    edge_sem,
):
    ctx = lax.axis_index("ctx")
    x, z = ctx // NZ, ctx % NZ
    z_r = x * NZ + lax.rem(z + 1, NZ)
    z_l = x * NZ + lax.rem(z + NZ - 1, NZ)
    p_r = lax.rem(x + 1, NX)
    p_l = lax.rem(x + NX - 1, NX)
    p_o = lax.rem(x + 2, NX)
    x_r = p_r * NZ + z
    x_l = p_l * NZ + z
    outer = (x == 0) | (x == NX - 1)
    inner = (x == 1) | (x == NX - 2)
    rim = (z == 0) | (z == NZ - 1)
    beyond = lax.rem(jnp.where(z == 0, ctx + NX * NZ - 1, ctx + 1), NX * NZ)

    def to(device, src, dst, sems):
        return pltpu.make_async_remote_copy(
            src_ref=src,
            dst_ref=dst,
            send_sem=sems.at[0],
            recv_sem=sems.at[1],
            device_id={"ctx": device},
            device_id_type=MESH,
        )

    barrier = pltpu.get_barrier_semaphore()

    def greet(device):
        pl.semaphore_signal(barrier, inc=1, device_id={"ctx": device}, device_id_type=MESH)

    for device in (z_r, z_l, x_r, x_l):
        greet(device)

    @pl.when(rim)
    def _():
        greet(beyond)

    pl.semaphore_wait(barrier, 4 + rim.astype(jnp.int32))

    def gather_copy(u, s, half, right):
        row = lax.rem(z + NZ - (s - 1), NZ) if right else lax.rem(z + s - 1, NZ)
        cut = pl.ds(row * BPD + half * HALF, HALF)
        src = kv.at[u, pl.ds(half * HALF, HALF)] if s == 1 else table[u].at[cut]
        way = 0 if right else 1
        return to(z_r if right else z_l, src, table[u].at[cut], ag_sem.at[u, s - 1, half, way])

    def moves(s):
        return [
            (half, right)
            for half in (0, 1)
            for right in (True, False)
            if s < 4 or right == (half == 0)
        ]

    def gather_start(u):
        for half, right in moves(1):
            gather_copy(u, 1, half, right).start()

    def gather_step(u, s, half):
        for right in (True, False):
            gather_copy(u, s - 1, half, right).wait_recv()
            if (half, right) in moves(s):
                gather_copy(u, s, half, right).start()

    def gather_end(u):
        for half, right in moves(4):
            gather_copy(u, 4, half, right).wait_recv()

    def gather_sent(u):
        for s in (1, 2, 3, 4):
            for half, right in moves(s):
                gather_copy(u, s, half, right).wait_send()

    def place_own(h):
        for p in (0, 1):

            @pl.loop(0, BPD)
            def _(b):
                table[2 * h + p][z * BPD + b] = kv[2 * h + p, b]

    def edge_copy():
        return to(beyond, edge_out, edge_in, edge_sem.at[UNITS])

    def send_edges():
        @pl.when(rim)
        def _():
            @pl.loop(0, UNITS)
            def _(u):
                edge_out[u] = kv[u, jnp.where(z == 0, 0, BPD - 1)]

            edge_copy().start()

    def relay_copy(u, side):
        return to(
            (x_r, x_l)[side], relay_out[u].at[side], relay_in[u].at[1 - side], x_sem.at[0, u, side]
        )

    def merged_copy(u, side):
        return to(
            (x_r, x_l)[side],
            merged_out[u].at[side],
            received[u].at[pl.ds((FROM_L, FROM_R)[side], MAIN)],
            x_sem.at[1, u, side],
        )

    def anchor_copy(u, side):
        return to(
            (x_r, x_l)[side],
            table[u].at[jnp.where(x == 0, 0, TARGETS - 1)],
            anchor_in.at[u, 0],
            anchor_sem.at[u, side],
        )

    def anchor_arrived(u):
        @pl.when((x == 0) | (x == 1))
        def _():
            anchor_copy(u, 0).wait_recv()

        @pl.when((x == 2) | (x == 3))
        def _():
            anchor_copy(u, 1).wait_recv()

    def anchor_pass(u):
        return to(
            jnp.where(x == 1, x_r, x_l), anchor_in.at[u, 0], anchor_in.at[u, 1], anchor_sem.at[u, 2]
        )

    def send_relays(u):
        h = u // 2

        @pl.when(outer)
        def _():
            for side in (0, 1):
                anchor_copy(u, side).start()

        @pl.loop(0, RELAY)
        def _(k):
            relay_out[u][0, k] = table[u][relay_t[h, p_o * 2 * RELAY + RELAY + k]]
            relay_out[u][1, k] = table[u][relay_t[h, p_o * 2 * RELAY + k]]

        for side in (0, 1):
            relay_copy(u, side).start()

        @pl.loop(0, MAIN)
        def _(k):
            received[u][OWN + k] = table[u][merged_t[h, x * RECEIVED + OWN + k]]

    def send_merged(u):
        h = u // 2
        for side in (0, 1):
            relay_copy(u, side).wait_recv()

        @pl.loop(0, MAIN)
        def _(k):
            for side, plane, first, back in ((0, p_r, FROM_L, 1), (1, p_l, FROM_R, 0)):
                code = merged_t[h, plane * RECEIVED + first + k]
                direct = table[u][jnp.minimum(code, TARGETS - 1)]
                passed = relay_in[u][back, jnp.maximum(code - TARGETS, 0)]
                merged_out[u][side, k] = jnp.where(code < TARGETS, direct, passed)

        for side in (0, 1):
            merged_copy(u, side).start()
        anchor_arrived(u)

        @pl.when(inner)
        def _():
            anchor_pass(u).start()

    def lay_keys(h):
        for p in (0, 1):
            u = 2 * h + p
            for side in (0, 1):
                merged_copy(u, side).wait_recv()

            @pl.when(inner)
            def _():
                anchor_pass(u).wait_recv()

            row_above = lax.rem(z + NZ - 1, NZ) * BPD + BPD - 1
            row_below = lax.rem(z + 1, NZ) * BPD
            wide[p, 0:BLOCK] = jnp.where(z > 0, table[u][row_above], edge_in[u])
            wide[p, BLOCK * (BPD + 1) :] = jnp.where(z < NZ - 1, table[u][row_below], edge_in[u])
            for b in range(BPD):
                wide[p, BLOCK * (b + 1) : BLOCK * (b + 2)] = kv[u, b]
            came, passed = anchor_in[u, 0], anchor_in[u, 1]
            anchor_kv[p, :BLOCK] = jnp.where(x == 0, table[u][0], jnp.where(x == 2, passed, came))
            anchor_kv[p, BLOCK:] = jnp.where(
                x == 3, table[u][TARGETS - 1], jnp.where(x == 1, passed, came)
            )
        near[h][...] = jnp.zeros_like(near[h])
        anchor_acc[h][...] = jnp.zeros_like(anchor_acc[h])

    def compute(h, piece):
        if piece == 0:
            if h == 0:

                @pl.when(rim)
                def _():
                    edge_copy().wait_recv()

            lay_keys(h)
        column = lax.broadcasted_iota(jnp.int32, (1, 8 * BLOCK), 1)

        @pl.loop(piece * BPD // PIECES, (piece + 1) * BPD // PIECES)
        def _(i):
            rows = pl.ds(pl.multiple_of(i * BLOCK, BLOCK), 3 * BLOCK)
            spots = [place_t[h, i * R + r] for r in range(R)]
            keys, values = (
                jnp.concatenate(
                    [wide[p, rows], anchor_kv[p]] + [received[2 * h + p][s] for s in spots], axis=0
                )
                for p in (0, 1)
            )
            q, g = query[h, i], grad[h, i]
            block = ctx * BPD + i
            low = jnp.where(block == 0, BLOCK, 0)
            cut = jnp.where(block == NX * NZ * BPD - 1, 2 * BLOCK, 3 * BLOCK)
            masked = (column < low) | ((column >= cut) & (column < 3 * BLOCK))
            contract_last = (((1,), (1,)), ((), ()))
            contract_first = (((0,), (0,)), ((), ()))
            scores = lax.dot_general(q, keys, contract_last, preferred_element_type=F32) * SCALE
            scores = jnp.where(masked, -1e30, scores)
            powers = jnp.exp(scores - jnp.max(scores, axis=-1, keepdims=True))
            probs = powers * (1.0 / jnp.sum(powers, axis=-1, keepdims=True))
            low_probs = probs.astype(BF16)
            attended = jnp.dot(low_probs, values, preferred_element_type=F32).astype(BF16)
            out_o[h, i] = attended
            delta = jnp.sum(g.astype(F32) * attended.astype(F32), axis=-1, keepdims=True)
            grad_probs = lax.dot_general(g, values, contract_last, preferred_element_type=F32)
            grad_scores = (probs * (grad_probs - delta)).astype(BF16)
            out_q[h, i] = (
                jnp.dot(grad_scores, keys, preferred_element_type=F32) * SCALE
            ).astype(BF16)
            key_part = (
                lax.dot_general(grad_scores, q, contract_first, preferred_element_type=F32) * SCALE
            )
            value_part = lax.dot_general(
                low_probs, g, contract_first, preferred_element_type=F32
            )
            for p, part in ((0, key_part), (1, value_part)):
                near[h][p, rows] += part[: 3 * BLOCK]
                anchor_acc[h][p] += part[3 * BLOCK : 5 * BLOCK]
                for r in range(R):
                    terms[p, i * R + r] = part[(5 + r) * BLOCK : (6 + r) * BLOCK].astype(BF16)

    def terms_copy(u, side):
        return to(
            (x_r, x_l)[side],
            merged_out[u].at[side],
            terms_in[u].at[pl.ds((FROM_L, FROM_R)[side], MAIN)],
            x_sem.at[2, u, side],
        )

    def terms_relay_copy(u, side):
        return to(
            (x_r, x_l)[side], relay_out[u].at[side], terms_relay[u].at[1 - side],
            x_sem.at[3, u, side],
        )

    def part_first(u):
        return to(
            jnp.where(x == 1, x_r, x_l), part_out.at[u, 0], part_in.at[u, 0], part_sem.at[u, 0]
        )

    def part_second(u, side):
        return to(
            (x_r, x_l)[side], part_out.at[u, 1], part_in.at[u, 1 + side], part_sem.at[u, 1 + side]
        )

    def leftward():
        return (x == 0) | (x == 1)

    def edge_part_copy(u):
        return to(beyond, edge_part_out.at[u], edge_part_in.at[u], edge_sem.at[u])

    def anchor(u, which):
        return anchor_acc[u // 2][u % 2, which * BLOCK : (which + 1) * BLOCK]

    def near_rows(u, b):
        return near[u // 2][u % 2, (b + 1) * BLOCK : (b + 2) * BLOCK]

    def send_terms(u):
        h, p = u // 2, u % 2
        for side in (0, 1):
            merged_copy(u, side).wait_send()

        @pl.loop(0, MAIN)
        def _(k):
            merged_out[u][0, k] = terms[p, giver_t[h, FROM_R + k]]
            merged_out[u][1, k] = terms[p, giver_t[h, FROM_L + k]]
            terms_in[u][B_OWN + k] = terms[p, giver_t[h, OWN + k]]

        for side in (0, 1):
            terms_copy(u, side).start()
        terms_in[u][B_ZERO] = jnp.zeros((BLOCK, HD), BF16)

        @pl.when(inner)
        def _():
            part_out[u, 0] = jnp.where(x == 1, anchor(u, 1), anchor(u, 0)).astype(BF16)
            part_first(u).start()

        @pl.when(rim)
        def _():
            edge_part_out[u] = jnp.where(z == 0, near_rows(u, -1), near_rows(u, BPD)).astype(BF16)
            edge_part_copy(u).start()

    def relay_terms(u):
        h = u // 2
        for side in (0, 1):
            relay_copy(u, side).wait_send()
            terms_copy(u, side).wait_recv()

        @pl.loop(0, RELAY)
        def _(k):
            from_left = count_t[h, p_l * 2] + k
            from_right = count_t[h, p_r * 2 + 1] + k
            relay_out[u][0, k] = terms_in[u][FROM_L + jnp.minimum(from_left, MAIN - 1)]
            relay_out[u][1, k] = terms_in[u][FROM_R + jnp.minimum(from_right, MAIN - 1)]

        for side in (0, 1):
            terms_relay_copy(u, side).start()

        @pl.when(inner)
        def _():
            part_first(u).wait_recv()
            mine = jnp.where(x == 1, anchor(u, 0), anchor(u, 1))
            part_out[u, 1] = (mine + part_in[u, 0].astype(F32)).astype(BF16)

        @pl.when(outer)
        def _():
            part_out[u, 1] = jnp.where(x == 0, anchor(u, 1), anchor(u, 0)).astype(BF16)

        @pl.when(leftward())
        def _():
            part_second(u, 1).start()

        @pl.when(jnp.logical_not(leftward()))
        def _():
            part_second(u, 0).start()

    def land(u):
        gather_sent(u)

        @pl.when(outer)
        def _():
            for side in (0, 1):
                anchor_copy(u, side).wait_send()
                part_second(u, side).wait_recv()

        for side in (0, 1):
            terms_relay_copy(u, side).wait_recv()

        @pl.loop(0, RELAY)
        def _(k):
            terms_in[u][B_RR + k] = terms_relay[u][0, k]
            terms_in[u][B_RL + k] = terms_relay[u][1, k]

    def rows(u, group):
        h = u // 2
        for away in {1: (4,), 2: (3, 5), 3: (2, 6), 4: (1, 7), 5: (0,)}[group]:
            row = lax.rem(z + away, NZ)

            @pl.loop(0, BPD)
            def _(b):
                t = row * BPD + b
                total = terms_in[u][source_t[h, t * DEEP]].astype(F32)
                for k in range(1, DEEP):
                    total += terms_in[u][source_t[h, t * DEEP + k]].astype(F32)
                table[u][t] = total.astype(BF16)

            def add(t, part):
                table[u][t] = (table[u][t].astype(F32) + part).astype(BF16)

            def both():
                return part_in[u, 1].astype(F32) + part_in[u, 2].astype(F32)

            @pl.when((x == 0) & (row == 0))
            def _():
                add(0, anchor(u, 0) + both())

            @pl.when((x == NX - 1) & (row == NZ - 1))
            def _():
                add(TARGETS - 1, anchor(u, 1) + both())

            if away == NZ - 1:

                @pl.when(z > 0)
                def _():
                    add(row * BPD + BPD - 1, near_rows(u, -1))

            if away == 1:

                @pl.when(z < NZ - 1)
                def _():
                    add(row * BPD, near_rows(u, BPD))

    def sum_copy(u, s, half, right):
        row = lax.rem(z + 5 - s, NZ) if right else lax.rem(z + NZ - 5 + s, NZ)
        way = 0 if right else 1
        return to(
            z_r if right else z_l,
            table[u].at[pl.ds(row * BPD + half * HALF, HALF)],
            (sums_r if right else sums_l)[u].at[s - 1, pl.ds(half * HALF, HALF)],
            rs_sem.at[u, s - 1, half, way],
        )

    def sum_moves(s):
        return moves(4 if s == 1 else 1)

    def sum_start(u):
        for half, right in sum_moves(1):
            sum_copy(u, 1, half, right).start()

    def sum_step(u, s, half):
        for right in (True, False):
            if (half, right) in sum_moves(s - 1):
                sum_copy(u, s - 1, half, right).wait_recv()
                row = lax.rem(z + 5 - s, NZ) if right else lax.rem(z + NZ - 5 + s, NZ)
                came = (sums_r if right else sums_l)[u]

                @pl.loop(0, HALF)
                def _(b):
                    here = row * BPD + half * HALF + b
                    table[u][here] = (
                        table[u][here].astype(F32) + came[s - 2, half * HALF + b].astype(F32)
                    ).astype(BF16)

            sum_copy(u, s, half, right).start()

    def finish(u):
        h, p = u // 2, u % 2
        for half, right in sum_moves(4):
            sum_copy(u, 4, half, right).wait_recv()

        @pl.when(rim)
        def _():
            edge_part_copy(u).wait_recv()
            lone = pl.ds(pl.multiple_of(jnp.where(z == 0, 1, BPD) * BLOCK, BLOCK), BLOCK)
            near[h][p, lone] += edge_part_in[u].astype(F32)

        @pl.loop(0, BPD)
        def _(b):
            total = (
                table[u][z * BPD + b].astype(F32)
                + sums_r[u][3, b].astype(F32)
                + sums_l[u][3, b].astype(F32)
                + near[h][p, pl.ds(pl.multiple_of((b + 1) * BLOCK, BLOCK), BLOCK)]
            )
            (out_k, out_v)[p][h, b] = total.astype(BF16)

    def drain(u):
        for s in (1, 2, 3, 4):
            for half, right in sum_moves(s):
                sum_copy(u, s, half, right).wait_send()
        for side in (0, 1):
            terms_copy(u, side).wait_send()
            terms_relay_copy(u, side).wait_send()

        @pl.when(inner)
        def _():
            anchor_pass(u).wait_send()
            part_first(u).wait_send()

        @pl.when(leftward())
        def _():
            part_second(u, 1).wait_send()

        @pl.when(jnp.logical_not(leftward()))
        def _():
            part_second(u, 0).wait_send()

        @pl.when(rim)
        def _():
            edge_part_copy(u).wait_send()

    steps = {
        "GS": gather_start,
        "G": gather_step,
        "GE": gather_end,
        "PO": place_own,
        "SR": send_relays,
        "SM": send_merged,
        "C": compute,
        "ST": send_terms,
        "RT": relay_terms,
        "L": land,
        "R": rows,
        "SS": sum_start,
        "S": sum_step,
        "F": finish,
    }
    send_edges()
    for name, *where in ORDER:
        steps[name](*where)
    for u in range(UNITS):
        drain(u)

    @pl.when(rim)
    def _():
        edge_copy().wait_send()


def local(query, key, value, out_grad, random_links):
    def head_major(array):
        return array.reshape(BPD, BLOCK, H, HD).transpose(2, 0, 1, 3)

    def seq_major(array):
        return array.transpose(1, 2, 0, 3).reshape(BPD * BLOCK, H, HD)

    tables = slot_tables(random_links)
    kv = jnp.stack((head_major(key), head_major(value)), axis=1).reshape(UNITS, BPD, BLOCK, HD)
    block = (BLOCK, HD)

    def per(count, *shape, dtype=BF16):
        return [pltpu.VMEM(shape, dtype) for _ in range(count)]

    dma = pltpu.SemaphoreType.DMA
    vmem = pl.BlockSpec(memory_space=pltpu.VMEM)
    smem = pl.BlockSpec(memory_space=pltpu.SMEM)
    outs = pl.pallas_call(
        kernel,
        out_shape=[jax.ShapeDtypeStruct((H, BPD, BLOCK, HD), BF16)] * 4,
        in_specs=[vmem] * 3 + [smem] * len(tables),
        out_specs=[vmem] * 4,
        scratch_shapes=[
            per(UNITS, TARGETS, *block),
            per(UNITS, 2, RELAY, *block),
            per(UNITS, 2, RELAY, *block),
            per(UNITS, 2, MAIN, *block),
            per(UNITS, RECEIVED, *block),
            per(UNITS, B_SIZE, *block),
            per(UNITS, 2, RELAY, *block),
            per(UNITS, 4, BPD, *block),
            per(UNITS, 4, BPD, *block),
            per(H, 2, (BPD + 2) * BLOCK, HD, dtype=F32),
            per(H, 2, 2 * BLOCK, HD, dtype=F32),
            pltpu.VMEM((UNITS, 2, *block), BF16),
            pltpu.VMEM((UNITS, 2, *block), BF16),
            pltpu.VMEM((UNITS, 3, *block), BF16),
            pltpu.VMEM((UNITS, *block), BF16),
            pltpu.VMEM((UNITS, *block), BF16),
            pltpu.VMEM((UNITS, *block), BF16),
            pltpu.VMEM((UNITS, *block), BF16),
            pltpu.VMEM((2, 2 * BLOCK, HD), BF16),
            pltpu.VMEM((2, (BPD + 2) * BLOCK, HD), BF16),
            pltpu.VMEM((2, REFS, *block), BF16),
            dma((UNITS, 4, 2, 2, 2)),
            dma((UNITS, 4, 2, 2, 2)),
            dma((4, UNITS, 2, 2)),
            dma((UNITS, 3, 2)),
            dma((UNITS, 3, 2)),
            dma((UNITS + 1, 2)),
        ],
        compiler_params=pltpu.CompilerParams(
            collective_id=0, has_side_effects=True, vmem_limit_bytes=60 * 2**20
        ),
        cost_estimate=pl.CostEstimate(
            flops=2 * 6 * BLOCK * 8 * BLOCK * HD * H * BPD,
            bytes_accessed=4 * 2**20,
            transcendentals=H * BPD * BLOCK * 8 * BLOCK,
        ),
    )(kv, head_major(query), head_major(out_grad), *tables)
    return tuple(seq_major(array) for array in outs)


def solution(mesh):
    split = P("ctx", "head", None)
    return jax.shard_map(
        local,
        mesh=mesh,
        in_specs=(split, split, split, split, P(None, "head", None)),
        out_specs=(split, split, split, split),
        check_vma=False,
    )
```

```python
import math

import jax
import jax.numpy as jnp
from jax import lax
from jax.experimental import pallas as pl
from jax.experimental.pallas import tpu as pltpu
from jax.sharding import PartitionSpec as P

BLOCK = 64
HD = 128
NX = 4
NZ = 8
BPD = 8
HALF = BPD // 2
H = 4
R = 3
REFS = BPD * R
TARGETS = NZ * BPD
MAIN = 16
RELAY = 8
UNITS = 2 * H
FROM_R, FROM_L, OWN = 0, MAIN, 2 * MAIN
RECEIVED = OWN + MAIN
B_RR = 2 * MAIN
B_RL = B_RR + RELAY
B_OWN = B_RL + RELAY
B_ZERO = B_OWN + MAIN
B_SIZE = B_ZERO + 1
T_RELAY = RECEIVED
T_GIVER = T_RELAY + 2 * RELAY
T_PLACE = T_GIVER + RECEIVED
T_RIGHT = T_PLACE + REFS
T_LEFT = T_RIGHT + 1
T_SIZE = T_LEFT + 1
PIECES = 2
DEEP = 8
F32 = jnp.float32
BF16 = jnp.bfloat16
MESH = pl.DeviceIdType.MESH
SCALE = 1.0 / math.sqrt(HD)


def slot_tables(links):
    ctx = lax.axis_index("ctx")
    x, z = ctx // NZ, ctx % NZ
    row = lax.dynamic_slice_in_dim(links.reshape(NX, NZ, BPD, H, R), z, 1, 1)[:, 0]
    named = row.transpose(2, 0, 1, 3).reshape(H, NX, REFS)
    planes = jnp.arange(NX, dtype=jnp.int32)
    away = (named // TARGETS - planes[None, :, None]) % NX
    target = named % TARGETS
    entry = jnp.arange(REFS, dtype=jnp.int32)
    before = entry[None, :] < entry[:, None]
    rank = jnp.sum(
        ((away[..., None, :] == away[..., :, None]) & before).astype(jnp.int32), axis=-1
    )
    n_r = jnp.sum((away == 1).astype(jnp.int32), axis=-1)
    n_o = jnp.sum((away == 2).astype(jnp.int32), axis=-1)
    n_l = jnp.sum((away == 3).astype(jnp.int32), axis=-1)
    by_right = jnp.minimum(n_o, jnp.minimum(RELAY, MAIN - n_r))[..., None]
    right_way = rank < by_right
    place = jnp.where(
        away == 0,
        OWN + rank,
        jnp.where(
            away == 1,
            FROM_R + rank,
            jnp.where(
                away == 3,
                FROM_L + rank,
                jnp.where(
                    right_way,
                    FROM_R + n_r[..., None] + rank,
                    FROM_L + n_l[..., None] + rank - by_right,
                ),
            ),
        ),
    )
    relay_rank = jnp.where(right_way, rank, rank - by_right)
    code = jnp.where(away == 2, TARGETS + relay_rank, target)
    relay_place = jnp.where(away == 2, jnp.where(right_way, 0, RELAY) + relay_rank, -1)
    spots = jnp.arange(T_SIZE, dtype=jnp.int32)
    where = [place, relay_place + T_RELAY, place + T_GIVER, entry + T_PLACE]
    what = [code, target, entry, place]
    where[1] = jnp.where(relay_place >= 0, where[1], -1)
    lowest = (0, T_RELAY, T_GIVER, T_PLACE)
    at, put = (jnp.broadcast_to(a[0], named.shape)[..., None] for a in (where, what))
    for low, at_next, put_next in zip(lowest[1:], where[1:], what[1:]):
        at = jnp.where(spots >= low, jnp.broadcast_to(at_next, named.shape)[..., None], at)
        put = jnp.where(spots >= low, jnp.broadcast_to(put_next, named.shape)[..., None], put)
    hit = at == spots
    hit = jnp.where(spots == T_RIGHT, (away == 1)[..., None], hit)
    hit = jnp.where(spots == T_LEFT, (away == 3)[..., None], hit)
    put = jnp.where(spots >= T_RIGHT, 1, put)
    first = jnp.sum(jnp.where(hit, put, 0), axis=2)
    landing = jnp.where(
        away == 0,
        B_OWN + rank,
        jnp.where(
            away == 1,
            FROM_L + rank,
            jnp.where(
                away == 3, FROM_R + rank, jnp.where(right_way, B_RL, B_RR) + relay_rank
            ),
        ),
    ).reshape(H, NX * REFS)
    here = jnp.where(named // TARGETS == x, target, -1).reshape(H, NX * REFS)
    every = jnp.arange(NX * REFS, dtype=jnp.int32)
    same = (here[:, None, :] == here[:, :, None]) & (every[None, :] < every[:, None])
    depth = jnp.sum(same.astype(jnp.int32), axis=-1)
    cell = jnp.where(here >= 0, here * DEEP + depth, -1)
    cells = jnp.arange(TARGETS * DEEP, dtype=jnp.int32)
    sources = B_ZERO + jnp.sum(
        jnp.where(cell[:, :, None] == cells, landing[:, :, None] - B_ZERO, 0), axis=1
    )
    return first, sources


ORDER = (
    ("GS", 0), ("G", 0, 2, 0), ("G", 0, 2, 1), ("G", 0, 3, 0), ("G", 0, 3, 1), ("GS", 1),
    ("G", 0, 4, 0), ("G", 0, 4, 1), ("G", 1, 2, 0), ("G", 1, 2, 1), ("GE", 0), ("SR", 0),
    ("G", 1, 3, 0), ("G", 1, 3, 1), ("GS", 2), ("SM", 0), ("G", 1, 4, 0), ("G", 1, 4, 1),
    ("G", 2, 2, 0), ("GE", 1), ("G", 2, 2, 1), ("SR", 1), ("G", 2, 3, 0), ("G", 2, 3, 1),
    ("GS", 3), ("G", 2, 4, 0), ("SM", 1), ("G", 2, 4, 1), ("G", 3, 2, 0), ("GE", 2),
    ("G", 3, 2, 1), ("SR", 2), ("G", 3, 3, 0), ("C", 0, 0), ("SM", 2), ("G", 3, 3, 1), ("GS", 4),
    ("C", 0, 1), ("G", 3, 4, 0), ("G", 3, 4, 1), ("ST", 0), ("G", 4, 2, 0), ("G", 4, 2, 1),
    ("ST", 1), ("G", 4, 3, 0), ("GE", 3), ("G", 4, 3, 1), ("GS", 5), ("SR", 3), ("G", 4, 4, 0),
    ("RT", 0), ("G", 4, 4, 1), ("G", 5, 2, 0), ("G", 5, 2, 1), ("G", 5, 3, 0), ("GE", 4),
    ("G", 5, 3, 1), ("GS", 6), ("RT", 1), ("G", 5, 4, 0), ("SM", 3), ("G", 5, 4, 1),
    ("G", 6, 2, 0), ("SR", 4), ("L", 0), ("G", 6, 2, 1), ("R", 0, 2), ("GE", 5), ("SR", 5),
    ("R", 0, 3), ("G", 6, 3, 0), ("R", 0, 1), ("SM", 4), ("L", 1), ("R", 1, 2), ("R", 1, 1),
    ("G", 6, 3, 1), ("SS", 0), ("GS", 7), ("C", 1, 0), ("SM", 5), ("G", 6, 4, 0), ("G", 7, 2, 0),
    ("C", 1, 1), ("SS", 1), ("S", 0, 2, 0), ("ST", 2), ("R", 1, 5), ("G", 6, 4, 1), ("R", 1, 3),
    ("R", 0, 4), ("S", 1, 2, 0), ("ST", 3), ("C", 2, 0), ("G", 7, 2, 1), ("S", 0, 2, 1), ("RT", 2),
    ("GE", 6), ("S", 1, 2, 1), ("G", 7, 3, 0), ("C", 2, 1), ("S", 0, 3, 0), ("R", 1, 4),
    ("G", 7, 3, 1), ("RT", 3), ("ST", 5), ("L", 2), ("S", 1, 3, 0), ("R", 2, 2), ("S", 1, 3, 1),
    ("G", 7, 4, 0), ("L", 3), ("G", 7, 4, 1), ("S", 1, 4, 0), ("R", 3, 1), ("S", 1, 4, 1),
    ("R", 3, 5), ("S", 0, 3, 1), ("SS", 3), ("SR", 6), ("S", 0, 4, 0), ("R", 3, 3), ("R", 2, 1),
    ("R", 3, 2), ("GE", 7), ("R", 2, 3), ("SR", 7), ("S", 0, 4, 1), ("F", 1), ("SM", 6),
    ("S", 3, 2, 0), ("R", 2, 4), ("SS", 2), ("R", 3, 4), ("S", 3, 2, 1), ("R", 0, 5),
    ("S", 3, 3, 0), ("SM", 7), ("ST", 4), ("F", 0), ("S", 2, 2, 0), ("RT", 5), ("S", 2, 2, 1),
    ("S", 2, 3, 0), ("S", 3, 3, 1), ("R", 2, 5), ("S", 2, 3, 1), ("S", 2, 4, 0), ("C", 3, 0),
    ("S", 3, 4, 0), ("S", 2, 4, 1), ("S", 3, 4, 1), ("RT", 4), ("C", 3, 1), ("L", 5), ("R", 5, 1),
    ("SS", 5), ("ST", 6), ("R", 5, 2), ("ST", 7), ("L", 4), ("R", 4, 1), ("SS", 4), ("R", 4, 2),
    ("F", 3), ("S", 5, 2, 0), ("R", 4, 3), ("S", 5, 2, 1), ("R", 4, 4), ("F", 2), ("S", 4, 2, 0),
    ("R", 5, 5), ("S", 4, 2, 1), ("R", 5, 3), ("S", 5, 3, 0), ("S", 4, 3, 0), ("R", 5, 4),
    ("R", 4, 5), ("S", 4, 3, 1), ("S", 5, 3, 1), ("RT", 6), ("RT", 7), ("S", 4, 4, 0),
    ("S", 5, 4, 0), ("L", 6), ("S", 4, 4, 1), ("R", 6, 2), ("R", 6, 1), ("SS", 6), ("S", 5, 4, 1),
    ("L", 7), ("R", 7, 3), ("R", 7, 1), ("R", 7, 2), ("SS", 7), ("F", 4), ("S", 6, 2, 0),
    ("S", 6, 2, 1), ("F", 5), ("R", 6, 3), ("S", 7, 2, 0), ("R", 6, 5), ("S", 7, 2, 1),
    ("R", 6, 4), ("S", 6, 3, 0), ("R", 7, 4), ("S", 7, 3, 0), ("S", 7, 3, 1), ("S", 6, 3, 1),
    ("R", 7, 5), ("S", 7, 4, 0), ("S", 6, 4, 0), ("S", 6, 4, 1), ("S", 7, 4, 1), ("F", 6),
    ("F", 7),
)


def kernel(
    kv,
    query,
    grad,
    slot_t,
    source_t,
    out_o,
    out_q,
    out_k,
    out_v,
    table,
    relay_out,
    relay_in,
    merged_out,
    received,
    terms_in,
    terms_relay,
    sums_r,
    sums_l,
    near,
    anchor_acc,
    anchor_in,
    part_out,
    part_in,
    edge_out,
    edge_in,
    edge_part_out,
    edge_part_in,
    anchor_kv,
    wide,
    terms,
    ag_sent,
    ag_sem,
    rs_sent,
    rs_sem,
    x_sem,
    anchor_sem,
    part_sem,
    edge_sem,
):
    ctx = lax.axis_index("ctx")
    x, z = ctx // NZ, ctx % NZ
    z_r = x * NZ + lax.rem(z + 1, NZ)
    z_l = x * NZ + lax.rem(z + NZ - 1, NZ)
    p_r = lax.rem(x + 1, NX)
    p_l = lax.rem(x + NX - 1, NX)
    p_o = lax.rem(x + 2, NX)
    x_r = p_r * NZ + z
    x_l = p_l * NZ + z
    outer = (x == 0) | (x == NX - 1)
    inner = (x == 1) | (x == NX - 2)
    rim = (z == 0) | (z == NZ - 1)
    beyond = lax.rem(jnp.where(z == 0, ctx + NX * NZ - 1, ctx + 1), NX * NZ)

    def to(device, src, dst, sent, came=None):
        return pltpu.make_async_remote_copy(
            src_ref=src,
            dst_ref=dst,
            send_sem=sent if came is not None else sent.at[0],
            recv_sem=came if came is not None else sent.at[1],
            device_id={"ctx": device},
            device_id_type=MESH,
        )

    barrier = pltpu.get_barrier_semaphore()

    def place_own(u):
        @pl.loop(0, BPD)
        def _(b):
            table[u][z * BPD + b] = kv[u, b]

    def greet(device):
        pl.semaphore_signal(barrier, inc=1, device_id={"ctx": device}, device_id_type=MESH)

    for device in (z_r, z_l, x_r, x_l):
        greet(device)

    for u in range(UNITS):
        place_own(u)

    @pl.when(rim)
    def _():
        @pl.loop(0, UNITS)
        def _(u):
            edge_out[u] = kv[u, jnp.where(z == 0, 0, BPD - 1)]

    pl.semaphore_wait(barrier, 4)

    def gather_copy(u, s, half, right):
        row = lax.rem(z + NZ - (s - 1), NZ) if right else lax.rem(z + s - 1, NZ)
        cut = pl.ds(row * BPD + half * HALF, HALF)
        src = kv.at[u, pl.ds(half * HALF, HALF)] if s == 1 else table[u].at[cut]
        way = 0 if right else 1
        came = ag_sem.at[u % 2, s - 1, half, way]
        return to(z_r if right else z_l, src, table[u].at[cut], ag_sent.at[u], came)

    def moves(s):
        return [
            (half, right)
            for half in (0, 1)
            for right in (True, False)
            if s < 4 or right == (half == 0)
        ]

    def gather_start(u):
        for half, right in moves(1):
            gather_copy(u, 1, half, right).start()

    def gather_step(u, s, half):
        for right in (True, False):
            gather_copy(u, s - 1, half, right).wait_recv()
            if (half, right) in moves(s):
                gather_copy(u, s, half, right).start()

    def gather_end(u):
        for half, right in moves(4):
            gather_copy(u, 4, half, right).wait_recv()

    def all_sent(u, sent):
        whole = table[u].at[pl.ds(0, 14 * HALF)]
        to(z_r, whole, whole, sent.at[u], ag_sem.at[0, 0, 0, 0]).wait_send()

    def gather_sent(u):
        all_sent(u, ag_sent)

    def edge_copy():
        return to(beyond, edge_out, edge_in, edge_sem.at[UNITS])

    def send_edges():
        @pl.when(rim)
        def _():
            edge_copy().start()

    def relay_copy(u, side):
        return to(
            (x_r, x_l)[side], relay_out[u].at[side], relay_in[u].at[1 - side], x_sem.at[0, u, side]
        )

    def merged_copy(u, side):
        return to(
            (x_r, x_l)[side],
            merged_out[u].at[side],
            received[u].at[pl.ds((FROM_L, FROM_R)[side], MAIN)],
            x_sem.at[1, u, side],
        )

    def anchor_copy(u, side):
        return to(
            (x_r, x_l)[side],
            table[u].at[jnp.where(x == 0, 0, TARGETS - 1)],
            anchor_in.at[u, 0],
            anchor_sem.at[u, side],
        )

    def anchor_arrived(u):
        @pl.when((x == 0) | (x == 1))
        def _():
            anchor_copy(u, 0).wait_recv()

        @pl.when((x == 2) | (x == 3))
        def _():
            anchor_copy(u, 1).wait_recv()

    def anchor_pass(u):
        return to(
            jnp.where(x == 1, x_r, x_l), anchor_in.at[u, 0], anchor_in.at[u, 1], anchor_sem.at[u, 2]
        )

    def send_relays(u):
        h = u // 2

        @pl.when(outer)
        def _():
            for side in (0, 1):
                anchor_copy(u, side).start()

        @pl.loop(0, RELAY)
        def _(k):
            relay_out[u][0, k] = table[u][slot_t[h, p_o, T_RELAY + RELAY + k]]
            relay_out[u][1, k] = table[u][slot_t[h, p_o, T_RELAY + k]]

        for side in (0, 1):
            relay_copy(u, side).start()

        @pl.loop(0, MAIN)
        def _(k):
            received[u][OWN + k] = table[u][slot_t[h, x, OWN + k]]

    def send_merged(u):
        h = u // 2
        for side in (0, 1):
            relay_copy(u, side).wait_recv()

        @pl.loop(0, MAIN)
        def _(k):
            for side, plane, first, back in ((0, p_r, FROM_L, 1), (1, p_l, FROM_R, 0)):
                code = slot_t[h, plane, first + k]
                direct = table[u][jnp.minimum(code, TARGETS - 1)]
                passed = relay_in[u][back, jnp.maximum(code - TARGETS, 0)]
                merged_out[u][side, k] = jnp.where(code < TARGETS, direct, passed)

        for side in (0, 1):
            merged_copy(u, side).start()
        anchor_arrived(u)

        @pl.when(inner)
        def _():
            anchor_pass(u).start()

        if u == 0:
            send_edges()

    def lay_keys(h):
        for p in (0, 1):
            u = 2 * h + p
            for side in (0, 1):
                merged_copy(u, side).wait_recv()

            @pl.when(inner)
            def _():
                anchor_pass(u).wait_recv()

            row_above = lax.rem(z + NZ - 1, NZ) * BPD + BPD - 1
            row_below = lax.rem(z + 1, NZ) * BPD
            wide[p, 0:BLOCK] = jnp.where(z > 0, table[u][row_above], edge_in[u])
            wide[p, BLOCK * (BPD + 1) :] = jnp.where(z < NZ - 1, table[u][row_below], edge_in[u])
            for b in range(BPD):
                wide[p, BLOCK * (b + 1) : BLOCK * (b + 2)] = kv[u, b]
            came, passed = anchor_in[u, 0], anchor_in[u, 1]
            anchor_kv[p, :BLOCK] = jnp.where(x == 0, table[u][0], jnp.where(x == 2, passed, came))
            anchor_kv[p, BLOCK:] = jnp.where(
                x == 3, table[u][TARGETS - 1], jnp.where(x == 1, passed, came)
            )
        near[h][...] = jnp.zeros_like(near[h])
        anchor_acc[h][...] = jnp.zeros_like(anchor_acc[h])

    def compute(h, piece):
        if piece == 0:
            if h == 0:

                @pl.when(rim)
                def _():
                    edge_copy().wait_recv()

            lay_keys(h)
        column = lax.broadcasted_iota(jnp.int32, (1, 8 * BLOCK), 1)

        @pl.loop(piece * BPD // PIECES, (piece + 1) * BPD // PIECES)
        def _(i):
            rows = pl.ds(pl.multiple_of(i * BLOCK, BLOCK), 3 * BLOCK)
            spots = [slot_t[h, x, T_PLACE + i * R + r] for r in range(R)]
            keys, values = (
                jnp.concatenate(
                    [wide[p, rows], anchor_kv[p]] + [received[2 * h + p][s] for s in spots], axis=0
                )
                for p in (0, 1)
            )
            q, g = query[h, i], grad[h, i]
            block = ctx * BPD + i
            low = jnp.where(block == 0, BLOCK, 0)
            cut = jnp.where(block == NX * NZ * BPD - 1, 2 * BLOCK, 3 * BLOCK)
            masked = (column < low) | ((column >= cut) & (column < 3 * BLOCK))
            contract_last = (((1,), (1,)), ((), ()))
            contract_first = (((0,), (0,)), ((), ()))
            scores = lax.dot_general(q, keys, contract_last, preferred_element_type=F32) * SCALE
            scores = jnp.where(masked, -1e30, scores)
            powers = jnp.exp(scores - jnp.max(scores, axis=-1, keepdims=True))
            probs = powers * (1.0 / jnp.sum(powers, axis=-1, keepdims=True))
            low_probs = probs.astype(BF16)
            attended = jnp.dot(low_probs, values, preferred_element_type=F32).astype(BF16)
            out_o[h, i] = attended
            delta = jnp.sum(g.astype(F32) * attended.astype(F32), axis=-1, keepdims=True)
            grad_probs = lax.dot_general(g, values, contract_last, preferred_element_type=F32)
            grad_scores = (probs * (grad_probs - delta)).astype(BF16)
            out_q[h, i] = (
                jnp.dot(grad_scores, keys, preferred_element_type=F32) * SCALE
            ).astype(BF16)
            key_part = (
                lax.dot_general(grad_scores, q, contract_first, preferred_element_type=F32) * SCALE
            )
            value_part = lax.dot_general(
                low_probs, g, contract_first, preferred_element_type=F32
            )
            for p, part in ((0, key_part), (1, value_part)):
                near[h][p, rows] += part[: 3 * BLOCK]
                anchor_acc[h][p] += part[3 * BLOCK : 5 * BLOCK]
                for r in range(R):
                    terms[p, i * R + r] = part[(5 + r) * BLOCK : (6 + r) * BLOCK].astype(BF16)

    def terms_copy(u, side):
        return to(
            (x_r, x_l)[side],
            merged_out[u].at[side],
            terms_in[u].at[pl.ds((FROM_L, FROM_R)[side], MAIN)],
            x_sem.at[2, u, side],
        )

    def terms_relay_copy(u, side):
        return to(
            (x_r, x_l)[side], relay_out[u].at[side], terms_relay[u].at[1 - side],
            x_sem.at[3, u, side],
        )

    def part_first(u):
        return to(
            jnp.where(x == 1, x_r, x_l), part_out.at[u, 0], part_in.at[u, 0], part_sem.at[u, 0]
        )

    def part_second(u, side):
        return to(
            (x_r, x_l)[side], part_out.at[u, 1], part_in.at[u, 1 + side], part_sem.at[u, 1 + side]
        )

    def leftward():
        return (x == 0) | (x == 1)

    def edge_part_copy(u):
        return to(beyond, edge_part_out.at[u], edge_part_in.at[u], edge_sem.at[u])

    def anchor(u, which):
        return anchor_acc[u // 2][u % 2, which * BLOCK : (which + 1) * BLOCK]

    def near_rows(u, b):
        return near[u // 2][u % 2, (b + 1) * BLOCK : (b + 2) * BLOCK]

    def send_terms(u):
        h, p = u // 2, u % 2
        for side in (0, 1):
            merged_copy(u, side).wait_send()

        @pl.loop(0, MAIN)
        def _(k):
            merged_out[u][0, k] = terms[p, slot_t[h, x, T_GIVER + FROM_R + k]]
            merged_out[u][1, k] = terms[p, slot_t[h, x, T_GIVER + FROM_L + k]]
            terms_in[u][B_OWN + k] = terms[p, slot_t[h, x, T_GIVER + OWN + k]]

        for side in (0, 1):
            terms_copy(u, side).start()
        terms_in[u][B_ZERO] = jnp.zeros((BLOCK, HD), BF16)

        @pl.when(inner)
        def _():
            part_out[u, 0] = jnp.where(x == 1, anchor(u, 1), anchor(u, 0)).astype(BF16)
            part_first(u).start()

        @pl.when(rim)
        def _():
            edge_part_out[u] = jnp.where(z == 0, near_rows(u, -1), near_rows(u, BPD)).astype(BF16)
            edge_part_copy(u).start()

    def relay_terms(u):
        h = u // 2
        for side in (0, 1):
            relay_copy(u, side).wait_send()
            terms_copy(u, side).wait_recv()

        @pl.loop(0, RELAY)
        def _(k):
            from_left = slot_t[h, p_l, T_RIGHT] + k
            from_right = slot_t[h, p_r, T_LEFT] + k
            relay_out[u][0, k] = terms_in[u][FROM_L + jnp.minimum(from_left, MAIN - 1)]
            relay_out[u][1, k] = terms_in[u][FROM_R + jnp.minimum(from_right, MAIN - 1)]

        for side in (0, 1):
            terms_relay_copy(u, side).start()

        @pl.when(inner)
        def _():
            part_first(u).wait_recv()
            mine = jnp.where(x == 1, anchor(u, 0), anchor(u, 1))
            part_out[u, 1] = (mine + part_in[u, 0].astype(F32)).astype(BF16)

        @pl.when(outer)
        def _():
            part_out[u, 1] = jnp.where(x == 0, anchor(u, 1), anchor(u, 0)).astype(BF16)

        @pl.when(leftward())
        def _():
            part_second(u, 1).start()

        @pl.when(jnp.logical_not(leftward()))
        def _():
            part_second(u, 0).start()

    def land(u):
        gather_sent(u)

        @pl.when(outer)
        def _():
            for side in (0, 1):
                anchor_copy(u, side).wait_send()
                part_second(u, side).wait_recv()

        for side in (0, 1):
            terms_relay_copy(u, side).wait_recv()

        @pl.loop(0, RELAY)
        def _(k):
            terms_in[u][B_RR + k] = terms_relay[u][0, k]
            terms_in[u][B_RL + k] = terms_relay[u][1, k]

    def rows(u, group):
        h = u // 2
        for away in {1: (4,), 2: (3, 5), 3: (2, 6), 4: (1, 7), 5: (0,)}[group]:
            row = lax.rem(z + away, NZ)

            @pl.loop(0, BPD)
            def _(b):
                t = row * BPD + b
                total = terms_in[u][source_t[h, t * DEEP]].astype(F32)
                for k in range(1, DEEP):
                    total += terms_in[u][source_t[h, t * DEEP + k]].astype(F32)
                table[u][t] = total.astype(BF16)

            def add(t, part):
                table[u][t] = (table[u][t].astype(F32) + part).astype(BF16)

            def both():
                return part_in[u, 1].astype(F32) + part_in[u, 2].astype(F32)

            @pl.when((x == 0) & (row == 0))
            def _():
                add(0, anchor(u, 0) + both())

            @pl.when((x == NX - 1) & (row == NZ - 1))
            def _():
                add(TARGETS - 1, anchor(u, 1) + both())

            if away == NZ - 1:

                @pl.when(z > 0)
                def _():
                    add(row * BPD + BPD - 1, near_rows(u, -1))

            if away == 1:

                @pl.when(z < NZ - 1)
                def _():
                    add(row * BPD, near_rows(u, BPD))

    def sum_copy(u, s, half, right):
        row = lax.rem(z + 5 - s, NZ) if right else lax.rem(z + NZ - 5 + s, NZ)
        way = 0 if right else 1
        return to(
            z_r if right else z_l,
            table[u].at[pl.ds(row * BPD + half * HALF, HALF)],
            (sums_r if right else sums_l)[u].at[s - 1, pl.ds(half * HALF, HALF)],
            rs_sent.at[u],
            rs_sem.at[u % 2, s - 1, half, way],
        )

    def sum_moves(s):
        return moves(4 if s == 1 else 1)

    def sum_start(u):
        for half, right in sum_moves(1):
            sum_copy(u, 1, half, right).start()

    def sum_step(u, s, half):
        for right in (True, False):
            if (half, right) in sum_moves(s - 1):
                sum_copy(u, s - 1, half, right).wait_recv()
                row = lax.rem(z + 5 - s, NZ) if right else lax.rem(z + NZ - 5 + s, NZ)
                came = (sums_r if right else sums_l)[u]

                @pl.loop(0, HALF)
                def _(b):
                    here = row * BPD + half * HALF + b
                    table[u][here] = (
                        table[u][here].astype(F32) + came[s - 2, half * HALF + b].astype(F32)
                    ).astype(BF16)

            sum_copy(u, s, half, right).start()

    def finish(u):
        h, p = u // 2, u % 2
        for half, right in sum_moves(4):
            sum_copy(u, 4, half, right).wait_recv()

        @pl.when(rim)
        def _():
            edge_part_copy(u).wait_recv()
            lone = pl.ds(pl.multiple_of(jnp.where(z == 0, 1, BPD) * BLOCK, BLOCK), BLOCK)
            near[h][p, lone] += edge_part_in[u].astype(F32)

        @pl.loop(0, BPD)
        def _(b):
            total = (
                table[u][z * BPD + b].astype(F32)
                + sums_r[u][3, b].astype(F32)
                + sums_l[u][3, b].astype(F32)
                + near[h][p, pl.ds(pl.multiple_of((b + 1) * BLOCK, BLOCK), BLOCK)]
            )
            (out_k, out_v)[p][h, b] = total.astype(BF16)

    def drain(u):
        all_sent(u, rs_sent)
        for side in (0, 1):
            terms_copy(u, side).wait_send()
            terms_relay_copy(u, side).wait_send()

        @pl.when(inner)
        def _():
            anchor_pass(u).wait_send()
            part_first(u).wait_send()

        @pl.when(leftward())
        def _():
            part_second(u, 1).wait_send()

        @pl.when(jnp.logical_not(leftward()))
        def _():
            part_second(u, 0).wait_send()

        @pl.when(rim)
        def _():
            edge_part_copy(u).wait_send()

    steps = {
        "GS": gather_start,
        "G": gather_step,
        "GE": gather_end,
        "SR": send_relays,
        "SM": send_merged,
        "C": compute,
        "ST": send_terms,
        "RT": relay_terms,
        "L": land,
        "R": rows,
        "SS": sum_start,
        "S": sum_step,
        "F": finish,
    }
    for name, *where in ORDER:
        steps[name](*where)
    for u in range(UNITS):
        drain(u)

    @pl.when(rim)
    def _():
        edge_copy().wait_send()


def local(query, key, value, out_grad, random_links):
    def head_major(array):
        return array.reshape(BPD, BLOCK, H, HD).transpose(2, 0, 1, 3)

    def seq_major(array):
        return array.transpose(1, 2, 0, 3).reshape(BPD * BLOCK, H, HD)

    tables = slot_tables(random_links)
    kv = jnp.stack((head_major(key), head_major(value)), axis=1).reshape(UNITS, BPD, BLOCK, HD)
    block = (BLOCK, HD)

    def per(count, *shape, dtype=BF16):
        return [pltpu.VMEM(shape, dtype) for _ in range(count)]

    dma = pltpu.SemaphoreType.DMA
    vmem = pl.BlockSpec(memory_space=pltpu.VMEM)
    smem = pl.BlockSpec(memory_space=pltpu.SMEM)
    outs = pl.pallas_call(
        kernel,
        out_shape=[jax.ShapeDtypeStruct((H, BPD, BLOCK, HD), BF16)] * 4,
        in_specs=[vmem] * 3 + [smem] * len(tables),
        out_specs=[vmem] * 4,
        scratch_shapes=[
            per(UNITS, TARGETS, *block),
            per(UNITS, 2, RELAY, *block),
            per(UNITS, 2, RELAY, *block),
            per(UNITS, 2, MAIN, *block),
            per(UNITS, RECEIVED, *block),
            per(UNITS, B_SIZE, *block),
            per(UNITS, 2, RELAY, *block),
            per(UNITS, 4, BPD, *block),
            per(UNITS, 4, BPD, *block),
            per(H, 2, (BPD + 2) * BLOCK, HD, dtype=F32),
            per(H, 2, 2 * BLOCK, HD, dtype=F32),
            pltpu.VMEM((UNITS, 2, *block), BF16),
            pltpu.VMEM((UNITS, 2, *block), BF16),
            pltpu.VMEM((UNITS, 3, *block), BF16),
            pltpu.VMEM((UNITS, *block), BF16),
            pltpu.VMEM((UNITS, *block), BF16),
            pltpu.VMEM((UNITS, *block), BF16),
            pltpu.VMEM((UNITS, *block), BF16),
            pltpu.VMEM((2, 2 * BLOCK, HD), BF16),
            pltpu.VMEM((2, (BPD + 2) * BLOCK, HD), BF16),
            pltpu.VMEM((2, REFS, *block), BF16),
            dma((UNITS,)),
            dma((2, 4, 2, 2)),
            dma((UNITS,)),
            dma((2, 4, 2, 2)),
            dma((4, UNITS, 2, 2)),
            dma((UNITS, 3, 2)),
            dma((UNITS, 3, 2)),
            dma((UNITS + 1, 2)),
        ],
        compiler_params=pltpu.CompilerParams(
            collective_id=0, has_side_effects=True, vmem_limit_bytes=60 * 2**20
        ),
        cost_estimate=pl.CostEstimate(
            flops=2 * 6 * BLOCK * 8 * BLOCK * HD * H * BPD,
            bytes_accessed=4 * 2**20,
            transcendentals=H * BPD * BLOCK * 8 * BLOCK,
        ),
    )(kv, head_major(query), head_major(out_grad), *tables)
    return tuple(seq_major(array) for array in outs)


def solution(mesh):
    split = P("ctx", "head", None)
    return jax.shard_map(
        local,
        mesh=mesh,
        in_specs=(split, split, split, split, P(None, "head", None)),
        out_specs=(split, split, split, split),
        check_vma=False,
    )
```

```python
import math

import jax
import jax.numpy as jnp
from jax import lax
from jax.experimental import pallas as pl
from jax.experimental.pallas import tpu as pltpu
from jax.sharding import PartitionSpec as P

BLOCK = 64
HD = 128
NX = 4
NZ = 8
BPD = 8
HALF = BPD // 2
H = 4
R = 3
REFS = BPD * R
TARGETS = NZ * BPD
MAIN = 16
RELAY = 8
UNITS = 2 * H
FROM_R, FROM_L, OWN = 0, MAIN, 2 * MAIN
RECEIVED = OWN + MAIN
B_RR = 2 * MAIN
B_RL = B_RR + RELAY
B_OWN = B_RL + RELAY
B_ZERO = B_OWN + MAIN
B_SIZE = B_ZERO + 1
T_RELAY = RECEIVED
T_GIVER = T_RELAY + 2 * RELAY
T_PLACE = T_GIVER + RECEIVED
T_RIGHT = T_PLACE + REFS
T_LEFT = T_RIGHT + 1
T_WIDTH = 256
PIECES = 2
DEEP = 8
F32 = jnp.float32
BF16 = jnp.bfloat16
MESH = pl.DeviceIdType.MESH
SCALE = 1.0 / math.sqrt(HD)


def named_blocks(links):
    z = lax.axis_index("ctx") % NZ
    row = lax.dynamic_slice_in_dim(links.reshape(NX, NZ, BPD, H, R), z, 1, 1)[:, 0]
    return row.transpose(0, 2, 1, 3).reshape(NX * H, REFS)


def slot_tables(named, x):
    plane = lax.broadcasted_iota(jnp.int32, named.shape, 0) // H
    lane = lax.broadcasted_iota(jnp.int32, named.shape, 1)
    away = ((named >> 6) - plane) & (NX - 1)
    target = named & (TARGETS - 1)

    def entry(array, e):
        return array[:, e : e + 1]

    rank = jnp.zeros_like(named)
    n_r, n_o, n_l = (jnp.zeros((NX * H, 1), jnp.int32) for _ in range(3))
    for e in range(REFS):
        way = entry(away, e)
        rank += jnp.where((away == way) & (lane > e), 1, 0)
        n_r += jnp.where(way == 1, 1, 0)
        n_o += jnp.where(way == 2, 1, 0)
        n_l += jnp.where(way == 3, 1, 0)
    by_right = jnp.minimum(n_o, jnp.minimum(RELAY, MAIN - n_r))
    right_way = rank < by_right
    relay_rank = jnp.where(right_way, rank, rank - by_right)
    opposite = jnp.where(right_way, FROM_R + n_r + rank, FROM_L + n_l + relay_rank)
    place = jnp.where(
        away == 0,
        OWN + rank,
        jnp.where(away == 1, FROM_R + rank, jnp.where(away == 3, FROM_L + rank, opposite)),
    )
    code = jnp.where(away == 2, TARGETS + relay_rank, target)
    relay_place = jnp.where(
        away == 2, T_RELAY + relay_rank + jnp.where(right_way, 0, RELAY), -1
    )
    spots = lax.broadcasted_iota(jnp.int32, (NX * H, T_WIDTH), 1)
    first = jnp.where(spots == T_RIGHT, n_r, jnp.where(spots == T_LEFT, n_l, 0))
    for e in range(REFS):
        here = entry(place, e)
        at = jnp.where(
            spots < T_RELAY,
            here,
            jnp.where(
                spots < T_GIVER,
                entry(relay_place, e),
                jnp.where(spots < T_PLACE, T_GIVER + here, T_PLACE + e),
            ),
        )
        put = jnp.where(
            spots < T_RELAY,
            entry(code, e),
            jnp.where(
                spots < T_GIVER, entry(target, e), jnp.where(spots < T_PLACE, e, here)
            ),
        )
        first += jnp.where(at == spots, put, 0)
    most = jnp.where(
        spots < T_RELAY,
        TARGETS + RELAY - 1,
        jnp.where(
            spots < T_GIVER,
            TARGETS - 1,
            jnp.where(spots < T_PLACE, REFS - 1, jnp.where(spots < T_RIGHT, RECEIVED - 1, REFS)),
        ),
    )
    first = jnp.clip(first, 0, most)
    landing = jnp.where(
        away == 0,
        B_OWN + rank,
        jnp.where(
            away == 1,
            FROM_L + rank,
            jnp.where(
                away == 3, FROM_R + rank, jnp.where(right_way, B_RL, B_RR) + relay_rank
            ),
        ),
    )
    mine = jnp.where((named >> 6) == x, target, -1)
    cells = lax.broadcasted_iota(jnp.int32, (H, TARGETS * DEEP), 1)
    sources = jnp.full((H, TARGETS * DEEP), B_ZERO, jnp.int32)
    parts = [slice(a * H, (a + 1) * H) for a in range(NX)]
    for a in range(NX):
        aim = mine[parts[a]]
        depth = jnp.zeros_like(aim)
        for b in range(a + 1):
            for e in range(REFS):
                same = aim == entry(mine[parts[b]], e)
                if b == a:
                    same = same & (lane[:H] > e)
                depth += jnp.where(same, 1, 0)
        cell = jnp.where(aim >= 0, aim * DEEP + depth, -1)
        land = landing[parts[a]]
        for e in range(REFS):
            sources += jnp.where(entry(cell, e) == cells, entry(land, e) - B_ZERO, 0)
    return first, jnp.clip(sources, 0, B_SIZE - 1)


ORDER = (
    ("GS", 0), ("G", 0, 2, 0), ("G", 0, 2, 1), ("G", 0, 3, 0), ("G", 0, 3, 1), ("GS", 1),
    ("G", 0, 4, 0), ("G", 0, 4, 1), ("G", 1, 2, 0), ("G", 1, 2, 1), ("GE", 0), ("SR", 0),
    ("G", 1, 3, 0), ("G", 1, 3, 1), ("GS", 2), ("SM", 0), ("G", 1, 4, 0), ("G", 1, 4, 1),
    ("G", 2, 2, 0), ("GE", 1), ("G", 2, 2, 1), ("SR", 1), ("G", 2, 3, 0), ("G", 2, 3, 1),
    ("GS", 3), ("G", 2, 4, 0), ("SM", 1), ("G", 2, 4, 1), ("G", 3, 2, 0), ("GE", 2),
    ("G", 3, 2, 1), ("SR", 2), ("G", 3, 3, 0), ("C", 0, 0), ("SM", 2), ("G", 3, 3, 1), ("GS", 4),
    ("C", 0, 1), ("G", 3, 4, 0), ("G", 3, 4, 1), ("ST", 0), ("G", 4, 2, 0), ("G", 4, 2, 1),
    ("ST", 1), ("G", 4, 3, 0), ("GE", 3), ("G", 4, 3, 1), ("GS", 5), ("SR", 3), ("G", 4, 4, 0),
    ("RT", 0), ("G", 4, 4, 1), ("G", 5, 2, 0), ("G", 5, 2, 1), ("G", 5, 3, 0), ("GE", 4),
    ("G", 5, 3, 1), ("GS", 6), ("RT", 1), ("G", 5, 4, 0), ("SM", 3), ("G", 5, 4, 1),
    ("G", 6, 2, 0), ("SR", 4), ("L", 0), ("G", 6, 2, 1), ("R", 0, 2), ("GE", 5), ("SR", 5),
    ("R", 0, 3), ("G", 6, 3, 0), ("R", 0, 1), ("SM", 4), ("L", 1), ("R", 1, 2), ("R", 1, 1),
    ("G", 6, 3, 1), ("SS", 0), ("GS", 7), ("C", 1, 0), ("SM", 5), ("G", 6, 4, 0), ("G", 7, 2, 0),
    ("C", 1, 1), ("SS", 1), ("S", 0, 2, 0), ("ST", 2), ("R", 1, 5), ("G", 6, 4, 1), ("R", 1, 3),
    ("R", 0, 4), ("S", 1, 2, 0), ("ST", 3), ("C", 2, 0), ("G", 7, 2, 1), ("S", 0, 2, 1), ("RT", 2),
    ("GE", 6), ("S", 1, 2, 1), ("G", 7, 3, 0), ("C", 2, 1), ("S", 0, 3, 0), ("R", 1, 4),
    ("G", 7, 3, 1), ("RT", 3), ("ST", 5), ("L", 2), ("S", 1, 3, 0), ("R", 2, 2), ("S", 1, 3, 1),
    ("G", 7, 4, 0), ("L", 3), ("G", 7, 4, 1), ("S", 1, 4, 0), ("R", 3, 1), ("S", 1, 4, 1),
    ("R", 3, 5), ("S", 0, 3, 1), ("SS", 3), ("SR", 6), ("S", 0, 4, 0), ("R", 3, 3), ("R", 2, 1),
    ("R", 3, 2), ("GE", 7), ("R", 2, 3), ("SR", 7), ("S", 0, 4, 1), ("F", 1), ("SM", 6),
    ("S", 3, 2, 0), ("R", 2, 4), ("SS", 2), ("R", 3, 4), ("S", 3, 2, 1), ("R", 0, 5),
    ("S", 3, 3, 0), ("SM", 7), ("ST", 4), ("F", 0), ("S", 2, 2, 0), ("RT", 5), ("S", 2, 2, 1),
    ("S", 2, 3, 0), ("S", 3, 3, 1), ("R", 2, 5), ("S", 2, 3, 1), ("S", 2, 4, 0), ("C", 3, 0),
    ("S", 3, 4, 0), ("S", 2, 4, 1), ("S", 3, 4, 1), ("RT", 4), ("C", 3, 1), ("L", 5), ("R", 5, 1),
    ("SS", 5), ("ST", 6), ("R", 5, 2), ("ST", 7), ("L", 4), ("R", 4, 1), ("SS", 4), ("R", 4, 2),
    ("F", 3), ("S", 5, 2, 0), ("R", 4, 3), ("S", 5, 2, 1), ("R", 4, 4), ("F", 2), ("S", 4, 2, 0),
    ("R", 5, 5), ("S", 4, 2, 1), ("R", 5, 3), ("S", 5, 3, 0), ("S", 4, 3, 0), ("R", 5, 4),
    ("R", 4, 5), ("S", 4, 3, 1), ("S", 5, 3, 1), ("RT", 6), ("RT", 7), ("S", 4, 4, 0),
    ("S", 5, 4, 0), ("L", 6), ("S", 4, 4, 1), ("R", 6, 2), ("R", 6, 1), ("SS", 6), ("S", 5, 4, 1),
    ("L", 7), ("R", 7, 3), ("R", 7, 1), ("R", 7, 2), ("SS", 7), ("F", 4), ("S", 6, 2, 0),
    ("S", 6, 2, 1), ("F", 5), ("R", 6, 3), ("S", 7, 2, 0), ("R", 6, 5), ("S", 7, 2, 1),
    ("R", 6, 4), ("S", 6, 3, 0), ("R", 7, 4), ("S", 7, 3, 0), ("S", 7, 3, 1), ("S", 6, 3, 1),
    ("R", 7, 5), ("S", 7, 4, 0), ("S", 6, 4, 0), ("S", 6, 4, 1), ("S", 7, 4, 1), ("F", 6),
    ("F", 7),
)


def kernel(
    kv,
    query,
    grad,
    links,
    out_o,
    out_q,
    out_k,
    out_v,
    table,
    relay_out,
    relay_in,
    merged_out,
    received,
    terms_in,
    terms_relay,
    sums_r,
    sums_l,
    near,
    anchor_acc,
    anchor_in,
    part_out,
    part_in,
    edge_out,
    edge_in,
    edge_part_out,
    edge_part_in,
    anchor_kv,
    wide,
    terms,
    ag_sent,
    ag_sem,
    rs_sent,
    rs_sem,
    x_sem,
    anchor_sem,
    part_sem,
    edge_sem,
    slot_v,
    source_v,
    slot_t,
    source_t,
    table_sem,
):
    ctx = lax.axis_index("ctx")
    x, z = ctx // NZ, ctx % NZ
    z_r = x * NZ + lax.rem(z + 1, NZ)
    z_l = x * NZ + lax.rem(z + NZ - 1, NZ)
    p_r = lax.rem(x + 1, NX)
    p_l = lax.rem(x + NX - 1, NX)
    p_o = lax.rem(x + 2, NX)
    x_r = p_r * NZ + z
    x_l = p_l * NZ + z
    outer = (x == 0) | (x == NX - 1)
    inner = (x == 1) | (x == NX - 2)
    rim = (z == 0) | (z == NZ - 1)
    beyond = lax.rem(jnp.where(z == 0, ctx + NX * NZ - 1, ctx + 1), NX * NZ)

    def to(device, src, dst, sent, came=None):
        return pltpu.make_async_remote_copy(
            src_ref=src,
            dst_ref=dst,
            send_sem=sent if came is not None else sent.at[0],
            recv_sem=came if came is not None else sent.at[1],
            device_id={"ctx": device},
            device_id_type=MESH,
        )

    barrier = pltpu.get_barrier_semaphore()

    def place_own(u):
        @pl.loop(0, BPD)
        def _(b):
            table[u][z * BPD + b] = kv[u, b]

    def greet(device):
        pl.semaphore_signal(barrier, inc=1, device_id={"ctx": device}, device_id_type=MESH)

    for device in (z_r, z_l, x_r, x_l):
        greet(device)

    slot_v[...], source_v[...] = slot_tables(links[...], x)
    copies = (
        pltpu.make_async_copy(slot_v, slot_t, table_sem.at[0]),
        pltpu.make_async_copy(source_v, source_t, table_sem.at[1]),
    )
    for copy in copies:
        copy.start()
    for u in range(UNITS):
        place_own(u)

    @pl.when(rim)
    def _():
        @pl.loop(0, UNITS)
        def _(u):
            edge_out[u] = kv[u, jnp.where(z == 0, 0, BPD - 1)]

    for copy in copies:
        copy.wait()
    pl.semaphore_wait(barrier, 4)

    def gather_copy(u, s, half, right):
        row = lax.rem(z + NZ - (s - 1), NZ) if right else lax.rem(z + s - 1, NZ)
        cut = pl.ds(row * BPD + half * HALF, HALF)
        src = kv.at[u, pl.ds(half * HALF, HALF)] if s == 1 else table[u].at[cut]
        way = 0 if right else 1
        came = ag_sem.at[u % 2, s - 1, half, way]
        return to(z_r if right else z_l, src, table[u].at[cut], ag_sent.at[u], came)

    def moves(s):
        return [
            (half, right)
            for half in (0, 1)
            for right in (True, False)
            if s < 4 or right == (half == 0)
        ]

    def gather_start(u):
        for half, right in moves(1):
            gather_copy(u, 1, half, right).start()

    def gather_step(u, s, half):
        for right in (True, False):
            gather_copy(u, s - 1, half, right).wait_recv()
            if (half, right) in moves(s):
                gather_copy(u, s, half, right).start()

    def gather_end(u):
        for half, right in moves(4):
            gather_copy(u, 4, half, right).wait_recv()

    def all_sent(u, sent):
        whole = table[u].at[pl.ds(0, 14 * HALF)]
        to(z_r, whole, whole, sent.at[u], ag_sem.at[0, 0, 0, 0]).wait_send()

    def gather_sent(u):
        all_sent(u, ag_sent)

    def edge_copy():
        return to(beyond, edge_out, edge_in, edge_sem.at[UNITS])

    def send_edges():
        @pl.when(rim)
        def _():
            edge_copy().start()

    def relay_copy(u, side):
        return to(
            (x_r, x_l)[side], relay_out[u].at[side], relay_in[u].at[1 - side], x_sem.at[0, u, side]
        )

    def merged_copy(u, side):
        return to(
            (x_r, x_l)[side],
            merged_out[u].at[side],
            received[u].at[pl.ds((FROM_L, FROM_R)[side], MAIN)],
            x_sem.at[1, u, side],
        )

    def anchor_copy(u, side):
        return to(
            (x_r, x_l)[side],
            table[u].at[jnp.where(x == 0, 0, TARGETS - 1)],
            anchor_in.at[u, 0],
            anchor_sem.at[u, side],
        )

    def anchor_arrived(u):
        @pl.when((x == 0) | (x == 1))
        def _():
            anchor_copy(u, 0).wait_recv()

        @pl.when((x == 2) | (x == 3))
        def _():
            anchor_copy(u, 1).wait_recv()

    def anchor_pass(u):
        return to(
            jnp.where(x == 1, x_r, x_l), anchor_in.at[u, 0], anchor_in.at[u, 1], anchor_sem.at[u, 2]
        )

    def send_relays(u):
        h = u // 2

        @pl.when(outer)
        def _():
            for side in (0, 1):
                anchor_copy(u, side).start()

        @pl.loop(0, RELAY)
        def _(k):
            relay_out[u][0, k] = table[u][slot_t[p_o * H + h, T_RELAY + RELAY + k]]
            relay_out[u][1, k] = table[u][slot_t[p_o * H + h, T_RELAY + k]]

        for side in (0, 1):
            relay_copy(u, side).start()

        @pl.loop(0, MAIN)
        def _(k):
            received[u][OWN + k] = table[u][slot_t[x * H + h, OWN + k]]

    def send_merged(u):
        h = u // 2
        for side in (0, 1):
            relay_copy(u, side).wait_recv()

        @pl.loop(0, MAIN)
        def _(k):
            for side, plane, first, back in ((0, p_r, FROM_L, 1), (1, p_l, FROM_R, 0)):
                code = slot_t[plane * H + h, first + k]
                direct = table[u][jnp.minimum(code, TARGETS - 1)]
                passed = relay_in[u][back, jnp.maximum(code - TARGETS, 0)]
                merged_out[u][side, k] = jnp.where(code < TARGETS, direct, passed)

        for side in (0, 1):
            merged_copy(u, side).start()
        anchor_arrived(u)

        @pl.when(inner)
        def _():
            anchor_pass(u).start()

        if u == 0:
            send_edges()

    def lay_keys(h):
        for p in (0, 1):
            u = 2 * h + p
            for side in (0, 1):
                merged_copy(u, side).wait_recv()

            @pl.when(inner)
            def _():
                anchor_pass(u).wait_recv()

            row_above = lax.rem(z + NZ - 1, NZ) * BPD + BPD - 1
            row_below = lax.rem(z + 1, NZ) * BPD
            wide[p, 0:BLOCK] = jnp.where(z > 0, table[u][row_above], edge_in[u])
            wide[p, BLOCK * (BPD + 1) :] = jnp.where(z < NZ - 1, table[u][row_below], edge_in[u])
            for b in range(BPD):
                wide[p, BLOCK * (b + 1) : BLOCK * (b + 2)] = kv[u, b]
            came, passed = anchor_in[u, 0], anchor_in[u, 1]
            anchor_kv[p, :BLOCK] = jnp.where(x == 0, table[u][0], jnp.where(x == 2, passed, came))
            anchor_kv[p, BLOCK:] = jnp.where(
                x == 3, table[u][TARGETS - 1], jnp.where(x == 1, passed, came)
            )
        near[h][...] = jnp.zeros_like(near[h])
        anchor_acc[h][...] = jnp.zeros_like(anchor_acc[h])

    def compute(h, piece):
        if piece == 0:
            if h == 0:

                @pl.when(rim)
                def _():
                    edge_copy().wait_recv()

            lay_keys(h)
        column = lax.broadcasted_iota(jnp.int32, (1, 8 * BLOCK), 1)

        @pl.loop(piece * BPD // PIECES, (piece + 1) * BPD // PIECES)
        def _(i):
            rows = pl.ds(pl.multiple_of(i * BLOCK, BLOCK), 3 * BLOCK)
            spots = [slot_t[x * H + h, T_PLACE + i * R + r] for r in range(R)]
            keys, values = (
                jnp.concatenate(
                    [wide[p, rows], anchor_kv[p]] + [received[2 * h + p][s] for s in spots], axis=0
                )
                for p in (0, 1)
            )
            q, g = query[h, i], grad[h, i]
            block = ctx * BPD + i
            low = jnp.where(block == 0, BLOCK, 0)
            cut = jnp.where(block == NX * NZ * BPD - 1, 2 * BLOCK, 3 * BLOCK)
            masked = (column < low) | ((column >= cut) & (column < 3 * BLOCK))
            contract_last = (((1,), (1,)), ((), ()))
            contract_first = (((0,), (0,)), ((), ()))
            scores = lax.dot_general(q, keys, contract_last, preferred_element_type=F32) * SCALE
            scores = jnp.where(masked, -1e30, scores)
            powers = jnp.exp(scores - jnp.max(scores, axis=-1, keepdims=True))
            probs = powers * (1.0 / jnp.sum(powers, axis=-1, keepdims=True))
            low_probs = probs.astype(BF16)
            attended = jnp.dot(low_probs, values, preferred_element_type=F32).astype(BF16)
            out_o[h, i] = attended
            delta = jnp.sum(g.astype(F32) * attended.astype(F32), axis=-1, keepdims=True)
            grad_probs = lax.dot_general(g, values, contract_last, preferred_element_type=F32)
            grad_scores = (probs * (grad_probs - delta)).astype(BF16)
            out_q[h, i] = (
                jnp.dot(grad_scores, keys, preferred_element_type=F32) * SCALE
            ).astype(BF16)
            key_part = (
                lax.dot_general(grad_scores, q, contract_first, preferred_element_type=F32) * SCALE
            )
            value_part = lax.dot_general(
                low_probs, g, contract_first, preferred_element_type=F32
            )
            for p, part in ((0, key_part), (1, value_part)):
                near[h][p, rows] += part[: 3 * BLOCK]
                anchor_acc[h][p] += part[3 * BLOCK : 5 * BLOCK]
                for r in range(R):
                    terms[p, i * R + r] = part[(5 + r) * BLOCK : (6 + r) * BLOCK].astype(BF16)

    def terms_copy(u, side):
        return to(
            (x_r, x_l)[side],
            merged_out[u].at[side],
            terms_in[u].at[pl.ds((FROM_L, FROM_R)[side], MAIN)],
            x_sem.at[2, u, side],
        )

    def terms_relay_copy(u, side):
        return to(
            (x_r, x_l)[side], relay_out[u].at[side], terms_relay[u].at[1 - side],
            x_sem.at[3, u, side],
        )

    def part_first(u):
        return to(
            jnp.where(x == 1, x_r, x_l), part_out.at[u, 0], part_in.at[u, 0], part_sem.at[u, 0]
        )

    def part_second(u, side):
        return to(
            (x_r, x_l)[side], part_out.at[u, 1], part_in.at[u, 1 + side], part_sem.at[u, 1 + side]
        )

    def leftward():
        return (x == 0) | (x == 1)

    def edge_part_copy(u):
        return to(beyond, edge_part_out.at[u], edge_part_in.at[u], edge_sem.at[u])

    def anchor(u, which):
        return anchor_acc[u // 2][u % 2, which * BLOCK : (which + 1) * BLOCK]

    def near_rows(u, b):
        return near[u // 2][u % 2, (b + 1) * BLOCK : (b + 2) * BLOCK]

    def send_terms(u):
        h, p = u // 2, u % 2
        for side in (0, 1):
            merged_copy(u, side).wait_send()

        @pl.loop(0, MAIN)
        def _(k):
            merged_out[u][0, k] = terms[p, slot_t[x * H + h, T_GIVER + FROM_R + k]]
            merged_out[u][1, k] = terms[p, slot_t[x * H + h, T_GIVER + FROM_L + k]]
            terms_in[u][B_OWN + k] = terms[p, slot_t[x * H + h, T_GIVER + OWN + k]]

        for side in (0, 1):
            terms_copy(u, side).start()
        terms_in[u][B_ZERO] = jnp.zeros((BLOCK, HD), BF16)

        @pl.when(inner)
        def _():
            part_out[u, 0] = jnp.where(x == 1, anchor(u, 1), anchor(u, 0)).astype(BF16)
            part_first(u).start()

        @pl.when(rim)
        def _():
            edge_part_out[u] = jnp.where(z == 0, near_rows(u, -1), near_rows(u, BPD)).astype(BF16)
            edge_part_copy(u).start()

    def relay_terms(u):
        h = u // 2
        for side in (0, 1):
            relay_copy(u, side).wait_send()
            terms_copy(u, side).wait_recv()

        @pl.loop(0, RELAY)
        def _(k):
            from_left = slot_t[p_l * H + h, T_RIGHT] + k
            from_right = slot_t[p_r * H + h, T_LEFT] + k
            relay_out[u][0, k] = terms_in[u][FROM_L + jnp.minimum(from_left, MAIN - 1)]
            relay_out[u][1, k] = terms_in[u][FROM_R + jnp.minimum(from_right, MAIN - 1)]

        for side in (0, 1):
            terms_relay_copy(u, side).start()

        @pl.when(inner)
        def _():
            part_first(u).wait_recv()
            mine = jnp.where(x == 1, anchor(u, 0), anchor(u, 1))
            part_out[u, 1] = (mine + part_in[u, 0].astype(F32)).astype(BF16)

        @pl.when(outer)
        def _():
            part_out[u, 1] = jnp.where(x == 0, anchor(u, 1), anchor(u, 0)).astype(BF16)

        @pl.when(leftward())
        def _():
            part_second(u, 1).start()

        @pl.when(jnp.logical_not(leftward()))
        def _():
            part_second(u, 0).start()

    def land(u):
        gather_sent(u)

        @pl.when(outer)
        def _():
            for side in (0, 1):
                anchor_copy(u, side).wait_send()
                part_second(u, side).wait_recv()

        for side in (0, 1):
            terms_relay_copy(u, side).wait_recv()

        @pl.loop(0, RELAY)
        def _(k):
            terms_in[u][B_RR + k] = terms_relay[u][0, k]
            terms_in[u][B_RL + k] = terms_relay[u][1, k]

    def rows(u, group):
        h = u // 2
        for away in {1: (4,), 2: (3, 5), 3: (2, 6), 4: (1, 7), 5: (0,)}[group]:
            row = lax.rem(z + away, NZ)

            @pl.loop(0, BPD)
            def _(b):
                t = row * BPD + b
                total = terms_in[u][source_t[h, t * DEEP]].astype(F32)
                for k in range(1, DEEP):
                    total += terms_in[u][source_t[h, t * DEEP + k]].astype(F32)
                table[u][t] = total.astype(BF16)

            def add(t, part):
                table[u][t] = (table[u][t].astype(F32) + part).astype(BF16)

            def both():
                return part_in[u, 1].astype(F32) + part_in[u, 2].astype(F32)

            @pl.when((x == 0) & (row == 0))
            def _():
                add(0, anchor(u, 0) + both())

            @pl.when((x == NX - 1) & (row == NZ - 1))
            def _():
                add(TARGETS - 1, anchor(u, 1) + both())

            if away == NZ - 1:

                @pl.when(z > 0)
                def _():
                    add(row * BPD + BPD - 1, near_rows(u, -1))

            if away == 1:

                @pl.when(z < NZ - 1)
                def _():
                    add(row * BPD, near_rows(u, BPD))

    def sum_copy(u, s, half, right):
        row = lax.rem(z + 5 - s, NZ) if right else lax.rem(z + NZ - 5 + s, NZ)
        way = 0 if right else 1
        return to(
            z_r if right else z_l,
            table[u].at[pl.ds(row * BPD + half * HALF, HALF)],
            (sums_r if right else sums_l)[u].at[s - 1, pl.ds(half * HALF, HALF)],
            rs_sent.at[u],
            rs_sem.at[u % 2, s - 1, half, way],
        )

    def sum_moves(s):
        return moves(4 if s == 1 else 1)

    def sum_start(u):
        for half, right in sum_moves(1):
            sum_copy(u, 1, half, right).start()

    def sum_step(u, s, half):
        for right in (True, False):
            if (half, right) in sum_moves(s - 1):
                sum_copy(u, s - 1, half, right).wait_recv()
                row = lax.rem(z + 5 - s, NZ) if right else lax.rem(z + NZ - 5 + s, NZ)
                came = (sums_r if right else sums_l)[u]

                @pl.loop(0, HALF)
                def _(b):
                    here = row * BPD + half * HALF + b
                    table[u][here] = (
                        table[u][here].astype(F32) + came[s - 2, half * HALF + b].astype(F32)
                    ).astype(BF16)

            sum_copy(u, s, half, right).start()

    def finish(u):
        h, p = u // 2, u % 2
        for half, right in sum_moves(4):
            sum_copy(u, 4, half, right).wait_recv()

        @pl.when(rim)
        def _():
            edge_part_copy(u).wait_recv()
            lone = pl.ds(pl.multiple_of(jnp.where(z == 0, 1, BPD) * BLOCK, BLOCK), BLOCK)
            near[h][p, lone] += edge_part_in[u].astype(F32)

        @pl.loop(0, BPD)
        def _(b):
            total = (
                table[u][z * BPD + b].astype(F32)
                + sums_r[u][3, b].astype(F32)
                + sums_l[u][3, b].astype(F32)
                + near[h][p, pl.ds(pl.multiple_of((b + 1) * BLOCK, BLOCK), BLOCK)]
            )
            (out_k, out_v)[p][h, b] = total.astype(BF16)

    def drain(u):
        all_sent(u, rs_sent)
        for side in (0, 1):
            terms_copy(u, side).wait_send()
            terms_relay_copy(u, side).wait_send()

        @pl.when(inner)
        def _():
            anchor_pass(u).wait_send()
            part_first(u).wait_send()

        @pl.when(leftward())
        def _():
            part_second(u, 1).wait_send()

        @pl.when(jnp.logical_not(leftward()))
        def _():
            part_second(u, 0).wait_send()

        @pl.when(rim)
        def _():
            edge_part_copy(u).wait_send()

    steps = {
        "GS": gather_start,
        "G": gather_step,
        "GE": gather_end,
        "SR": send_relays,
        "SM": send_merged,
        "C": compute,
        "ST": send_terms,
        "RT": relay_terms,
        "L": land,
        "R": rows,
        "SS": sum_start,
        "S": sum_step,
        "F": finish,
    }
    for name, *where in ORDER:
        steps[name](*where)
    for u in range(UNITS):
        drain(u)

    @pl.when(rim)
    def _():
        edge_copy().wait_send()


def local(query, key, value, out_grad, random_links):
    def head_major(array):
        return array.reshape(BPD, BLOCK, H, HD).transpose(2, 0, 1, 3)

    def seq_major(array):
        return array.transpose(1, 2, 0, 3).reshape(BPD * BLOCK, H, HD)

    kv = jnp.stack((head_major(key), head_major(value)), axis=1).reshape(UNITS, BPD, BLOCK, HD)
    block = (BLOCK, HD)

    def per(count, *shape, dtype=BF16):
        return [pltpu.VMEM(shape, dtype) for _ in range(count)]

    dma = pltpu.SemaphoreType.DMA
    vmem = pl.BlockSpec(memory_space=pltpu.VMEM)
    outs = pl.pallas_call(
        kernel,
        out_shape=[jax.ShapeDtypeStruct((H, BPD, BLOCK, HD), BF16)] * 4,
        in_specs=[vmem] * 4,
        out_specs=[vmem] * 4,
        scratch_shapes=[
            per(UNITS, TARGETS, *block),
            per(UNITS, 2, RELAY, *block),
            per(UNITS, 2, RELAY, *block),
            per(UNITS, 2, MAIN, *block),
            per(UNITS, RECEIVED, *block),
            per(UNITS, B_SIZE, *block),
            per(UNITS, 2, RELAY, *block),
            per(UNITS, 4, BPD, *block),
            per(UNITS, 4, BPD, *block),
            per(H, 2, (BPD + 2) * BLOCK, HD, dtype=F32),
            per(H, 2, 2 * BLOCK, HD, dtype=F32),
            pltpu.VMEM((UNITS, 2, *block), BF16),
            pltpu.VMEM((UNITS, 2, *block), BF16),
            pltpu.VMEM((UNITS, 3, *block), BF16),
            pltpu.VMEM((UNITS, *block), BF16),
            pltpu.VMEM((UNITS, *block), BF16),
            pltpu.VMEM((UNITS, *block), BF16),
            pltpu.VMEM((UNITS, *block), BF16),
            pltpu.VMEM((2, 2 * BLOCK, HD), BF16),
            pltpu.VMEM((2, (BPD + 2) * BLOCK, HD), BF16),
            pltpu.VMEM((2, REFS, *block), BF16),
            dma((UNITS,)),
            dma((2, 4, 2, 2)),
            dma((UNITS,)),
            dma((2, 4, 2, 2)),
            dma((4, UNITS, 2, 2)),
            dma((UNITS, 3, 2)),
            dma((UNITS, 3, 2)),
            dma((UNITS + 1, 2)),
            pltpu.VMEM((NX * H, T_WIDTH), jnp.int32),
            pltpu.VMEM((H, TARGETS * DEEP), jnp.int32),
            pltpu.SMEM((NX * H, T_WIDTH), jnp.int32),
            pltpu.SMEM((H, TARGETS * DEEP), jnp.int32),
            dma((2,)),
        ],
        compiler_params=pltpu.CompilerParams(
            collective_id=0, has_side_effects=True, vmem_limit_bytes=60 * 2**20
        ),
        cost_estimate=pl.CostEstimate(
            flops=2 * 6 * BLOCK * 8 * BLOCK * HD * H * BPD,
            bytes_accessed=4 * 2**20,
            transcendentals=H * BPD * BLOCK * 8 * BLOCK,
        ),
    )(kv, head_major(query), head_major(out_grad), named_blocks(random_links))
    return tuple(seq_major(array) for array in outs)


def solution(mesh):
    split = P("ctx", "head", None)
    return jax.shard_map(
        local,
        mesh=mesh,
        in_specs=(split, split, split, split, P(None, "head", None)),
        out_specs=(split, split, split, split),
        check_vma=False,
    )
```

```python
import math

import jax
import jax.numpy as jnp
from jax import lax
from jax.experimental import pallas as pl
from jax.experimental.pallas import tpu as pltpu
from jax.sharding import PartitionSpec as P

BLOCK = 64
HD = 128
NX = 4
NZ = 8
BPD = 8
HALF = BPD // 2
H = 4
R = 3
REFS = BPD * R
TARGETS = NZ * BPD
MAIN = 16
RELAY = 8
UNITS = 2 * H
FROM_R, FROM_L, OWN = 0, MAIN, 2 * MAIN
RECEIVED = OWN + MAIN
B_RR = 2 * MAIN
B_RL = B_RR + RELAY
B_OWN = B_RL + RELAY
B_ZERO = B_OWN + MAIN
B_SIZE = B_ZERO + 1
T_RELAY = RECEIVED
T_GIVER = T_RELAY + 2 * RELAY
T_PLACE = T_GIVER + RECEIVED
T_RIGHT = T_PLACE + REFS
T_LEFT = T_RIGHT + 1
T_WIDTH = 256
PIECES = 2
DEEP = 8
F32 = jnp.float32
BF16 = jnp.bfloat16
MESH = pl.DeviceIdType.MESH
SCALE = 1.0 / math.sqrt(HD)


def named_blocks(links):
    z = lax.axis_index("ctx") % NZ
    row = lax.dynamic_slice_in_dim(links.reshape(NX, NZ, BPD, H, R), z, 1, 1)[:, 0]
    return row.transpose(0, 2, 1, 3).reshape(NX * H, REFS)


def slot_tables(named, x):
    plane = lax.broadcasted_iota(jnp.int32, named.shape, 0) // H
    lane = lax.broadcasted_iota(jnp.int32, named.shape, 1)
    away = ((named >> 6) - plane) & (NX - 1)
    target = named & (TARGETS - 1)

    def entry(array, e):
        return array[:, e : e + 1]

    rank = jnp.zeros_like(named)
    n_r, n_o, n_l = (jnp.zeros((NX * H, 1), jnp.int32) for _ in range(3))
    for e in range(REFS):
        way = entry(away, e)
        rank += jnp.where((away == way) & (lane > e), 1, 0)
        n_r += jnp.where(way == 1, 1, 0)
        n_o += jnp.where(way == 2, 1, 0)
        n_l += jnp.where(way == 3, 1, 0)
    by_right = jnp.minimum(n_o, jnp.minimum(RELAY, MAIN - n_r))
    right_way = rank < by_right
    relay_rank = jnp.where(right_way, rank, rank - by_right)
    opposite = jnp.where(right_way, FROM_R + n_r + rank, FROM_L + n_l + relay_rank)
    place = jnp.where(
        away == 0,
        OWN + rank,
        jnp.where(away == 1, FROM_R + rank, jnp.where(away == 3, FROM_L + rank, opposite)),
    )
    code = jnp.where(away == 2, TARGETS + relay_rank, target)
    relay_place = jnp.where(
        away == 2, T_RELAY + relay_rank + jnp.where(right_way, 0, RELAY), -1
    )
    spots = lax.broadcasted_iota(jnp.int32, (NX * H, T_WIDTH), 1)
    first = jnp.where(spots == T_RIGHT, n_r, jnp.where(spots == T_LEFT, n_l, 0))
    for e in range(REFS):
        here = entry(place, e)
        at = jnp.where(
            spots < T_RELAY,
            here,
            jnp.where(
                spots < T_GIVER,
                entry(relay_place, e),
                jnp.where(spots < T_PLACE, T_GIVER + here, T_PLACE + e),
            ),
        )
        put = jnp.where(
            spots < T_RELAY,
            entry(code, e),
            jnp.where(
                spots < T_GIVER, entry(target, e), jnp.where(spots < T_PLACE, e, here)
            ),
        )
        first += jnp.where(at == spots, put, 0)
    most = jnp.where(
        spots < T_RELAY,
        TARGETS + RELAY - 1,
        jnp.where(
            spots < T_GIVER,
            TARGETS - 1,
            jnp.where(spots < T_PLACE, REFS - 1, jnp.where(spots < T_RIGHT, RECEIVED - 1, REFS)),
        ),
    )
    first = jnp.clip(first, 0, most)
    landing = jnp.where(
        away == 0,
        B_OWN + rank,
        jnp.where(
            away == 1,
            FROM_L + rank,
            jnp.where(
                away == 3, FROM_R + rank, jnp.where(right_way, B_RL, B_RR) + relay_rank
            ),
        ),
    )
    mine = jnp.where((named >> 6) == x, target, -1)
    cells = lax.broadcasted_iota(jnp.int32, (H, TARGETS * DEEP), 1)
    sources = jnp.full((H, TARGETS * DEEP), B_ZERO, jnp.int32)
    parts = [slice(a * H, (a + 1) * H) for a in range(NX)]
    for a in range(NX):
        aim = mine[parts[a]]
        depth = jnp.zeros_like(aim)
        for b in range(a + 1):
            for e in range(REFS):
                same = aim == entry(mine[parts[b]], e)
                if b == a:
                    same = same & (lane[:H] > e)
                depth += jnp.where(same, 1, 0)
        cell = jnp.where(aim >= 0, aim * DEEP + depth, -1)
        land = landing[parts[a]]
        for e in range(REFS):
            sources += jnp.where(entry(cell, e) == cells, entry(land, e) - B_ZERO, 0)
    return first, jnp.clip(sources, 0, B_SIZE - 1)


ORDER = (
    ("GS", 0), ("G", 0, 2, 0), ("G", 0, 2, 1), ("G", 0, 3, 0), ("G", 0, 3, 1), ("GS", 1),
    ("G", 0, 4, 0), ("G", 0, 4, 1), ("G", 1, 2, 0), ("G", 1, 2, 1), ("GE", 0), ("SR", 0),
    ("G", 1, 3, 0), ("G", 1, 3, 1), ("GS", 2), ("SM", 0), ("G", 1, 4, 0), ("G", 1, 4, 1),
    ("G", 2, 2, 0), ("GE", 1), ("G", 2, 2, 1), ("SR", 1), ("G", 2, 3, 0), ("G", 2, 3, 1),
    ("GS", 3), ("G", 2, 4, 0), ("SM", 1), ("G", 2, 4, 1), ("G", 3, 2, 0), ("GE", 2),
    ("G", 3, 2, 1), ("SR", 2), ("G", 3, 3, 0), ("C", 0, 0), ("SM", 2), ("G", 3, 3, 1), ("GS", 4),
    ("C", 0, 1), ("G", 3, 4, 0), ("G", 3, 4, 1), ("ST", 0), ("G", 4, 2, 0), ("G", 4, 2, 1),
    ("ST", 1), ("G", 4, 3, 0), ("GE", 3), ("G", 4, 3, 1), ("GS", 5), ("SR", 3), ("G", 4, 4, 0),
    ("RT", 0), ("G", 4, 4, 1), ("G", 5, 2, 0), ("G", 5, 2, 1), ("G", 5, 3, 0), ("GE", 4),
    ("G", 5, 3, 1), ("GS", 6), ("RT", 1), ("G", 5, 4, 0), ("SM", 3), ("G", 5, 4, 1),
    ("G", 6, 2, 0), ("SR", 4), ("L", 0), ("G", 6, 2, 1), ("R", 0, 2), ("GE", 5), ("SR", 5),
    ("R", 0, 3), ("G", 6, 3, 0), ("R", 0, 1), ("SM", 4), ("L", 1), ("R", 1, 2), ("R", 1, 1),
    ("G", 6, 3, 1), ("SS", 0), ("GS", 7), ("C", 1, 0), ("SM", 5), ("G", 6, 4, 0), ("G", 7, 2, 0),
    ("C", 1, 1), ("SS", 1), ("S", 0, 2, 0), ("ST", 2), ("R", 1, 5), ("G", 6, 4, 1), ("R", 1, 3),
    ("R", 0, 4), ("S", 1, 2, 0), ("ST", 3), ("C", 2, 0), ("G", 7, 2, 1), ("S", 0, 2, 1), ("RT", 2),
    ("GE", 6), ("S", 1, 2, 1), ("G", 7, 3, 0), ("C", 2, 1), ("S", 0, 3, 0), ("R", 1, 4),
    ("G", 7, 3, 1), ("RT", 3), ("ST", 5), ("L", 2), ("S", 1, 3, 0), ("R", 2, 2), ("S", 1, 3, 1),
    ("G", 7, 4, 0), ("L", 3), ("G", 7, 4, 1), ("S", 1, 4, 0), ("R", 3, 1), ("S", 1, 4, 1),
    ("R", 3, 5), ("S", 0, 3, 1), ("SS", 3), ("SR", 6), ("S", 0, 4, 0), ("R", 3, 3), ("R", 2, 1),
    ("R", 3, 2), ("GE", 7), ("R", 2, 3), ("SR", 7), ("S", 0, 4, 1), ("F", 1), ("SM", 6),
    ("S", 3, 2, 0), ("R", 2, 4), ("SS", 2), ("R", 3, 4), ("S", 3, 2, 1), ("R", 0, 5),
    ("S", 3, 3, 0), ("SM", 7), ("ST", 4), ("F", 0), ("S", 2, 2, 0), ("RT", 5), ("S", 2, 2, 1),
    ("S", 2, 3, 0), ("S", 3, 3, 1), ("R", 2, 5), ("S", 2, 3, 1), ("S", 2, 4, 0), ("C", 3, 0),
    ("S", 3, 4, 0), ("S", 2, 4, 1), ("S", 3, 4, 1), ("RT", 4), ("C", 3, 1), ("L", 5), ("R", 5, 1),
    ("SS", 5), ("ST", 6), ("R", 5, 2), ("ST", 7), ("L", 4), ("R", 4, 1), ("SS", 4), ("R", 4, 2),
    ("F", 3), ("S", 5, 2, 0), ("R", 4, 3), ("S", 5, 2, 1), ("R", 4, 4), ("F", 2), ("S", 4, 2, 0),
    ("R", 5, 5), ("S", 4, 2, 1), ("R", 5, 3), ("S", 5, 3, 0), ("S", 4, 3, 0), ("R", 5, 4),
    ("R", 4, 5), ("S", 4, 3, 1), ("S", 5, 3, 1), ("RT", 6), ("RT", 7), ("S", 4, 4, 0),
    ("S", 5, 4, 0), ("L", 6), ("S", 4, 4, 1), ("R", 6, 2), ("R", 6, 1), ("SS", 6), ("S", 5, 4, 1),
    ("L", 7), ("R", 7, 3), ("R", 7, 1), ("R", 7, 2), ("SS", 7), ("F", 4), ("S", 6, 2, 0),
    ("S", 6, 2, 1), ("F", 5), ("R", 6, 3), ("S", 7, 2, 0), ("R", 6, 5), ("S", 7, 2, 1),
    ("R", 6, 4), ("S", 6, 3, 0), ("R", 7, 4), ("S", 7, 3, 0), ("S", 7, 3, 1), ("S", 6, 3, 1),
    ("R", 7, 5), ("S", 7, 4, 0), ("S", 6, 4, 0), ("S", 6, 4, 1), ("S", 7, 4, 1), ("F", 6),
    ("F", 7),
)


def kernel(
    kv,
    query,
    grad,
    links,
    out_o,
    out_q,
    out_k,
    out_v,
    table,
    relay_out,
    relay_in,
    merged_out,
    received,
    terms_in,
    terms_relay,
    sums_r,
    sums_l,
    near,
    anchor_acc,
    anchor_in,
    part_out,
    part_in,
    edge_out,
    edge_in,
    edge_part_out,
    edge_part_in,
    anchor_kv,
    wide,
    terms,
    ag_sent,
    ag_sem,
    rs_sent,
    rs_sem,
    x_sem,
    anchor_sem,
    part_sem,
    edge_sem,
    slot_v,
    source_v,
    slot_t,
    source_t,
    table_sem,
):
    ctx = lax.axis_index("ctx")
    x, z = ctx // NZ, ctx % NZ
    z_r = x * NZ + lax.rem(z + 1, NZ)
    z_l = x * NZ + lax.rem(z + NZ - 1, NZ)
    p_r = lax.rem(x + 1, NX)
    p_l = lax.rem(x + NX - 1, NX)
    p_o = lax.rem(x + 2, NX)
    x_r = p_r * NZ + z
    x_l = p_l * NZ + z
    outer = (x == 0) | (x == NX - 1)
    inner = (x == 1) | (x == NX - 2)
    rim = (z == 0) | (z == NZ - 1)
    beyond = lax.rem(jnp.where(z == 0, ctx + NX * NZ - 1, ctx + 1), NX * NZ)

    def to(device, src, dst, sent, came=None):
        return pltpu.make_async_remote_copy(
            src_ref=src,
            dst_ref=dst,
            send_sem=sent if came is not None else sent.at[0],
            recv_sem=came if came is not None else sent.at[1],
            device_id={"ctx": device},
            device_id_type=MESH,
        )

    barrier = pltpu.get_barrier_semaphore()

    def place_own(u):
        @pl.loop(0, BPD)
        def _(b):
            table[u][z * BPD + b] = kv[u, b]

    def greet(device):
        pl.semaphore_signal(barrier, inc=1, device_id={"ctx": device}, device_id_type=MESH)

    for device in (z_r, z_l, x_r, x_l):
        greet(device)

    for u in range(UNITS):
        place_own(u)

    @pl.when(rim)
    def _():
        @pl.loop(0, UNITS)
        def _(u):
            edge_out[u] = kv[u, jnp.where(z == 0, 0, BPD - 1)]

    pl.semaphore_wait(barrier, 4)

    def gather_copy(u, s, half, right):
        row = lax.rem(z + NZ - (s - 1), NZ) if right else lax.rem(z + s - 1, NZ)
        cut = pl.ds(row * BPD + half * HALF, HALF)
        src = kv.at[u, pl.ds(half * HALF, HALF)] if s == 1 else table[u].at[cut]
        way = 0 if right else 1
        came = ag_sem.at[u % 2, s - 1, half, way]
        return to(z_r if right else z_l, src, table[u].at[cut], ag_sent.at[u], came)

    def moves(s):
        return [
            (half, right)
            for half in (0, 1)
            for right in (True, False)
            if s < 4 or right == (half == 0)
        ]

    def gather_start(u):
        for half, right in moves(1):
            gather_copy(u, 1, half, right).start()

    def gather_step(u, s, half):
        for right in (True, False):
            gather_copy(u, s - 1, half, right).wait_recv()
            if (half, right) in moves(s):
                gather_copy(u, s, half, right).start()

    def gather_end(u):
        for half, right in moves(4):
            gather_copy(u, 4, half, right).wait_recv()

    def all_sent(u, sent):
        whole = table[u].at[pl.ds(0, 14 * HALF)]
        to(z_r, whole, whole, sent.at[u], ag_sem.at[0, 0, 0, 0]).wait_send()

    def gather_sent(u):
        all_sent(u, ag_sent)

    def edge_copy():
        return to(beyond, edge_out, edge_in, edge_sem.at[UNITS])

    def send_edges():
        @pl.when(rim)
        def _():
            edge_copy().start()

    def relay_copy(u, side):
        return to(
            (x_r, x_l)[side], relay_out[u].at[side], relay_in[u].at[1 - side], x_sem.at[0, u, side]
        )

    def merged_copy(u, side):
        return to(
            (x_r, x_l)[side],
            merged_out[u].at[side],
            received[u].at[pl.ds((FROM_L, FROM_R)[side], MAIN)],
            x_sem.at[1, u, side],
        )

    def anchor_copy(u, side):
        return to(
            (x_r, x_l)[side],
            table[u].at[jnp.where(x == 0, 0, TARGETS - 1)],
            anchor_in.at[u, 0],
            anchor_sem.at[u, side],
        )

    def anchor_arrived(u):
        @pl.when((x == 0) | (x == 1))
        def _():
            anchor_copy(u, 0).wait_recv()

        @pl.when((x == 2) | (x == 3))
        def _():
            anchor_copy(u, 1).wait_recv()

    def anchor_pass(u):
        return to(
            jnp.where(x == 1, x_r, x_l), anchor_in.at[u, 0], anchor_in.at[u, 1], anchor_sem.at[u, 2]
        )

    def send_relays(u):
        h = u // 2

        @pl.when(outer)
        def _():
            for side in (0, 1):
                anchor_copy(u, side).start()

        @pl.loop(0, RELAY)
        def _(k):
            relay_out[u][0, k] = table[u][slot_t[p_o * H + h, T_RELAY + RELAY + k]]
            relay_out[u][1, k] = table[u][slot_t[p_o * H + h, T_RELAY + k]]

        for side in (0, 1):
            relay_copy(u, side).start()

        @pl.loop(0, MAIN)
        def _(k):
            received[u][OWN + k] = table[u][slot_t[x * H + h, OWN + k]]

    def send_merged(u):
        h = u // 2
        for side in (0, 1):
            relay_copy(u, side).wait_recv()

        @pl.loop(0, MAIN)
        def _(k):
            for side, plane, first, back in ((0, p_r, FROM_L, 1), (1, p_l, FROM_R, 0)):
                code = slot_t[plane * H + h, first + k]
                direct = table[u][jnp.minimum(code, TARGETS - 1)]
                passed = relay_in[u][back, jnp.maximum(code - TARGETS, 0)]
                merged_out[u][side, k] = jnp.where(code < TARGETS, direct, passed)

        for side in (0, 1):
            merged_copy(u, side).start()
        anchor_arrived(u)

        @pl.when(inner)
        def _():
            anchor_pass(u).start()

        if u == 0:
            send_edges()

    def lay_keys(h):
        for p in (0, 1):
            u = 2 * h + p
            for side in (0, 1):
                merged_copy(u, side).wait_recv()

            @pl.when(inner)
            def _():
                anchor_pass(u).wait_recv()

            row_above = lax.rem(z + NZ - 1, NZ) * BPD + BPD - 1
            row_below = lax.rem(z + 1, NZ) * BPD
            wide[p, 0:BLOCK] = jnp.where(z > 0, table[u][row_above], edge_in[u])
            wide[p, BLOCK * (BPD + 1) :] = jnp.where(z < NZ - 1, table[u][row_below], edge_in[u])
            for b in range(BPD):
                wide[p, BLOCK * (b + 1) : BLOCK * (b + 2)] = kv[u, b]
            came, passed = anchor_in[u, 0], anchor_in[u, 1]
            anchor_kv[p, :BLOCK] = jnp.where(x == 0, table[u][0], jnp.where(x == 2, passed, came))
            anchor_kv[p, BLOCK:] = jnp.where(
                x == 3, table[u][TARGETS - 1], jnp.where(x == 1, passed, came)
            )
        near[h][...] = jnp.zeros_like(near[h])
        anchor_acc[h][...] = jnp.zeros_like(anchor_acc[h])

    def compute(h, piece):
        if piece == 0:
            if h == 0:

                @pl.when(rim)
                def _():
                    edge_copy().wait_recv()

            lay_keys(h)
        column = lax.broadcasted_iota(jnp.int32, (1, 8 * BLOCK), 1)

        @pl.loop(piece * BPD // PIECES, (piece + 1) * BPD // PIECES)
        def _(i):
            rows = pl.ds(pl.multiple_of(i * BLOCK, BLOCK), 3 * BLOCK)
            spots = [slot_t[x * H + h, T_PLACE + i * R + r] for r in range(R)]
            keys, values = (
                jnp.concatenate(
                    [wide[p, rows], anchor_kv[p]] + [received[2 * h + p][s] for s in spots], axis=0
                )
                for p in (0, 1)
            )
            q, g = query[h, i], grad[h, i]
            block = ctx * BPD + i
            low = jnp.where(block == 0, BLOCK, 0)
            cut = jnp.where(block == NX * NZ * BPD - 1, 2 * BLOCK, 3 * BLOCK)
            masked = (column < low) | ((column >= cut) & (column < 3 * BLOCK))
            contract_last = (((1,), (1,)), ((), ()))
            contract_first = (((0,), (0,)), ((), ()))
            scores = lax.dot_general(q, keys, contract_last, preferred_element_type=F32) * SCALE
            scores = jnp.where(masked, -1e30, scores)
            powers = jnp.exp(scores - jnp.max(scores, axis=-1, keepdims=True))
            probs = powers * (1.0 / jnp.sum(powers, axis=-1, keepdims=True))
            low_probs = probs.astype(BF16)
            attended = jnp.dot(low_probs, values, preferred_element_type=F32).astype(BF16)
            out_o[h, i] = attended
            delta = jnp.sum(g.astype(F32) * attended.astype(F32), axis=-1, keepdims=True)
            grad_probs = lax.dot_general(g, values, contract_last, preferred_element_type=F32)
            grad_scores = (probs * (grad_probs - delta)).astype(BF16)
            out_q[h, i] = (
                jnp.dot(grad_scores, keys, preferred_element_type=F32) * SCALE
            ).astype(BF16)
            key_part = (
                lax.dot_general(grad_scores, q, contract_first, preferred_element_type=F32) * SCALE
            )
            value_part = lax.dot_general(
                low_probs, g, contract_first, preferred_element_type=F32
            )
            for p, part in ((0, key_part), (1, value_part)):
                near[h][p, rows] += part[: 3 * BLOCK]
                anchor_acc[h][p] += part[3 * BLOCK : 5 * BLOCK]
                for r in range(R):
                    terms[p, i * R + r] = part[(5 + r) * BLOCK : (6 + r) * BLOCK].astype(BF16)

    def terms_copy(u, side):
        return to(
            (x_r, x_l)[side],
            merged_out[u].at[side],
            terms_in[u].at[pl.ds((FROM_L, FROM_R)[side], MAIN)],
            x_sem.at[2, u, side],
        )

    def terms_relay_copy(u, side):
        return to(
            (x_r, x_l)[side], relay_out[u].at[side], terms_relay[u].at[1 - side],
            x_sem.at[3, u, side],
        )

    def part_first(u):
        return to(
            jnp.where(x == 1, x_r, x_l), part_out.at[u, 0], part_in.at[u, 0], part_sem.at[u, 0]
        )

    def part_second(u, side):
        return to(
            (x_r, x_l)[side], part_out.at[u, 1], part_in.at[u, 1 + side], part_sem.at[u, 1 + side]
        )

    def leftward():
        return (x == 0) | (x == 1)

    def edge_part_copy(u):
        return to(beyond, edge_part_out.at[u], edge_part_in.at[u], edge_sem.at[u])

    def anchor(u, which):
        return anchor_acc[u // 2][u % 2, which * BLOCK : (which + 1) * BLOCK]

    def near_rows(u, b):
        return near[u // 2][u % 2, (b + 1) * BLOCK : (b + 2) * BLOCK]

    def send_terms(u):
        h, p = u // 2, u % 2
        for side in (0, 1):
            merged_copy(u, side).wait_send()

        @pl.loop(0, MAIN)
        def _(k):
            merged_out[u][0, k] = terms[p, slot_t[x * H + h, T_GIVER + FROM_R + k]]
            merged_out[u][1, k] = terms[p, slot_t[x * H + h, T_GIVER + FROM_L + k]]
            terms_in[u][B_OWN + k] = terms[p, slot_t[x * H + h, T_GIVER + OWN + k]]

        for side in (0, 1):
            terms_copy(u, side).start()
        terms_in[u][B_ZERO] = jnp.zeros((BLOCK, HD), BF16)

        @pl.when(inner)
        def _():
            part_out[u, 0] = jnp.where(x == 1, anchor(u, 1), anchor(u, 0)).astype(BF16)
            part_first(u).start()

        @pl.when(rim)
        def _():
            edge_part_out[u] = jnp.where(z == 0, near_rows(u, -1), near_rows(u, BPD)).astype(BF16)
            edge_part_copy(u).start()

    def relay_terms(u):
        h = u // 2
        for side in (0, 1):
            relay_copy(u, side).wait_send()
            terms_copy(u, side).wait_recv()

        @pl.loop(0, RELAY)
        def _(k):
            from_left = slot_t[p_l * H + h, T_RIGHT] + k
            from_right = slot_t[p_r * H + h, T_LEFT] + k
            relay_out[u][0, k] = terms_in[u][FROM_L + jnp.minimum(from_left, MAIN - 1)]
            relay_out[u][1, k] = terms_in[u][FROM_R + jnp.minimum(from_right, MAIN - 1)]

        for side in (0, 1):
            terms_relay_copy(u, side).start()

        @pl.when(inner)
        def _():
            part_first(u).wait_recv()
            mine = jnp.where(x == 1, anchor(u, 0), anchor(u, 1))
            part_out[u, 1] = (mine + part_in[u, 0].astype(F32)).astype(BF16)

        @pl.when(outer)
        def _():
            part_out[u, 1] = jnp.where(x == 0, anchor(u, 1), anchor(u, 0)).astype(BF16)

        @pl.when(leftward())
        def _():
            part_second(u, 1).start()

        @pl.when(jnp.logical_not(leftward()))
        def _():
            part_second(u, 0).start()

    def land(u):
        gather_sent(u)

        @pl.when(outer)
        def _():
            for side in (0, 1):
                anchor_copy(u, side).wait_send()
                part_second(u, side).wait_recv()

        for side in (0, 1):
            terms_relay_copy(u, side).wait_recv()

        @pl.loop(0, RELAY)
        def _(k):
            terms_in[u][B_RR + k] = terms_relay[u][0, k]
            terms_in[u][B_RL + k] = terms_relay[u][1, k]

    def rows(u, group):
        h = u // 2
        for away in {1: (4,), 2: (3, 5), 3: (2, 6), 4: (1, 7), 5: (0,)}[group]:
            row = lax.rem(z + away, NZ)

            @pl.loop(0, BPD)
            def _(b):
                t = row * BPD + b
                total = terms_in[u][source_t[h, t * DEEP]].astype(F32)
                for k in range(1, DEEP):
                    total += terms_in[u][source_t[h, t * DEEP + k]].astype(F32)
                table[u][t] = total.astype(BF16)

            def add(t, part):
                table[u][t] = (table[u][t].astype(F32) + part).astype(BF16)

            def both():
                return part_in[u, 1].astype(F32) + part_in[u, 2].astype(F32)

            @pl.when((x == 0) & (row == 0))
            def _():
                add(0, anchor(u, 0) + both())

            @pl.when((x == NX - 1) & (row == NZ - 1))
            def _():
                add(TARGETS - 1, anchor(u, 1) + both())

            if away == NZ - 1:

                @pl.when(z > 0)
                def _():
                    add(row * BPD + BPD - 1, near_rows(u, -1))

            if away == 1:

                @pl.when(z < NZ - 1)
                def _():
                    add(row * BPD, near_rows(u, BPD))

    def sum_copy(u, s, half, right):
        row = lax.rem(z + 5 - s, NZ) if right else lax.rem(z + NZ - 5 + s, NZ)
        way = 0 if right else 1
        return to(
            z_r if right else z_l,
            table[u].at[pl.ds(row * BPD + half * HALF, HALF)],
            (sums_r if right else sums_l)[u].at[s - 1, pl.ds(half * HALF, HALF)],
            rs_sent.at[u],
            rs_sem.at[u % 2, s - 1, half, way],
        )

    def sum_moves(s):
        return moves(4 if s == 1 else 1)

    def sum_start(u):
        for half, right in sum_moves(1):
            sum_copy(u, 1, half, right).start()

    def sum_step(u, s, half):
        for right in (True, False):
            if (half, right) in sum_moves(s - 1):
                sum_copy(u, s - 1, half, right).wait_recv()
                row = lax.rem(z + 5 - s, NZ) if right else lax.rem(z + NZ - 5 + s, NZ)
                came = (sums_r if right else sums_l)[u]

                @pl.loop(0, HALF)
                def _(b):
                    here = row * BPD + half * HALF + b
                    table[u][here] = (
                        table[u][here].astype(F32) + came[s - 2, half * HALF + b].astype(F32)
                    ).astype(BF16)

            sum_copy(u, s, half, right).start()

    def finish(u):
        h, p = u // 2, u % 2
        for half, right in sum_moves(4):
            sum_copy(u, 4, half, right).wait_recv()

        @pl.when(rim)
        def _():
            edge_part_copy(u).wait_recv()
            lone = pl.ds(pl.multiple_of(jnp.where(z == 0, 1, BPD) * BLOCK, BLOCK), BLOCK)
            near[h][p, lone] += edge_part_in[u].astype(F32)

        @pl.loop(0, BPD)
        def _(b):
            total = (
                table[u][z * BPD + b].astype(F32)
                + sums_r[u][3, b].astype(F32)
                + sums_l[u][3, b].astype(F32)
                + near[h][p, pl.ds(pl.multiple_of((b + 1) * BLOCK, BLOCK), BLOCK)]
            )
            (out_k, out_v)[p][h, b] = total.astype(BF16)

    def drain(u):
        all_sent(u, rs_sent)
        for side in (0, 1):
            terms_copy(u, side).wait_send()
            terms_relay_copy(u, side).wait_send()

        @pl.when(inner)
        def _():
            anchor_pass(u).wait_send()
            part_first(u).wait_send()

        @pl.when(leftward())
        def _():
            part_second(u, 1).wait_send()

        @pl.when(jnp.logical_not(leftward()))
        def _():
            part_second(u, 0).wait_send()

        @pl.when(rim)
        def _():
            edge_part_copy(u).wait_send()

    steps = {
        "GS": gather_start,
        "G": gather_step,
        "GE": gather_end,
        "SR": send_relays,
        "SM": send_merged,
        "C": compute,
        "ST": send_terms,
        "RT": relay_terms,
        "L": land,
        "R": rows,
        "SS": sum_start,
        "S": sum_step,
        "F": finish,
    }
    first_name, *first_where = ORDER[0]
    steps[first_name](*first_where)
    slot_v[...], source_v[...] = slot_tables(links[...], x)
    copies = (
        pltpu.make_async_copy(slot_v, slot_t, table_sem.at[0]),
        pltpu.make_async_copy(source_v, source_t, table_sem.at[1]),
    )
    for copy in copies:
        copy.start()
    for copy in copies:
        copy.wait()
    for name, *where in ORDER[1:]:
        steps[name](*where)
    for u in range(UNITS):
        drain(u)

    @pl.when(rim)
    def _():
        edge_copy().wait_send()


def local(query, key, value, out_grad, random_links):
    def head_major(array):
        return array.reshape(BPD, BLOCK, H, HD).transpose(2, 0, 1, 3)

    def seq_major(array):
        return array.transpose(1, 2, 0, 3).reshape(BPD * BLOCK, H, HD)

    kv = jnp.stack((head_major(key), head_major(value)), axis=1).reshape(UNITS, BPD, BLOCK, HD)
    block = (BLOCK, HD)

    def per(count, *shape, dtype=BF16):
        return [pltpu.VMEM(shape, dtype) for _ in range(count)]

    dma = pltpu.SemaphoreType.DMA
    vmem = pl.BlockSpec(memory_space=pltpu.VMEM)
    outs = pl.pallas_call(
        kernel,
        out_shape=[jax.ShapeDtypeStruct((H, BPD, BLOCK, HD), BF16)] * 4,
        in_specs=[vmem] * 4,
        out_specs=[vmem] * 4,
        scratch_shapes=[
            per(UNITS, TARGETS, *block),
            per(UNITS, 2, RELAY, *block),
            per(UNITS, 2, RELAY, *block),
            per(UNITS, 2, MAIN, *block),
            per(UNITS, RECEIVED, *block),
            per(UNITS, B_SIZE, *block),
            per(UNITS, 2, RELAY, *block),
            per(UNITS, 4, BPD, *block),
            per(UNITS, 4, BPD, *block),
            per(H, 2, (BPD + 2) * BLOCK, HD, dtype=F32),
            per(H, 2, 2 * BLOCK, HD, dtype=F32),
            pltpu.VMEM((UNITS, 2, *block), BF16),
            pltpu.VMEM((UNITS, 2, *block), BF16),
            pltpu.VMEM((UNITS, 3, *block), BF16),
            pltpu.VMEM((UNITS, *block), BF16),
            pltpu.VMEM((UNITS, *block), BF16),
            pltpu.VMEM((UNITS, *block), BF16),
            pltpu.VMEM((UNITS, *block), BF16),
            pltpu.VMEM((2, 2 * BLOCK, HD), BF16),
            pltpu.VMEM((2, (BPD + 2) * BLOCK, HD), BF16),
            pltpu.VMEM((2, REFS, *block), BF16),
            dma((UNITS,)),
            dma((2, 4, 2, 2)),
            dma((UNITS,)),
            dma((2, 4, 2, 2)),
            dma((4, UNITS, 2, 2)),
            dma((UNITS, 3, 2)),
            dma((UNITS, 3, 2)),
            dma((UNITS + 1, 2)),
            pltpu.VMEM((NX * H, T_WIDTH), jnp.int32),
            pltpu.VMEM((H, TARGETS * DEEP), jnp.int32),
            pltpu.SMEM((NX * H, T_WIDTH), jnp.int32),
            pltpu.SMEM((H, TARGETS * DEEP), jnp.int32),
            dma((2,)),
        ],
        compiler_params=pltpu.CompilerParams(
            collective_id=0, has_side_effects=True, vmem_limit_bytes=60 * 2**20
        ),
        cost_estimate=pl.CostEstimate(
            flops=2 * 6 * BLOCK * 8 * BLOCK * HD * H * BPD,
            bytes_accessed=4 * 2**20,
            transcendentals=H * BPD * BLOCK * 8 * BLOCK,
        ),
    )(kv, head_major(query), head_major(out_grad), named_blocks(random_links))
    return tuple(seq_major(array) for array in outs)


def solution(mesh):
    split = P("ctx", "head", None)
    return jax.shard_map(
        local,
        mesh=mesh,
        in_specs=(split, split, split, split, P(None, "head", None)),
        out_specs=(split, split, split, split),
        check_vma=False,
    )
```

```python
import math

import jax
import jax.numpy as jnp
from jax import lax
from jax.experimental import pallas as pl
from jax.experimental.pallas import tpu as pltpu
from jax.sharding import PartitionSpec as P

BLOCK = 64
HD = 128
NX = 4
NZ = 8
BPD = 8
HALF = BPD // 2
H = 4
R = 3
REFS = BPD * R
TARGETS = NZ * BPD
MAIN = 16
RELAY = 8
UNITS = 2 * H
FROM_R, FROM_L, OWN = 0, MAIN, 2 * MAIN
RECEIVED = OWN + MAIN
B_RR = 2 * MAIN
B_RL = B_RR + RELAY
B_OWN = B_RL + RELAY
B_ZERO = B_OWN + MAIN
B_SIZE = B_ZERO + 1
T_RELAY = RECEIVED
T_GIVER = T_RELAY + 2 * RELAY
T_PLACE = T_GIVER + RECEIVED
T_WIDTH = 256
PIECES = 2
DEEP = 8
F32 = jnp.float32
BF16 = jnp.bfloat16
MESH = pl.DeviceIdType.MESH
SCALE = 1.0 / math.sqrt(HD)


def named_blocks(links):
    z = lax.axis_index("ctx") % NZ
    row = lax.dynamic_slice_in_dim(links.reshape(NX, NZ, BPD, H, R), z, 1, 1)[:, 0]
    return row.transpose(0, 2, 1, 3).reshape(NX * H, REFS)


def slot_tables(named, x):
    plane = lax.broadcasted_iota(jnp.int32, named.shape, 0) // H
    lane = lax.broadcasted_iota(jnp.int32, named.shape, 1)
    away = ((named >> 6) - plane) & (NX - 1)
    target = named & (TARGETS - 1)

    def entry(array, e):
        return array[:, e : e + 1]

    rank = jnp.zeros_like(named)
    n_r, n_o = (jnp.zeros((NX * H, 1), jnp.int32) for _ in range(2))
    for e in range(REFS):
        way = entry(away, e)
        rank += jnp.where((away == way) & (lane > e), 1, 0)
        n_r += jnp.where(way == 1, 1, 0)
        n_o += jnp.where(way == 2, 1, 0)
    by_right = jnp.minimum(n_o, jnp.minimum(RELAY, MAIN - n_r))
    right_way = rank < by_right
    relay_rank = jnp.where(right_way, rank, rank - by_right)
    opposite = jnp.where(right_way, FROM_R, FROM_L) + MAIN - 1 - relay_rank
    place = jnp.where(
        away == 0,
        OWN + rank,
        jnp.where(away == 1, FROM_R + rank, jnp.where(away == 3, FROM_L + rank, opposite)),
    )
    code = jnp.where(away == 2, TARGETS + relay_rank, target)
    relay_place = jnp.where(
        away == 2, T_RELAY + relay_rank + jnp.where(right_way, 0, RELAY), -1
    )
    spots = lax.broadcasted_iota(jnp.int32, (NX * H, T_WIDTH), 1)
    first = jnp.zeros_like(spots)
    for e in range(REFS):
        here = entry(place, e)
        at = jnp.where(
            spots < T_RELAY,
            here,
            jnp.where(
                spots < T_GIVER,
                entry(relay_place, e),
                jnp.where(spots < T_PLACE, T_GIVER + here, T_PLACE + e),
            ),
        )
        put = jnp.where(
            spots < T_RELAY,
            entry(code, e),
            jnp.where(
                spots < T_GIVER, entry(target, e), jnp.where(spots < T_PLACE, e, here)
            ),
        )
        first += jnp.where(at == spots, put, 0)
    most = jnp.where(
        spots < T_RELAY,
        TARGETS + RELAY - 1,
        jnp.where(
            spots < T_GIVER,
            TARGETS - 1,
            jnp.where(spots < T_PLACE, REFS - 1, RECEIVED - 1),
        ),
    )
    first = jnp.clip(first, 0, most)
    landing = jnp.where(
        away == 0,
        B_OWN + rank,
        jnp.where(
            away == 1,
            FROM_L + rank,
            jnp.where(
                away == 3, FROM_R + rank, jnp.where(right_way, B_RL, B_RR) + relay_rank
            ),
        ),
    )
    mine = jnp.where((named >> 6) == x, target, -1)
    cells = lax.broadcasted_iota(jnp.int32, (H, TARGETS * DEEP), 1)
    sources = jnp.full((H, TARGETS * DEEP), B_ZERO, jnp.int32)
    parts = [slice(a * H, (a + 1) * H) for a in range(NX)]
    for a in range(NX):
        aim = mine[parts[a]]
        depth = jnp.zeros_like(aim)
        for b in range(a + 1):
            for e in range(REFS):
                same = aim == entry(mine[parts[b]], e)
                if b == a:
                    same = same & (lane[:H] > e)
                depth += jnp.where(same, 1, 0)
        cell = jnp.where(aim >= 0, aim * DEEP + depth, -1)
        land = landing[parts[a]]
        for e in range(REFS):
            sources += jnp.where(entry(cell, e) == cells, entry(land, e) - B_ZERO, 0)
    return first, jnp.clip(sources, 0, B_SIZE - 1)


ORDER = (
    ("GS", 0), ("G", 0, 2, 0), ("G", 0, 2, 1), ("G", 0, 3, 0), ("G", 0, 3, 1), ("GS", 1),
    ("G", 0, 4, 0), ("G", 0, 4, 1), ("G", 1, 2, 0), ("G", 1, 2, 1), ("GE", 0), ("SR", 0),
    ("G", 1, 3, 0), ("G", 1, 3, 1), ("GS", 2), ("G", 1, 4, 0), ("SM", 0), ("G", 1, 4, 1),
    ("G", 2, 2, 0), ("G", 2, 2, 1), ("GE", 1), ("SR", 1), ("G", 2, 3, 0), ("G", 2, 3, 1),
    ("G", 2, 4, 0), ("SM", 1), ("G", 2, 4, 1), ("GS", 3), ("GE", 2), ("SR", 2), ("G", 3, 2, 0),
    ("C", 0, 0), ("G", 3, 2, 1), ("SM", 2), ("C", 0, 1), ("ST", 1), ("G", 3, 3, 0), ("ST", 0),
    ("G", 3, 3, 1), ("GS", 4), ("G", 3, 4, 0), ("G", 3, 4, 1), ("G", 4, 2, 0), ("G", 4, 2, 1),
    ("G", 4, 3, 0), ("RT", 1), ("RT", 0), ("GE", 3), ("G", 4, 3, 1), ("GS", 5), ("SR", 3),
    ("G", 4, 4, 0), ("G", 5, 2, 0), ("L", 1), ("G", 5, 2, 1), ("G", 4, 4, 1), ("L", 0),
    ("R", 1, 2), ("G", 5, 3, 0), ("SM", 3), ("R", 1, 5), ("G", 5, 3, 1), ("R", 0, 1), ("GS", 6),
    ("GE", 4), ("R", 1, 1), ("R", 0, 3), ("R", 1, 3), ("G", 5, 4, 0), ("SR", 4), ("G", 5, 4, 1),
    ("G", 6, 2, 0), ("SS", 1), ("GE", 5), ("G", 6, 2, 1), ("SR", 5), ("R", 0, 2), ("SS", 0),
    ("R", 0, 5), ("G", 6, 3, 0), ("C", 1, 0), ("G", 6, 3, 1), ("SM", 4), ("S", 1, 2, 0), ("GS", 7),
    ("SM", 5), ("C", 1, 1), ("S", 1, 2, 1), ("ST", 2), ("S", 1, 3, 0), ("G", 6, 4, 0),
    ("G", 7, 2, 0), ("S", 0, 2, 0), ("R", 0, 4), ("G", 7, 2, 1), ("S", 0, 2, 1), ("R", 1, 4),
    ("S", 1, 3, 1), ("RT", 2), ("G", 6, 4, 1), ("ST", 3), ("C", 2, 0), ("G", 7, 3, 0),
    ("G", 7, 3, 1), ("C", 2, 1), ("S", 1, 4, 0), ("S", 0, 3, 0), ("L", 2), ("S", 0, 3, 1),
    ("RT", 3), ("S", 1, 4, 1), ("ST", 5), ("S", 0, 4, 0), ("L", 3), ("R", 3, 1), ("R", 3, 5),
    ("SS", 3), ("G", 7, 4, 0), ("F", 1), ("R", 2, 4), ("R", 2, 2), ("RT", 5), ("S", 0, 4, 1),
    ("R", 3, 2), ("R", 2, 1), ("S", 3, 2, 0), ("S", 3, 2, 1), ("R", 3, 4), ("R", 3, 3), ("GE", 6),
    ("G", 7, 4, 1), ("R", 2, 3), ("SR", 6), ("S", 3, 3, 0), ("S", 3, 3, 1), ("SS", 2), ("L", 5),
    ("SM", 6), ("GE", 7), ("S", 3, 4, 0), ("R", 5, 2), ("SR", 7), ("R", 5, 5), ("R", 2, 5),
    ("S", 3, 4, 1), ("R", 5, 1), ("F", 0), ("SS", 5), ("S", 2, 2, 0), ("S", 2, 2, 1), ("F", 3),
    ("S", 5, 2, 0), ("SM", 7), ("S", 2, 3, 0), ("R", 5, 4), ("ST", 4), ("R", 5, 3), ("S", 5, 2, 1),
    ("S", 2, 3, 1), ("S", 5, 3, 0), ("S", 2, 4, 0), ("C", 3, 0), ("S", 5, 3, 1), ("RT", 4),
    ("S", 2, 4, 1), ("C", 3, 1), ("ST", 7), ("S", 5, 4, 0), ("L", 4), ("R", 4, 1), ("SS", 4),
    ("F", 2), ("R", 4, 2), ("S", 5, 4, 1), ("S", 4, 2, 0), ("R", 4, 4), ("S", 4, 2, 1), ("RT", 7),
    ("R", 4, 3), ("S", 4, 3, 0), ("ST", 6), ("S", 4, 3, 1), ("R", 4, 5), ("L", 7), ("R", 7, 1),
    ("SS", 7), ("F", 5), ("S", 4, 4, 0), ("R", 7, 2), ("R", 7, 3), ("RT", 6), ("S", 7, 2, 0),
    ("S", 4, 4, 1), ("R", 7, 4), ("S", 7, 2, 1), ("S", 7, 3, 0), ("L", 6), ("R", 6, 1), ("SS", 6),
    ("S", 7, 3, 1), ("R", 6, 3), ("S", 7, 4, 0), ("R", 6, 2), ("R", 6, 5), ("F", 4),
    ("S", 6, 2, 0), ("S", 6, 2, 1), ("R", 6, 4), ("S", 7, 4, 1), ("S", 6, 3, 0), ("S", 6, 3, 1),
    ("S", 6, 4, 0), ("R", 7, 5), ("S", 6, 4, 1), ("F", 7), ("F", 6),
)


def kernel(
    kv,
    query,
    grad,
    links,
    out_o,
    out_q,
    out_k,
    out_v,
    table,
    relay_out,
    relay_in,
    merged_out,
    received,
    terms_in,
    terms_relay,
    sums_r,
    sums_l,
    near,
    anchor_acc,
    anchor_in,
    part_out,
    part_in,
    edge_out,
    edge_in,
    edge_part_out,
    edge_part_in,
    anchor_kv,
    wide,
    terms,
    ag_sent,
    ag_sem,
    rs_sent,
    rs_sem,
    x_sem,
    anchor_sem,
    part_sem,
    edge_sem,
    slot_v,
    source_v,
    slot_t,
    source_t,
    table_sem,
):
    ctx = lax.axis_index("ctx")
    x, z = ctx // NZ, ctx % NZ
    z_r = x * NZ + lax.rem(z + 1, NZ)
    z_l = x * NZ + lax.rem(z + NZ - 1, NZ)
    p_r = lax.rem(x + 1, NX)
    p_l = lax.rem(x + NX - 1, NX)
    p_o = lax.rem(x + 2, NX)
    x_r = p_r * NZ + z
    x_l = p_l * NZ + z
    outer = (x == 0) | (x == NX - 1)
    inner = (x == 1) | (x == NX - 2)
    rim = (z == 0) | (z == NZ - 1)
    beyond = lax.rem(jnp.where(z == 0, ctx + NX * NZ - 1, ctx + 1), NX * NZ)

    def to(device, src, dst, sent, came=None):
        return pltpu.make_async_remote_copy(
            src_ref=src,
            dst_ref=dst,
            send_sem=sent if came is not None else sent.at[0],
            recv_sem=came if came is not None else sent.at[1],
            device_id={"ctx": device},
            device_id_type=MESH,
        )

    barrier = pltpu.get_barrier_semaphore()

    def place_own(u):
        @pl.loop(0, BPD)
        def _(b):
            table[u][z * BPD + b] = kv[u, b]

    def greet(device):
        pl.semaphore_signal(barrier, inc=1, device_id={"ctx": device}, device_id_type=MESH)

    for device in (z_r, z_l, x_r, x_l):
        greet(device)

    for u in range(UNITS):
        place_own(u)

    @pl.when(rim)
    def _():
        @pl.loop(0, UNITS)
        def _(u):
            edge_out[u] = kv[u, jnp.where(z == 0, 0, BPD - 1)]

    pl.semaphore_wait(barrier, 4)

    def gather_copy(u, s, half, right):
        row = lax.rem(z + NZ - (s - 1), NZ) if right else lax.rem(z + s - 1, NZ)
        cut = pl.ds(row * BPD + half * HALF, HALF)
        src = kv.at[u, pl.ds(half * HALF, HALF)] if s == 1 else table[u].at[cut]
        way = 0 if right else 1
        came = ag_sem.at[u % 2, s - 1, half, way]
        return to(z_r if right else z_l, src, table[u].at[cut], ag_sent.at[u], came)

    def moves(s):
        return [
            (half, right)
            for half in (0, 1)
            for right in (True, False)
            if s < 4 or right == (half == 0)
        ]

    def gather_start(u):
        for half, right in moves(1):
            gather_copy(u, 1, half, right).start()

    def gather_step(u, s, half):
        for right in (True, False):
            gather_copy(u, s - 1, half, right).wait_recv()
            if (half, right) in moves(s):
                gather_copy(u, s, half, right).start()

    def gather_end(u):
        for half, right in moves(4):
            gather_copy(u, 4, half, right).wait_recv()

    def all_sent(u, sent):
        whole = table[u].at[pl.ds(0, 14 * HALF)]
        to(z_r, whole, whole, sent.at[u], ag_sem.at[0, 0, 0, 0]).wait_send()

    def gather_sent(u):
        all_sent(u, ag_sent)

    def edge_copy():
        return to(beyond, edge_out, edge_in, edge_sem.at[UNITS])

    def send_edges():
        @pl.when(rim)
        def _():
            edge_copy().start()

    def relay_copy(u, side):
        return to(
            (x_r, x_l)[side], relay_out[u].at[side], relay_in[u].at[1 - side], x_sem.at[0, u, side]
        )

    def part_of(start, part):
        return pl.ds(start + part * RELAY, RELAY)

    def merged_copy(u, side, part):
        return to(
            (x_r, x_l)[side],
            merged_out[u].at[side, part_of(0, part)],
            received[u].at[part_of((FROM_L, FROM_R)[side], part)],
            x_sem.at[(4, 1)[part], u, side],
        )

    def anchor_copy(u, side):
        return to(
            (x_r, x_l)[side],
            table[u].at[jnp.where(x == 0, 0, TARGETS - 1)],
            anchor_in.at[u, 0],
            anchor_sem.at[u, side],
        )

    def anchor_arrived(u):
        @pl.when((x == 0) | (x == 1))
        def _():
            anchor_copy(u, 0).wait_recv()

        @pl.when((x == 2) | (x == 3))
        def _():
            anchor_copy(u, 1).wait_recv()

    def anchor_pass(u):
        return to(
            jnp.where(x == 1, x_r, x_l), anchor_in.at[u, 0], anchor_in.at[u, 1], anchor_sem.at[u, 2]
        )

    def send_relays(u):
        h = u // 2

        @pl.when(outer)
        def _():
            for side in (0, 1):
                anchor_copy(u, side).start()

        @pl.loop(0, RELAY)
        def _(k):
            relay_out[u][0, k] = table[u][slot_t[p_o * H + h, T_RELAY + RELAY + k]]
            relay_out[u][1, k] = table[u][slot_t[p_o * H + h, T_RELAY + k]]

        for side in (0, 1):
            relay_copy(u, side).start()

        @pl.loop(0, RELAY)
        def _(k):
            for side, plane, first in ((0, p_r, FROM_L), (1, p_l, FROM_R)):
                code = slot_t[plane * H + h, first + k]
                merged_out[u][side, k] = table[u][jnp.minimum(code, TARGETS - 1)]

        for side in (0, 1):
            merged_copy(u, side, 0).start()

        @pl.loop(0, MAIN)
        def _(k):
            received[u][OWN + k] = table[u][slot_t[x * H + h, OWN + k]]

    def send_merged(u):
        h = u // 2
        for side in (0, 1):
            relay_copy(u, side).wait_recv()

        @pl.loop(0, RELAY)
        def _(k):
            spot = MAIN - 1 - k
            for side, plane, first, back in ((0, p_r, FROM_L, 1), (1, p_l, FROM_R, 0)):
                code = slot_t[plane * H + h, first + spot]
                direct = table[u][jnp.minimum(code, TARGETS - 1)]
                merged_out[u][side, spot] = jnp.where(
                    code < TARGETS, direct, relay_in[u][back, k]
                )

        for side in (0, 1):
            merged_copy(u, side, 1).start()
        anchor_arrived(u)

        @pl.when(inner)
        def _():
            anchor_pass(u).start()

        if u == 0:
            send_edges()

    def lay_keys(h):
        for p in (0, 1):
            u = 2 * h + p
            for side in (0, 1):
                for part in (0, 1):
                    merged_copy(u, side, part).wait_recv()

            @pl.when(inner)
            def _():
                anchor_pass(u).wait_recv()

            row_above = lax.rem(z + NZ - 1, NZ) * BPD + BPD - 1
            row_below = lax.rem(z + 1, NZ) * BPD
            wide[p, 0:BLOCK] = jnp.where(z > 0, table[u][row_above], edge_in[u])
            wide[p, BLOCK * (BPD + 1) :] = jnp.where(z < NZ - 1, table[u][row_below], edge_in[u])
            for b in range(BPD):
                wide[p, BLOCK * (b + 1) : BLOCK * (b + 2)] = kv[u, b]
            came, passed = anchor_in[u, 0], anchor_in[u, 1]
            anchor_kv[p, :BLOCK] = jnp.where(x == 0, table[u][0], jnp.where(x == 2, passed, came))
            anchor_kv[p, BLOCK:] = jnp.where(
                x == 3, table[u][TARGETS - 1], jnp.where(x == 1, passed, came)
            )
        near[h][...] = jnp.zeros_like(near[h])
        anchor_acc[h][...] = jnp.zeros_like(anchor_acc[h])

    def compute(h, piece):
        if piece == 0:
            if h == 0:

                @pl.when(rim)
                def _():
                    edge_copy().wait_recv()

            lay_keys(h)
        column = lax.broadcasted_iota(jnp.int32, (1, 8 * BLOCK), 1)

        @pl.loop(piece * BPD // PIECES, (piece + 1) * BPD // PIECES)
        def _(i):
            rows = pl.ds(pl.multiple_of(i * BLOCK, BLOCK), 3 * BLOCK)
            spots = [slot_t[x * H + h, T_PLACE + i * R + r] for r in range(R)]
            keys, values = (
                jnp.concatenate(
                    [wide[p, rows], anchor_kv[p]] + [received[2 * h + p][s] for s in spots], axis=0
                )
                for p in (0, 1)
            )
            q, g = query[h, i], grad[h, i]
            block = ctx * BPD + i
            low = jnp.where(block == 0, BLOCK, 0)
            cut = jnp.where(block == NX * NZ * BPD - 1, 2 * BLOCK, 3 * BLOCK)
            masked = (column < low) | ((column >= cut) & (column < 3 * BLOCK))
            contract_last = (((1,), (1,)), ((), ()))
            contract_first = (((0,), (0,)), ((), ()))
            scores = lax.dot_general(q, keys, contract_last, preferred_element_type=F32) * SCALE
            scores = jnp.where(masked, -1e30, scores)
            powers = jnp.exp(scores - jnp.max(scores, axis=-1, keepdims=True))
            probs = powers * (1.0 / jnp.sum(powers, axis=-1, keepdims=True))
            low_probs = probs.astype(BF16)
            attended = jnp.dot(low_probs, values, preferred_element_type=F32).astype(BF16)
            out_o[h, i] = attended
            delta = jnp.sum(g.astype(F32) * attended.astype(F32), axis=-1, keepdims=True)
            grad_probs = lax.dot_general(g, values, contract_last, preferred_element_type=F32)
            grad_scores = (probs * (grad_probs - delta)).astype(BF16)
            out_q[h, i] = (
                jnp.dot(grad_scores, keys, preferred_element_type=F32) * SCALE
            ).astype(BF16)
            key_part = (
                lax.dot_general(grad_scores, q, contract_first, preferred_element_type=F32) * SCALE
            )
            value_part = lax.dot_general(
                low_probs, g, contract_first, preferred_element_type=F32
            )
            for p, part in ((0, key_part), (1, value_part)):
                near[h][p, rows] += part[: 3 * BLOCK]
                anchor_acc[h][p] += part[3 * BLOCK : 5 * BLOCK]
                for r in range(R):
                    terms[p, i * R + r] = part[(5 + r) * BLOCK : (6 + r) * BLOCK].astype(BF16)

    def terms_copy(u, side, part):
        return to(
            (x_r, x_l)[side],
            merged_out[u].at[side, part_of(0, part)],
            terms_in[u].at[part_of((FROM_L, FROM_R)[side], part)],
            x_sem.at[(5, 2)[part], u, side],
        )

    def terms_relay_copy(u, side):
        return to(
            (x_r, x_l)[side], relay_out[u].at[side], terms_relay[u].at[1 - side],
            x_sem.at[3, u, side],
        )

    def part_first(u):
        return to(
            jnp.where(x == 1, x_r, x_l), part_out.at[u, 0], part_in.at[u, 0], part_sem.at[u, 0]
        )

    def part_second(u, side):
        return to(
            (x_r, x_l)[side], part_out.at[u, 1], part_in.at[u, 1 + side], part_sem.at[u, 1 + side]
        )

    def leftward():
        return (x == 0) | (x == 1)

    def edge_part_copy(u):
        return to(beyond, edge_part_out.at[u], edge_part_in.at[u], edge_sem.at[u])

    def anchor(u, which):
        return anchor_acc[u // 2][u % 2, which * BLOCK : (which + 1) * BLOCK]

    def near_rows(u, b):
        return near[u // 2][u % 2, (b + 1) * BLOCK : (b + 2) * BLOCK]

    def send_terms(u):
        h, p = u // 2, u % 2
        for part in (1, 0):
            for side in (0, 1):
                merged_copy(u, side, part).wait_send()

            @pl.loop(part * RELAY, (part + 1) * RELAY)
            def _(k):
                merged_out[u][0, k] = terms[p, slot_t[x * H + h, T_GIVER + FROM_R + k]]
                merged_out[u][1, k] = terms[p, slot_t[x * H + h, T_GIVER + FROM_L + k]]

            for side in (0, 1):
                terms_copy(u, side, part).start()

        @pl.loop(0, MAIN)
        def _(k):
            terms_in[u][B_OWN + k] = terms[p, slot_t[x * H + h, T_GIVER + OWN + k]]

        terms_in[u][B_ZERO] = jnp.zeros((BLOCK, HD), BF16)

        @pl.when(inner)
        def _():
            part_out[u, 0] = jnp.where(x == 1, anchor(u, 1), anchor(u, 0)).astype(BF16)
            part_first(u).start()

        @pl.when(rim)
        def _():
            edge_part_out[u] = jnp.where(z == 0, near_rows(u, -1), near_rows(u, BPD)).astype(BF16)
            edge_part_copy(u).start()

    def relay_terms(u):
        for side in (0, 1):
            relay_copy(u, side).wait_send()
            terms_copy(u, side, 1).wait_recv()

        @pl.loop(0, RELAY)
        def _(k):
            relay_out[u][0, k] = terms_in[u][FROM_L + MAIN - 1 - k]
            relay_out[u][1, k] = terms_in[u][FROM_R + MAIN - 1 - k]

        for side in (0, 1):
            terms_relay_copy(u, side).start()

        @pl.when(inner)
        def _():
            part_first(u).wait_recv()
            mine = jnp.where(x == 1, anchor(u, 0), anchor(u, 1))
            part_out[u, 1] = (mine + part_in[u, 0].astype(F32)).astype(BF16)

        @pl.when(outer)
        def _():
            part_out[u, 1] = jnp.where(x == 0, anchor(u, 1), anchor(u, 0)).astype(BF16)

        @pl.when(leftward())
        def _():
            part_second(u, 1).start()

        @pl.when(jnp.logical_not(leftward()))
        def _():
            part_second(u, 0).start()

    def land(u):
        gather_sent(u)

        @pl.when(outer)
        def _():
            for side in (0, 1):
                anchor_copy(u, side).wait_send()
                part_second(u, side).wait_recv()

        for side in (0, 1):
            terms_copy(u, side, 0).wait_recv()
            terms_relay_copy(u, side).wait_recv()

        @pl.loop(0, RELAY)
        def _(k):
            terms_in[u][B_RR + k] = terms_relay[u][0, k]
            terms_in[u][B_RL + k] = terms_relay[u][1, k]

    def rows(u, group):
        h = u // 2
        for away in {1: (4,), 2: (3, 5), 3: (2, 6), 4: (1, 7), 5: (0,)}[group]:
            row = lax.rem(z + away, NZ)

            @pl.loop(0, BPD)
            def _(b):
                t = row * BPD + b
                total = terms_in[u][source_t[h, t * DEEP]].astype(F32)
                for k in range(1, DEEP):
                    total += terms_in[u][source_t[h, t * DEEP + k]].astype(F32)
                table[u][t] = total.astype(BF16)

            def add(t, part):
                table[u][t] = (table[u][t].astype(F32) + part).astype(BF16)

            def both():
                return part_in[u, 1].astype(F32) + part_in[u, 2].astype(F32)

            @pl.when((x == 0) & (row == 0))
            def _():
                add(0, anchor(u, 0) + both())

            @pl.when((x == NX - 1) & (row == NZ - 1))
            def _():
                add(TARGETS - 1, anchor(u, 1) + both())

            if away == NZ - 1:

                @pl.when(z > 0)
                def _():
                    add(row * BPD + BPD - 1, near_rows(u, -1))

            if away == 1:

                @pl.when(z < NZ - 1)
                def _():
                    add(row * BPD, near_rows(u, BPD))

    def sum_copy(u, s, half, right):
        row = lax.rem(z + 5 - s, NZ) if right else lax.rem(z + NZ - 5 + s, NZ)
        way = 0 if right else 1
        return to(
            z_r if right else z_l,
            table[u].at[pl.ds(row * BPD + half * HALF, HALF)],
            (sums_r if right else sums_l)[u].at[s - 1, pl.ds(half * HALF, HALF)],
            rs_sent.at[u],
            rs_sem.at[u % 2, s - 1, half, way],
        )

    def sum_moves(s):
        return moves(4 if s == 1 else 1)

    def sum_start(u):
        for half, right in sum_moves(1):
            sum_copy(u, 1, half, right).start()

    def sum_step(u, s, half):
        for right in (True, False):
            if (half, right) in sum_moves(s - 1):
                sum_copy(u, s - 1, half, right).wait_recv()
                row = lax.rem(z + 5 - s, NZ) if right else lax.rem(z + NZ - 5 + s, NZ)
                came = (sums_r if right else sums_l)[u]

                @pl.loop(0, HALF)
                def _(b):
                    here = row * BPD + half * HALF + b
                    table[u][here] = (
                        table[u][here].astype(F32) + came[s - 2, half * HALF + b].astype(F32)
                    ).astype(BF16)

            sum_copy(u, s, half, right).start()

    def finish(u):
        h, p = u // 2, u % 2
        for half, right in sum_moves(4):
            sum_copy(u, 4, half, right).wait_recv()

        @pl.when(rim)
        def _():
            edge_part_copy(u).wait_recv()
            lone = pl.ds(pl.multiple_of(jnp.where(z == 0, 1, BPD) * BLOCK, BLOCK), BLOCK)
            near[h][p, lone] += edge_part_in[u].astype(F32)

        @pl.loop(0, BPD)
        def _(b):
            total = (
                table[u][z * BPD + b].astype(F32)
                + sums_r[u][3, b].astype(F32)
                + sums_l[u][3, b].astype(F32)
                + near[h][p, pl.ds(pl.multiple_of((b + 1) * BLOCK, BLOCK), BLOCK)]
            )
            (out_k, out_v)[p][h, b] = total.astype(BF16)

    def drain(u):
        all_sent(u, rs_sent)
        for side in (0, 1):
            for part in (0, 1):
                terms_copy(u, side, part).wait_send()
            terms_relay_copy(u, side).wait_send()

        @pl.when(inner)
        def _():
            anchor_pass(u).wait_send()
            part_first(u).wait_send()

        @pl.when(leftward())
        def _():
            part_second(u, 1).wait_send()

        @pl.when(jnp.logical_not(leftward()))
        def _():
            part_second(u, 0).wait_send()

        @pl.when(rim)
        def _():
            edge_part_copy(u).wait_send()

    steps = {
        "GS": gather_start,
        "G": gather_step,
        "GE": gather_end,
        "SR": send_relays,
        "SM": send_merged,
        "C": compute,
        "ST": send_terms,
        "RT": relay_terms,
        "L": land,
        "R": rows,
        "SS": sum_start,
        "S": sum_step,
        "F": finish,
    }
    first_name, *first_where = ORDER[0]
    steps[first_name](*first_where)
    slot_v[...], source_v[...] = slot_tables(links[...], x)
    copies = (
        pltpu.make_async_copy(slot_v, slot_t, table_sem.at[0]),
        pltpu.make_async_copy(source_v, source_t, table_sem.at[1]),
    )
    for copy in copies:
        copy.start()
    for copy in copies:
        copy.wait()
    for name, *where in ORDER[1:]:
        steps[name](*where)
    for u in range(UNITS):
        drain(u)

    @pl.when(rim)
    def _():
        edge_copy().wait_send()


def local(query, key, value, out_grad, random_links):
    def head_major(array):
        return array.reshape(BPD, BLOCK, H, HD).transpose(2, 0, 1, 3)

    def seq_major(array):
        return array.transpose(1, 2, 0, 3).reshape(BPD * BLOCK, H, HD)

    kv = jnp.stack((head_major(key), head_major(value)), axis=1).reshape(UNITS, BPD, BLOCK, HD)
    block = (BLOCK, HD)

    def per(count, *shape, dtype=BF16):
        return [pltpu.VMEM(shape, dtype) for _ in range(count)]

    dma = pltpu.SemaphoreType.DMA
    vmem = pl.BlockSpec(memory_space=pltpu.VMEM)
    outs = pl.pallas_call(
        kernel,
        out_shape=[jax.ShapeDtypeStruct((H, BPD, BLOCK, HD), BF16)] * 4,
        in_specs=[vmem] * 4,
        out_specs=[vmem] * 4,
        scratch_shapes=[
            per(UNITS, TARGETS, *block),
            per(UNITS, 2, RELAY, *block),
            per(UNITS, 2, RELAY, *block),
            per(UNITS, 2, MAIN, *block),
            per(UNITS, RECEIVED, *block),
            per(UNITS, B_SIZE, *block),
            per(UNITS, 2, RELAY, *block),
            per(UNITS, 4, BPD, *block),
            per(UNITS, 4, BPD, *block),
            per(H, 2, (BPD + 2) * BLOCK, HD, dtype=F32),
            per(H, 2, 2 * BLOCK, HD, dtype=F32),
            pltpu.VMEM((UNITS, 2, *block), BF16),
            pltpu.VMEM((UNITS, 2, *block), BF16),
            pltpu.VMEM((UNITS, 3, *block), BF16),
            pltpu.VMEM((UNITS, *block), BF16),
            pltpu.VMEM((UNITS, *block), BF16),
            pltpu.VMEM((UNITS, *block), BF16),
            pltpu.VMEM((UNITS, *block), BF16),
            pltpu.VMEM((2, 2 * BLOCK, HD), BF16),
            pltpu.VMEM((2, (BPD + 2) * BLOCK, HD), BF16),
            pltpu.VMEM((2, REFS, *block), BF16),
            dma((UNITS,)),
            dma((2, 4, 2, 2)),
            dma((UNITS,)),
            dma((2, 4, 2, 2)),
            dma((6, UNITS, 2, 2)),
            dma((UNITS, 3, 2)),
            dma((UNITS, 3, 2)),
            dma((UNITS + 1, 2)),
            pltpu.VMEM((NX * H, T_WIDTH), jnp.int32),
            pltpu.VMEM((H, TARGETS * DEEP), jnp.int32),
            pltpu.SMEM((NX * H, T_WIDTH), jnp.int32),
            pltpu.SMEM((H, TARGETS * DEEP), jnp.int32),
            dma((2,)),
        ],
        compiler_params=pltpu.CompilerParams(
            collective_id=0, has_side_effects=True, vmem_limit_bytes=60 * 2**20
        ),
        cost_estimate=pl.CostEstimate(
            flops=2 * 6 * BLOCK * 8 * BLOCK * HD * H * BPD,
            bytes_accessed=4 * 2**20,
            transcendentals=H * BPD * BLOCK * 8 * BLOCK,
        ),
    )(kv, head_major(query), head_major(out_grad), named_blocks(random_links))
    return tuple(seq_major(array) for array in outs)


def solution(mesh):
    split = P("ctx", "head", None)
    return jax.shard_map(
        local,
        mesh=mesh,
        in_specs=(split, split, split, split, P(None, "head", None)),
        out_specs=(split, split, split, split),
        check_vma=False,
    )
```

```python
import math

import jax
import jax.numpy as jnp
from jax import lax
from jax.experimental import pallas as pl
from jax.experimental.pallas import tpu as pltpu
from jax.sharding import PartitionSpec as P

BLOCK = 64
HD = 128
NX = 4
NZ = 8
BPD = 8
HALF = BPD // 2
H = 4
R = 3
REFS = BPD * R
TARGETS = NZ * BPD
MAIN = 16
RELAY = 8
UNITS = 2 * H
FROM_R, FROM_L, OWN = 0, MAIN, 2 * MAIN
RECEIVED = OWN + MAIN
B_RR = 2 * MAIN
B_RL = B_RR + RELAY
B_OWN = B_RL + RELAY
B_ZERO = B_OWN + MAIN
B_SIZE = B_ZERO + 1
T_RELAY = RECEIVED
T_GIVER = T_RELAY + 2 * RELAY
T_PLACE = T_GIVER + RECEIVED
T_WIDTH = 256
PIECES = 2
DEEP = 8
F32 = jnp.float32
BF16 = jnp.bfloat16
MESH = pl.DeviceIdType.MESH
SCALE = 1.0 / math.sqrt(HD)


def named_blocks(links):
    z = lax.axis_index("ctx") % NZ
    row = lax.dynamic_slice_in_dim(links.reshape(NX, NZ, BPD, H, R), z, 1, 1)[:, 0]
    return row.transpose(0, 2, 1, 3).reshape(NX * H, REFS)


def slot_tables(named, x):
    plane = lax.broadcasted_iota(jnp.int32, named.shape, 0) // H
    lane = lax.broadcasted_iota(jnp.int32, named.shape, 1)
    away = ((named >> 6) - plane) & (NX - 1)
    target = named & (TARGETS - 1)

    def entry(array, e):
        return array[:, e : e + 1]

    rank = jnp.zeros_like(named)
    n_r, n_o = (jnp.zeros((NX * H, 1), jnp.int32) for _ in range(2))
    for e in range(REFS):
        way = entry(away, e)
        rank += jnp.where((away == way) & (lane > e), 1, 0)
        n_r += jnp.where(way == 1, 1, 0)
        n_o += jnp.where(way == 2, 1, 0)
    by_right = jnp.minimum(n_o, jnp.minimum(RELAY, MAIN - n_r))
    right_way = rank < by_right
    relay_rank = jnp.where(right_way, rank, rank - by_right)
    opposite = jnp.where(right_way, FROM_R, FROM_L) + MAIN - 1 - relay_rank
    place = jnp.where(
        away == 0,
        OWN + rank,
        jnp.where(away == 1, FROM_R + rank, jnp.where(away == 3, FROM_L + rank, opposite)),
    )
    code = jnp.where(away == 2, TARGETS + relay_rank, target)
    relay_place = jnp.where(
        away == 2, T_RELAY + relay_rank + jnp.where(right_way, 0, RELAY), -1
    )
    spots = lax.broadcasted_iota(jnp.int32, (NX * H, T_WIDTH), 1)
    first = jnp.zeros_like(spots)
    for e in range(REFS):
        here = entry(place, e)
        at = jnp.where(
            spots < T_RELAY,
            here,
            jnp.where(
                spots < T_GIVER,
                entry(relay_place, e),
                jnp.where(spots < T_PLACE, T_GIVER + here, T_PLACE + e),
            ),
        )
        put = jnp.where(
            spots < T_RELAY,
            entry(code, e),
            jnp.where(
                spots < T_GIVER, entry(target, e), jnp.where(spots < T_PLACE, e, here)
            ),
        )
        first += jnp.where(at == spots, put, 0)
    most = jnp.where(
        spots < T_RELAY,
        TARGETS + RELAY - 1,
        jnp.where(
            spots < T_GIVER,
            TARGETS - 1,
            jnp.where(spots < T_PLACE, REFS - 1, RECEIVED - 1),
        ),
    )
    first = jnp.clip(first, 0, most)
    landing = jnp.where(
        away == 0,
        B_OWN + rank,
        jnp.where(
            away == 1,
            FROM_L + rank,
            jnp.where(
                away == 3, FROM_R + rank, jnp.where(right_way, B_RL, B_RR) + relay_rank
            ),
        ),
    )
    mine = jnp.where((named >> 6) == x, target, -1)
    cells = lax.broadcasted_iota(jnp.int32, (H, TARGETS * DEEP), 1)
    sources = jnp.full((H, TARGETS * DEEP), B_ZERO, jnp.int32)
    parts = [slice(a * H, (a + 1) * H) for a in range(NX)]
    for a in range(NX):
        aim = mine[parts[a]]
        depth = jnp.zeros_like(aim)
        for b in range(a + 1):
            for e in range(REFS):
                same = aim == entry(mine[parts[b]], e)
                if b == a:
                    same = same & (lane[:H] > e)
                depth += jnp.where(same, 1, 0)
        cell = jnp.where(aim >= 0, aim * DEEP + depth, -1)
        land = landing[parts[a]]
        for e in range(REFS):
            sources += jnp.where(entry(cell, e) == cells, entry(land, e) - B_ZERO, 0)
    return first, jnp.clip(sources, 0, B_SIZE - 1)


ORDER = (
    ("GS", 0), ("G", 0, 2, 0), ("G", 0, 2, 1), ("G", 0, 3, 0), ("G", 0, 3, 1), ("GS", 1),
    ("G", 0, 4, 0), ("G", 0, 4, 1), ("G", 1, 2, 0), ("G", 1, 2, 1), ("GE", 0), ("SR", 0),
    ("G", 1, 3, 0), ("G", 1, 3, 1), ("GS", 2), ("SM", 0), ("G", 1, 4, 0), ("G", 1, 4, 1),
    ("G", 2, 2, 0), ("G", 2, 2, 1), ("GE", 1), ("SR", 1), ("G", 2, 3, 0), ("G", 2, 3, 1),
    ("G", 2, 4, 0), ("SM", 1), ("G", 2, 4, 1), ("GS", 3), ("GE", 2), ("SR", 2), ("G", 3, 2, 0),
    ("C", 0, 0), ("G", 3, 2, 1), ("G", 3, 3, 0), ("SM", 2), ("C", 0, 1), ("ST", 0), ("G", 3, 3, 1),
    ("GS", 4), ("G", 3, 4, 0), ("ST", 1), ("G", 4, 2, 0), ("G", 4, 2, 1), ("G", 3, 4, 1),
    ("G", 4, 3, 0), ("G", 4, 3, 1), ("GS", 5), ("GE", 3), ("SR", 3), ("G", 5, 2, 0),
    ("G", 5, 2, 1), ("SM", 3), ("G", 4, 4, 0), ("RT", 1), ("G", 4, 4, 1), ("G", 5, 3, 0),
    ("G", 5, 3, 1), ("GS", 6), ("RT", 0), ("GE", 4), ("SR", 4), ("C", 1, 0), ("L", 1),
    ("G", 5, 4, 0), ("R", 1, 1), ("G", 6, 2, 0), ("G", 5, 4, 1), ("SS", 1), ("R", 1, 5),
    ("R", 1, 2), ("C", 1, 1), ("L", 0), ("G", 6, 2, 1), ("ST", 3), ("GE", 5), ("R", 0, 1),
    ("ST", 2), ("SS", 0), ("G", 6, 3, 0), ("G", 6, 3, 1), ("S", 1, 2, 0), ("SR", 5),
    ("G", 6, 4, 0), ("GS", 7), ("R", 0, 2), ("S", 1, 2, 1), ("G", 7, 2, 0), ("G", 6, 4, 1),
    ("S", 0, 2, 0), ("G", 7, 2, 1), ("G", 7, 3, 0), ("S", 0, 2, 1), ("RT", 2), ("R", 0, 5),
    ("R", 0, 3), ("G", 7, 3, 1), ("S", 0, 3, 0), ("R", 0, 4), ("RT", 3), ("R", 1, 3),
    ("S", 0, 3, 1), ("GE", 6), ("S", 1, 3, 0), ("SM", 5), ("SM", 4), ("S", 1, 3, 1), ("L", 2),
    ("L", 3), ("R", 3, 1), ("G", 7, 4, 0), ("R", 3, 2), ("R", 1, 4), ("SR", 6), ("G", 7, 4, 1),
    ("R", 2, 3), ("S", 0, 4, 0), ("R", 2, 2), ("S", 0, 4, 1), ("R", 2, 5), ("R", 2, 1),
    ("S", 1, 4, 0), ("SS", 2), ("GE", 7), ("SR", 7), ("S", 1, 4, 1), ("R", 3, 3), ("C", 2, 0),
    ("SS", 3), ("F", 0), ("S", 2, 2, 0), ("S", 2, 2, 1), ("C", 2, 1), ("ST", 4), ("R", 3, 4),
    ("F", 1), ("S", 2, 3, 0), ("S", 3, 2, 0), ("R", 2, 4), ("S", 3, 2, 1), ("S", 2, 3, 1),
    ("S", 3, 3, 0), ("RT", 4), ("S", 3, 3, 1), ("S", 2, 4, 0), ("SM", 6), ("S", 2, 4, 1),
    ("SM", 7), ("L", 4), ("R", 4, 1), ("SS", 4), ("R", 4, 2), ("S", 3, 4, 0), ("S", 3, 4, 1),
    ("F", 2), ("ST", 5), ("R", 4, 3), ("S", 4, 2, 0), ("S", 4, 2, 1), ("C", 3, 0), ("RT", 5),
    ("S", 4, 3, 0), ("C", 3, 1), ("ST", 6), ("S", 4, 3, 1), ("L", 5), ("R", 5, 1), ("SS", 5),
    ("R", 4, 4), ("R", 3, 5), ("S", 4, 4, 0), ("S", 4, 4, 1), ("F", 3), ("R", 5, 2), ("RT", 6),
    ("R", 4, 5), ("S", 5, 2, 0), ("S", 5, 2, 1), ("R", 5, 3), ("ST", 7), ("S", 5, 3, 0),
    ("S", 5, 3, 1), ("F", 4), ("L", 6), ("R", 6, 5), ("R", 5, 4), ("R", 6, 1), ("SS", 6),
    ("S", 5, 4, 0), ("RT", 7), ("R", 6, 3), ("R", 6, 2), ("S", 5, 4, 1), ("S", 6, 2, 0),
    ("S", 6, 2, 1), ("L", 7), ("R", 7, 1), ("SS", 7), ("R", 7, 3), ("S", 6, 3, 0), ("R", 6, 4),
    ("S", 6, 3, 1), ("R", 7, 2), ("R", 5, 5), ("F", 5), ("S", 7, 2, 0), ("S", 7, 2, 1),
    ("S", 6, 4, 0), ("S", 7, 3, 0), ("S", 7, 3, 1), ("R", 7, 4), ("S", 6, 4, 1), ("S", 7, 4, 0),
    ("S", 7, 4, 1), ("R", 7, 5), ("F", 6), ("F", 7),
)


def kernel(
    kv,
    query,
    grad,
    links,
    out_o,
    out_q,
    out_k,
    out_v,
    table,
    relay_out,
    relay_in,
    merged_out,
    received,
    terms_in,
    terms_relay,
    sums_r,
    sums_l,
    near,
    anchor_acc,
    anchor_in,
    part_out,
    part_in,
    edge_out,
    edge_in,
    edge_part_out,
    edge_part_in,
    anchor_kv,
    wide,
    terms,
    ag_sent,
    ag_sem,
    rs_sent,
    rs_sem,
    x_sem,
    anchor_sem,
    part_sem,
    edge_sem,
    slot_v,
    source_v,
    slot_t,
    source_t,
    table_sem,
):
    ctx = lax.axis_index("ctx")
    x, z = ctx // NZ, ctx % NZ
    z_r = x * NZ + lax.rem(z + 1, NZ)
    z_l = x * NZ + lax.rem(z + NZ - 1, NZ)
    p_r = lax.rem(x + 1, NX)
    p_l = lax.rem(x + NX - 1, NX)
    p_o = lax.rem(x + 2, NX)
    x_r = p_r * NZ + z
    x_l = p_l * NZ + z
    outer = (x == 0) | (x == NX - 1)
    inner = (x == 1) | (x == NX - 2)
    rim = (z == 0) | (z == NZ - 1)
    beyond = lax.rem(jnp.where(z == 0, ctx + NX * NZ - 1, ctx + 1), NX * NZ)

    def to(device, src, dst, sent, came=None):
        return pltpu.make_async_remote_copy(
            src_ref=src,
            dst_ref=dst,
            send_sem=sent if came is not None else sent.at[0],
            recv_sem=came if came is not None else sent.at[1],
            device_id={"ctx": device},
            device_id_type=MESH,
        )

    barrier = pltpu.get_barrier_semaphore()

    def place_own(u):
        @pl.loop(0, BPD)
        def _(b):
            table[u][z * BPD + b] = kv[u, b]

    def greet(device):
        pl.semaphore_signal(barrier, inc=1, device_id={"ctx": device}, device_id_type=MESH)

    for device in (z_r, z_l, x_r, x_l):
        greet(device)

    for u in range(UNITS):
        place_own(u)

    @pl.when(rim)
    def _():
        @pl.loop(0, UNITS)
        def _(u):
            edge_out[u] = kv[u, jnp.where(z == 0, 0, BPD - 1)]

    pl.semaphore_wait(barrier, 4)

    def gather_copy(u, s, half, right):
        row = lax.rem(z + NZ - (s - 1), NZ) if right else lax.rem(z + s - 1, NZ)
        cut = pl.ds(row * BPD + half * HALF, HALF)
        src = kv.at[u, pl.ds(half * HALF, HALF)] if s == 1 else table[u].at[cut]
        way = 0 if right else 1
        came = ag_sem.at[u % 2, s - 1, half, way]
        return to(z_r if right else z_l, src, table[u].at[cut], ag_sent.at[u], came)

    def moves(s):
        return [
            (half, right)
            for half in (0, 1)
            for right in (True, False)
            if s < 4 or right == (half == 0)
        ]

    def gather_start(u):
        for half, right in moves(1):
            gather_copy(u, 1, half, right).start()

    def gather_step(u, s, half):
        for right in (True, False):
            gather_copy(u, s - 1, half, right).wait_recv()
            if (half, right) in moves(s):
                gather_copy(u, s, half, right).start()

    def gather_end(u):
        for half, right in moves(4):
            gather_copy(u, 4, half, right).wait_recv()

    def all_sent(u, sent):
        whole = table[u].at[pl.ds(0, 14 * HALF)]
        to(z_r, whole, whole, sent.at[u], ag_sem.at[0, 0, 0, 0]).wait_send()

    def gather_sent(u):
        all_sent(u, ag_sent)

    def edge_copy():
        return to(beyond, edge_out, edge_in, edge_sem.at[UNITS])

    def send_edges():
        @pl.when(rim)
        def _():
            edge_copy().start()

    def relay_copy(u, side):
        return to(
            (x_r, x_l)[side], relay_out[u].at[side], relay_in[u].at[1 - side], x_sem.at[0, u, side]
        )

    def part_of(start, part):
        return pl.ds(start + part * RELAY, RELAY)

    def merged_copy(u, side, part):
        return to(
            (x_r, x_l)[side],
            merged_out[u].at[side, part_of(0, part)],
            received[u].at[part_of((FROM_L, FROM_R)[side], part)],
            x_sem.at[(4, 1)[part], u, side],
        )

    def anchor_copy(u, side):
        return to(
            (x_r, x_l)[side],
            table[u].at[jnp.where(x == 0, 0, TARGETS - 1)],
            anchor_in.at[u, 0],
            anchor_sem.at[u, side],
        )

    def anchor_arrived(u):
        @pl.when((x == 0) | (x == 1))
        def _():
            anchor_copy(u, 0).wait_recv()

        @pl.when((x == 2) | (x == 3))
        def _():
            anchor_copy(u, 1).wait_recv()

    def anchor_pass(u):
        return to(
            jnp.where(x == 1, x_r, x_l), anchor_in.at[u, 0], anchor_in.at[u, 1], anchor_sem.at[u, 2]
        )

    def send_relays(u):
        h = u // 2

        @pl.when(outer)
        def _():
            for side in (0, 1):
                anchor_copy(u, side).start()

        @pl.loop(0, RELAY)
        def _(k):
            relay_out[u][0, k] = table[u][slot_t[p_o * H + h, T_RELAY + RELAY + k]]
            relay_out[u][1, k] = table[u][slot_t[p_o * H + h, T_RELAY + k]]

        for side in (0, 1):
            relay_copy(u, side).start()

        @pl.loop(0, RELAY)
        def _(k):
            for side, plane, first in ((0, p_r, FROM_L), (1, p_l, FROM_R)):
                code = slot_t[plane * H + h, first + k]
                merged_out[u][side, k] = table[u][jnp.minimum(code, TARGETS - 1)]

        for side in (0, 1):
            merged_copy(u, side, 0).start()

        @pl.loop(0, MAIN)
        def _(k):
            received[u][OWN + k] = table[u][slot_t[x * H + h, OWN + k]]

    def send_merged(u):
        h = u // 2
        for side in (0, 1):
            relay_copy(u, side).wait_recv()

        @pl.loop(0, RELAY)
        def _(k):
            spot = MAIN - 1 - k
            for side, plane, first, back in ((0, p_r, FROM_L, 1), (1, p_l, FROM_R, 0)):
                code = slot_t[plane * H + h, first + spot]
                direct = table[u][jnp.minimum(code, TARGETS - 1)]
                merged_out[u][side, spot] = jnp.where(
                    code < TARGETS, direct, relay_in[u][back, k]
                )

        for side in (0, 1):
            merged_copy(u, side, 1).start()
        anchor_arrived(u)

        @pl.when(inner)
        def _():
            anchor_pass(u).start()

        if u == 0:
            send_edges()

    def lay_keys(h):
        for p in (0, 1):
            u = 2 * h + p
            for side in (0, 1):
                for part in (0, 1):
                    merged_copy(u, side, part).wait_recv()

            @pl.when(inner)
            def _():
                anchor_pass(u).wait_recv()

            row_above = lax.rem(z + NZ - 1, NZ) * BPD + BPD - 1
            row_below = lax.rem(z + 1, NZ) * BPD
            wide[p, 0:BLOCK] = jnp.where(z > 0, table[u][row_above], edge_in[u])
            wide[p, BLOCK * (BPD + 1) :] = jnp.where(z < NZ - 1, table[u][row_below], edge_in[u])
            for b in range(BPD):
                wide[p, BLOCK * (b + 1) : BLOCK * (b + 2)] = kv[u, b]
            came, passed = anchor_in[u, 0], anchor_in[u, 1]
            anchor_kv[p, :BLOCK] = jnp.where(x == 0, table[u][0], jnp.where(x == 2, passed, came))
            anchor_kv[p, BLOCK:] = jnp.where(
                x == 3, table[u][TARGETS - 1], jnp.where(x == 1, passed, came)
            )
        near[h][...] = jnp.zeros_like(near[h])
        anchor_acc[h][...] = jnp.zeros_like(anchor_acc[h])

    def compute(h, piece):
        if piece == 0:
            if h == 0:

                @pl.when(rim)
                def _():
                    edge_copy().wait_recv()

            lay_keys(h)
        column = lax.broadcasted_iota(jnp.int32, (1, 8 * BLOCK), 1)

        @pl.loop(piece * BPD // PIECES, (piece + 1) * BPD // PIECES)
        def _(i):
            rows = pl.ds(pl.multiple_of(i * BLOCK, BLOCK), 3 * BLOCK)
            spots = [slot_t[x * H + h, T_PLACE + i * R + r] for r in range(R)]
            keys, values = (
                jnp.concatenate(
                    [wide[p, rows], anchor_kv[p]] + [received[2 * h + p][s] for s in spots], axis=0
                )
                for p in (0, 1)
            )
            q, g = query[h, i], grad[h, i]
            block = ctx * BPD + i
            low = jnp.where(block == 0, BLOCK, 0)
            cut = jnp.where(block == NX * NZ * BPD - 1, 2 * BLOCK, 3 * BLOCK)
            masked = (column < low) | ((column >= cut) & (column < 3 * BLOCK))
            contract_last = (((1,), (1,)), ((), ()))
            contract_first = (((0,), (0,)), ((), ()))
            scores = lax.dot_general(q, keys, contract_last, preferred_element_type=F32) * SCALE
            scores = jnp.where(masked, -1e30, scores)
            powers = jnp.exp(scores - jnp.max(scores, axis=-1, keepdims=True))
            probs = powers * (1.0 / jnp.sum(powers, axis=-1, keepdims=True))
            low_probs = probs.astype(BF16)
            attended = jnp.dot(low_probs, values, preferred_element_type=F32).astype(BF16)
            out_o[h, i] = attended
            delta = jnp.sum(g.astype(F32) * attended.astype(F32), axis=-1, keepdims=True)
            grad_probs = lax.dot_general(g, values, contract_last, preferred_element_type=F32)
            grad_scores = (probs * (grad_probs - delta)).astype(BF16)
            out_q[h, i] = (
                jnp.dot(grad_scores, keys, preferred_element_type=F32) * SCALE
            ).astype(BF16)
            key_part = (
                lax.dot_general(grad_scores, q, contract_first, preferred_element_type=F32) * SCALE
            )
            value_part = lax.dot_general(
                low_probs, g, contract_first, preferred_element_type=F32
            )
            for p, part in ((0, key_part), (1, value_part)):
                near[h][p, rows] += part[: 3 * BLOCK]
                anchor_acc[h][p] += part[3 * BLOCK : 5 * BLOCK]
                for r in range(R):
                    terms[p, i * R + r] = part[(5 + r) * BLOCK : (6 + r) * BLOCK].astype(BF16)

    def terms_copy(u, side, part):
        return to(
            (x_r, x_l)[side],
            merged_out[u].at[side, part_of(0, part)],
            terms_in[u].at[part_of((FROM_L, FROM_R)[side], part)],
            x_sem.at[(5, 2)[part], u, side],
        )

    def terms_relay_copy(u, side):
        return to(
            (x_r, x_l)[side], relay_out[u].at[side], terms_relay[u].at[1 - side],
            x_sem.at[3, u, side],
        )

    def part_first(u):
        return to(
            jnp.where(x == 1, x_r, x_l), part_out.at[u, 0], part_in.at[u, 0], part_sem.at[u, 0]
        )

    def part_second(u, side):
        return to(
            (x_r, x_l)[side], part_out.at[u, 1], part_in.at[u, 1 + side], part_sem.at[u, 1 + side]
        )

    def leftward():
        return (x == 0) | (x == 1)

    def edge_part_copy(u):
        return to(beyond, edge_part_out.at[u], edge_part_in.at[u], edge_sem.at[u])

    def anchor(u, which):
        return anchor_acc[u // 2][u % 2, which * BLOCK : (which + 1) * BLOCK]

    def near_rows(u, b):
        return near[u // 2][u % 2, (b + 1) * BLOCK : (b + 2) * BLOCK]

    def send_terms(u):
        h, p = u // 2, u % 2
        for part in (1, 0):
            for side in (0, 1):
                merged_copy(u, side, part).wait_send()

            @pl.loop(part * RELAY, (part + 1) * RELAY)
            def _(k):
                merged_out[u][0, k] = terms[p, slot_t[x * H + h, T_GIVER + FROM_R + k]]
                merged_out[u][1, k] = terms[p, slot_t[x * H + h, T_GIVER + FROM_L + k]]

            for side in (0, 1):
                terms_copy(u, side, part).start()

        @pl.loop(0, MAIN)
        def _(k):
            terms_in[u][B_OWN + k] = terms[p, slot_t[x * H + h, T_GIVER + OWN + k]]

        terms_in[u][B_ZERO] = jnp.zeros((BLOCK, HD), BF16)

        @pl.when(inner)
        def _():
            part_out[u, 0] = jnp.where(x == 1, anchor(u, 1), anchor(u, 0)).astype(BF16)
            part_first(u).start()

        @pl.when(rim)
        def _():
            edge_part_out[u] = jnp.where(z == 0, near_rows(u, -1), near_rows(u, BPD)).astype(BF16)
            edge_part_copy(u).start()

    def relay_terms(u):
        for side in (0, 1):
            relay_copy(u, side).wait_send()
            terms_copy(u, side, 1).wait_recv()

        @pl.loop(0, RELAY)
        def _(k):
            relay_out[u][0, k] = terms_in[u][FROM_L + MAIN - 1 - k]
            relay_out[u][1, k] = terms_in[u][FROM_R + MAIN - 1 - k]

        for side in (0, 1):
            terms_relay_copy(u, side).start()

        @pl.when(inner)
        def _():
            part_first(u).wait_recv()
            mine = jnp.where(x == 1, anchor(u, 0), anchor(u, 1))
            part_out[u, 1] = (mine + part_in[u, 0].astype(F32)).astype(BF16)

        @pl.when(outer)
        def _():
            part_out[u, 1] = jnp.where(x == 0, anchor(u, 1), anchor(u, 0)).astype(BF16)

        @pl.when(leftward())
        def _():
            part_second(u, 1).start()

        @pl.when(jnp.logical_not(leftward()))
        def _():
            part_second(u, 0).start()

    def land(u):
        gather_sent(u)

        @pl.when(outer)
        def _():
            for side in (0, 1):
                anchor_copy(u, side).wait_send()
                part_second(u, side).wait_recv()

        for side in (0, 1):
            terms_copy(u, side, 0).wait_recv()
            terms_relay_copy(u, side).wait_recv()

        @pl.loop(0, RELAY)
        def _(k):
            terms_in[u][B_RR + k] = terms_relay[u][0, k]
            terms_in[u][B_RL + k] = terms_relay[u][1, k]

    def rows(u, group):
        h = u // 2
        for away in {1: (4,), 2: (3, 5), 3: (2, 6), 4: (1, 7), 5: (0,)}[group]:
            row = lax.rem(z + away, NZ)

            @pl.loop(0, BPD)
            def _(b):
                t = row * BPD + b
                total = terms_in[u][source_t[h, t * DEEP]].astype(F32)
                for k in range(1, DEEP):
                    total += terms_in[u][source_t[h, t * DEEP + k]].astype(F32)
                table[u][t] = total.astype(BF16)

            def add(t, part):
                table[u][t] = (table[u][t].astype(F32) + part).astype(BF16)

            def both():
                return part_in[u, 1].astype(F32) + part_in[u, 2].astype(F32)

            @pl.when((x == 0) & (row == 0))
            def _():
                add(0, anchor(u, 0) + both())

            @pl.when((x == NX - 1) & (row == NZ - 1))
            def _():
                add(TARGETS - 1, anchor(u, 1) + both())

            if away == NZ - 1:

                @pl.when(z > 0)
                def _():
                    add(row * BPD + BPD - 1, near_rows(u, -1))

            if away == 1:

                @pl.when(z < NZ - 1)
                def _():
                    add(row * BPD, near_rows(u, BPD))

    def sum_copy(u, s, half, right):
        row = lax.rem(z + 5 - s, NZ) if right else lax.rem(z + NZ - 5 + s, NZ)
        way = 0 if right else 1
        return to(
            z_r if right else z_l,
            table[u].at[pl.ds(row * BPD + half * HALF, HALF)],
            (sums_r if right else sums_l)[u].at[s - 1, pl.ds(half * HALF, HALF)],
            rs_sent.at[u],
            rs_sem.at[u % 2, s - 1, half, way],
        )

    def sum_moves(s):
        return moves(4 if s == 1 else 1)

    def sum_start(u):
        for half, right in sum_moves(1):
            sum_copy(u, 1, half, right).start()

    def sum_step(u, s, half):
        for right in (True, False):
            if (half, right) in sum_moves(s - 1):
                sum_copy(u, s - 1, half, right).wait_recv()
                row = lax.rem(z + 5 - s, NZ) if right else lax.rem(z + NZ - 5 + s, NZ)
                came = (sums_r if right else sums_l)[u]

                @pl.loop(0, HALF)
                def _(b):
                    here = row * BPD + half * HALF + b
                    table[u][here] = (
                        table[u][here].astype(F32) + came[s - 2, half * HALF + b].astype(F32)
                    ).astype(BF16)

            sum_copy(u, s, half, right).start()

    def finish(u):
        h, p = u // 2, u % 2
        for half, right in sum_moves(4):
            sum_copy(u, 4, half, right).wait_recv()

        @pl.when(rim)
        def _():
            edge_part_copy(u).wait_recv()
            lone = pl.ds(pl.multiple_of(jnp.where(z == 0, 1, BPD) * BLOCK, BLOCK), BLOCK)
            near[h][p, lone] += edge_part_in[u].astype(F32)

        @pl.loop(0, BPD)
        def _(b):
            total = (
                table[u][z * BPD + b].astype(F32)
                + sums_r[u][3, b].astype(F32)
                + sums_l[u][3, b].astype(F32)
                + near[h][p, pl.ds(pl.multiple_of((b + 1) * BLOCK, BLOCK), BLOCK)]
            )
            (out_k, out_v)[p][h, b] = total.astype(BF16)

    def drain(u):
        all_sent(u, rs_sent)
        for side in (0, 1):
            for part in (0, 1):
                terms_copy(u, side, part).wait_send()
            terms_relay_copy(u, side).wait_send()

        @pl.when(inner)
        def _():
            anchor_pass(u).wait_send()
            part_first(u).wait_send()

        @pl.when(leftward())
        def _():
            part_second(u, 1).wait_send()

        @pl.when(jnp.logical_not(leftward()))
        def _():
            part_second(u, 0).wait_send()

        @pl.when(rim)
        def _():
            edge_part_copy(u).wait_send()

    steps = {
        "GS": gather_start,
        "G": gather_step,
        "GE": gather_end,
        "SR": send_relays,
        "SM": send_merged,
        "C": compute,
        "ST": send_terms,
        "RT": relay_terms,
        "L": land,
        "R": rows,
        "SS": sum_start,
        "S": sum_step,
        "F": finish,
    }
    first_name, *first_where = ORDER[0]
    steps[first_name](*first_where)
    slot_v[...], source_v[...] = slot_tables(links[...], x)
    copies = (
        pltpu.make_async_copy(slot_v, slot_t, table_sem.at[0]),
        pltpu.make_async_copy(source_v, source_t, table_sem.at[1]),
    )
    for copy in copies:
        copy.start()
    for copy in copies:
        copy.wait()
    for name, *where in ORDER[1:]:
        steps[name](*where)
    for u in range(UNITS):
        drain(u)

    @pl.when(rim)
    def _():
        edge_copy().wait_send()


def local(query, key, value, out_grad, random_links):
    def head_major(array):
        return array.reshape(BPD, BLOCK, H, HD).transpose(2, 0, 1, 3)

    def seq_major(array):
        return array.transpose(1, 2, 0, 3).reshape(BPD * BLOCK, H, HD)

    kv = jnp.stack((head_major(key), head_major(value)), axis=1).reshape(UNITS, BPD, BLOCK, HD)
    block = (BLOCK, HD)

    def per(count, *shape, dtype=BF16):
        return [pltpu.VMEM(shape, dtype) for _ in range(count)]

    dma = pltpu.SemaphoreType.DMA
    vmem = pl.BlockSpec(memory_space=pltpu.VMEM)
    outs = pl.pallas_call(
        kernel,
        out_shape=[jax.ShapeDtypeStruct((H, BPD, BLOCK, HD), BF16)] * 4,
        in_specs=[vmem] * 4,
        out_specs=[vmem] * 4,
        scratch_shapes=[
            per(UNITS, TARGETS, *block),
            per(UNITS, 2, RELAY, *block),
            per(UNITS, 2, RELAY, *block),
            per(UNITS, 2, MAIN, *block),
            per(UNITS, RECEIVED, *block),
            per(UNITS, B_SIZE, *block),
            per(UNITS, 2, RELAY, *block),
            per(UNITS, 4, BPD, *block),
            per(UNITS, 4, BPD, *block),
            per(H, 2, (BPD + 2) * BLOCK, HD, dtype=F32),
            per(H, 2, 2 * BLOCK, HD, dtype=F32),
            pltpu.VMEM((UNITS, 2, *block), BF16),
            pltpu.VMEM((UNITS, 2, *block), BF16),
            pltpu.VMEM((UNITS, 3, *block), BF16),
            pltpu.VMEM((UNITS, *block), BF16),
            pltpu.VMEM((UNITS, *block), BF16),
            pltpu.VMEM((UNITS, *block), BF16),
            pltpu.VMEM((UNITS, *block), BF16),
            pltpu.VMEM((2, 2 * BLOCK, HD), BF16),
            pltpu.VMEM((2, (BPD + 2) * BLOCK, HD), BF16),
            pltpu.VMEM((2, REFS, *block), BF16),
            dma((UNITS,)),
            dma((2, 4, 2, 2)),
            dma((UNITS,)),
            dma((2, 4, 2, 2)),
            dma((6, UNITS, 2, 2)),
            dma((UNITS, 3, 2)),
            dma((UNITS, 3, 2)),
            dma((UNITS + 1, 2)),
            pltpu.VMEM((NX * H, T_WIDTH), jnp.int32),
            pltpu.VMEM((H, TARGETS * DEEP), jnp.int32),
            pltpu.SMEM((NX * H, T_WIDTH), jnp.int32),
            pltpu.SMEM((H, TARGETS * DEEP), jnp.int32),
            dma((2,)),
        ],
        compiler_params=pltpu.CompilerParams(
            collective_id=0, has_side_effects=True, vmem_limit_bytes=60 * 2**20
        ),
        cost_estimate=pl.CostEstimate(
            flops=2 * 6 * BLOCK * 8 * BLOCK * HD * H * BPD,
            bytes_accessed=4 * 2**20,
            transcendentals=H * BPD * BLOCK * 8 * BLOCK,
        ),
    )(kv, head_major(query), head_major(out_grad), named_blocks(random_links))
    return tuple(seq_major(array) for array in outs)


def solution(mesh):
    split = P("ctx", "head", None)
    return jax.shard_map(
        local,
        mesh=mesh,
        in_specs=(split, split, split, split, P(None, "head", None)),
        out_specs=(split, split, split, split),
        check_vma=False,
    )
```
